32 devices in a mesh: groups: 2 (over y), pos: 4 (over z), strand: 2 (over core), heads: 2 (over x).
Axes of the slice: x: 2, y: 2, z: 4, core: 2. Of those that a mesh axis runs over, the one named last changes fastest.
Arguments:
- base_codes: int32 [131072], P(('groups', 'pos')), parts along dimension 0, may hold values from 0 to 3
- embed_table: bfloat16 [512, 1536], P(None, 'heads'), may hold values from -0.5 to 0.5
- attn_gain: float32 [1536], replicated, may hold values from 0.1 to 1.9
- w_query: bfloat16 [1536, 1024], P(None, 'heads')
- w_key: bfloat16 [1536, 128], P(None, 'heads')
- w_value: bfloat16 [1536, 192], P(None, 'heads'), may hold values from -0.15625 to 0.15625
- w_out: bfloat16 [1536, 1536], P('heads'), may hold values from -0.15625 to 0.15625
- head_gain: float32 [1536], replicated, may hold values from 0.1 to 1.9
- w_tracks: bfloat16 [1536, 2, 1536], P(None, None, 'heads'), may hold values from -0.15625 to 0.15625
- track_pairs: int32 [3072], P(('strand', 'heads')), may hold values from 0 to 3071, as said below
Outputs:
- tracks_out: float32 [1024, 3072], P(('groups', 'pos'), ('strand', 'heads')), parts along dimension 0
The draws below stay inside these ranges and needn't reach their ends.
There are 2 independent parts, one for each index of `groups`. The reference program is written for one: setup_inputs(seed, part) draws one part's arguments, and reference() takes and returns one part's arrays. A program takes and returns all parts, laid end to end along the dimension named above; an argument that names none is the same for every part. Nothing has to cross between parts.
Inputs may be any that keep to these rules, and one draw needn't show every extreme that they name: track_pairs is an involution: each aligned pair of tracks 2 j and 2 j + 1 is either swapped or left in place.
All inputs are finite; a program needn't handle non-finite values.
Results may differ from the reference program's by a relative error of at most 0.008.
Values may be sent and summed in bfloat16 or wider, within the bound.
No kernel may reach another device: no remote copies, remote signals or barrier semaphores. Data moves between devices by JAX's collectives and lax.ppermute only.
A program may use at most 64 MiB of HBM per device.

```python
import math
import jax
import jax.numpy as jnp
from jax import lax

D = 1536
HEADS = 8
KDIM = 128
VDIM = 192
TRACKS = 3072
BIN = 128
LEN = 512


def key_matrix(key):
    return jax.random.normal(jax.random.fold_in(key, 11), (D, KDIM), jnp.float32) * D ** (-0.5)


def draw_w_key(key, part):
    return key_matrix(key).astype(jnp.bfloat16)


def draw_w_query(key, part):
    base_draw = jax.random.normal(jax.random.fold_in(key, 23), (D, HEADS, KDIM), jnp.float32) * D ** (-0.5)
    spread = jax.random.uniform(jax.random.fold_in(key, 29), (HEADS,), jnp.float32, 1.0, 3.0)
    base_draw = base_draw * spread[None, :, None]
    return base_draw.reshape(D, HEADS * KDIM).astype(jnp.bfloat16)


def draw_track_pairs(key, part):
    flips = jax.random.randint(jax.random.fold_in(key, 41), (TRACKS // 2,), 0, 2, dtype=jnp.int32)
    indices = jnp.arange(TRACKS, dtype=jnp.int32)
    return indices + jnp.repeat(flips, 2) * (1 - 2 * (indices % 2))


def touch_ends(entries, rng, least, top_value):
    place = [jax.random.randint(jax.random.fold_in(rng, axis), (), 0, length) for axis, length in enumerate(entries.shape)]
    widest = entries.shape.index(max(entries.shape))
    beside = place[:widest] + [(place[widest] + 1) % entries.shape[widest]] + place[widest + 1:]
    return entries.at[tuple(place)].set(least).at[tuple(beside)].set(top_value)


def shard_levels(rng, dims, pieces, smallest, largest):
    loudness, own = 1.0, jax.random.fold_in(rng, 6)
    for position, blocks in pieces:
        heights = jnp.exp(jax.random.uniform(jax.random.fold_in(own, position), (blocks,), jnp.float32, smallest / len(pieces), largest / len(pieces)))
        loudness = loudness * jnp.repeat(heights, dims[position] // blocks).reshape([-1 if axis == position else 1 for axis in range(len(dims))])
    return loudness


def centred(rng, shape, width, reach, pieces=(), kind=jnp.bfloat16):
    drawn = jax.random.normal(rng, shape, jnp.float32) * width
    if len(pieces) > 0:
        drawn = shard_levels(rng, shape, pieces, -0.22, 0.18) * drawn
    return jnp.clip(drawn, min=-reach, max=reach).astype(kind)


def setup_inputs(seed: int = 0, part: int = 0) -> dict:
    keys = jax.random.split(jax.random.key(seed), 11)
    part_keys = jax.random.split(jax.random.fold_in(keys[10], part), 11)
    base_codes = touch_ends(jax.random.randint(part_keys[0], (LEN * BIN,), 0, 4), jax.random.fold_in(part_keys[0], 1), 0, 3).astype(jnp.int32)
    embed_table = centred(keys[1], (BIN * 4, D), BIN ** -0.5, 0.5, ((1, 2),))
    attn_gain = jnp.clip(1.0 + 0.18 * jax.random.normal(keys[2], (D,), jnp.float32), 0.1, 1.9)
    w_query = draw_w_query(jax.random.fold_in(keys[10], 71), part)
    w_key = draw_w_key(jax.random.fold_in(keys[10], 71), part)
    w_value = centred(keys[5], (D, VDIM), D ** -0.5, 0.15625, ((1, 2),))
    w_out = centred(keys[6], (HEADS * VDIM, D), (HEADS * VDIM) ** -0.5, 0.15625, ((0, 2),))
    head_gain = jnp.clip(1.0 + 0.18 * jax.random.normal(keys[7], (D,), jnp.float32), 0.1, 1.9)
    w_tracks = centred(keys[8], (D, 2, TRACKS // 2), D ** -0.5, 0.15625, ((2, 2),))
    track_pairs = draw_track_pairs(jax.random.fold_in(keys[10], 71), part)
    return {"base_codes": base_codes, "embed_table": embed_table, "attn_gain": attn_gain, "w_query": w_query, "w_key": w_key, "w_value": w_value, "w_out": w_out, "head_gain": head_gain, "w_tracks": w_tracks, "track_pairs": track_pairs}


def rotate(values, positions):
    row_total = values.shape[0]
    head_total = values.shape[1] // KDIM
    half_dim = KDIM // 2
    inverse = jnp.exp(jnp.arange(half_dim, dtype=jnp.float32) * (-math.log(10000.0) / half_dim))
    angles = positions.astype(jnp.float32)[:, None] * inverse[None, :]
    cosine = jnp.cos(angles)[:, None, :]
    sine_val = jnp.sin(angles)[:, None, :]
    shaped = values.astype(jnp.float32).reshape(row_total, head_total, KDIM)
    low_part = shaped[:, :, :half_dim]
    high_part = shaped[:, :, half_dim:]
    turned = jnp.concatenate([low_part * cosine - high_part * sine_val, high_part * cosine + low_part * sine_val], axis=2)
    return turned.reshape(row_total, head_total * KDIM).astype(jnp.bfloat16)

def embed_bases(base_block, lookup):
    onehot = (base_block[:, :, None] == jnp.arange(4, dtype=jnp.int32)[None, None, :]).astype(jnp.bfloat16)
    onehot = onehot.reshape(base_block.shape[0], base_block.shape[1] * 4)
    return jnp.dot(onehot, lookup, preferred_element_type=jnp.float32).astype(jnp.bfloat16)

def normalize(values, gain_vec):
    floats = values.astype(jnp.float32)
    square = lax.optimization_barrier(jnp.mean(floats * floats, axis=-1, keepdims=True))
    return (floats * lax.rsqrt(square + 1e-06) * gain_vec).astype(jnp.bfloat16)

def strand_pass(inputs, positions, attn_gain, w_query, w_key, w_value, w_out, head_gain, w_tracks):
    normed = normalize(inputs, attn_gain)
    queries = rotate(jnp.dot(normed, w_query, preferred_element_type=jnp.float32).astype(jnp.bfloat16), positions)
    keys_rot = rotate(jnp.dot(normed, w_key, preferred_element_type=jnp.float32).astype(jnp.bfloat16), positions)
    values = jnp.dot(normed, w_value, preferred_element_type=jnp.float32).astype(jnp.bfloat16)
    per_head = queries.reshape(LEN, HEADS, KDIM).transpose(1, 0, 2)

    def attend(query_block):
        scores = jnp.dot(query_block, keys_rot.T, preferred_element_type=jnp.float32) * KDIM ** (-0.5)
        top_score = lax.optimization_barrier(jnp.max(scores, axis=1, keepdims=True))
        weights = jnp.exp(scores - top_score)
        weight_sum = lax.optimization_barrier(jnp.sum(weights, axis=1, keepdims=True))
        weighted = jnp.dot(weights.astype(jnp.bfloat16), values, preferred_element_type=jnp.float32)
        return (weighted / weight_sum).astype(jnp.bfloat16)
    outputs = lax.map(attend, per_head)
    merged = outputs.transpose(1, 0, 2).reshape(LEN, HEADS * VDIM)
    mixed_sum = jnp.dot(merged, w_out, preferred_element_type=jnp.float32)
    hidden = (inputs.astype(jnp.float32) + mixed_sum).astype(jnp.bfloat16)
    normed_out = normalize(hidden, head_gain)
    logits = jnp.dot(normed_out, w_tracks.reshape(D, TRACKS), preferred_element_type=jnp.float32)
    return jax.nn.softplus(logits).astype(jnp.bfloat16)

def reference(base_codes, embed_table, attn_gain, w_query, w_key, w_value, w_out, head_gain, w_tracks, track_pairs):
    base_block = base_codes.reshape(LEN, BIN)
    flipped = 3 - base_block[::-1, ::-1]
    positions = jnp.arange(LEN, dtype=jnp.int32)
    forward = strand_pass(embed_bases(base_block, embed_table), positions, attn_gain, w_query, w_key, w_value, w_out, head_gain, w_tracks)
    reverse = strand_pass(embed_bases(flipped, embed_table), positions, attn_gain, w_query, w_key, w_value, w_out, head_gain, w_tracks)
    aligned = jnp.take(reverse[::-1], track_pairs, axis=1)
    return 0.5 * (forward.astype(jnp.float32) + aligned.astype(jnp.float32))
```

```python
import math

import jax
import jax.numpy as jnp
from jax import lax
from jax.sharding import PartitionSpec as P

KDIM = 128
VDIM = 192
BIN = 128
BASES = 4
F32 = jnp.float32
BF16 = jnp.bfloat16


def shifted(value, axis, distance):
    size = lax.axis_size(axis)
    return lax.ppermute(value, axis, [(i, (i + distance) % size) for i in range(size)])


def matmul(a, b):
    return jnp.dot(a, b, preferred_element_type=F32)


def share_over_strand(value, axis, strand_idx):
    size = lax.axis_size(axis)
    half = value.shape[0] // 2
    own_half = lax.dynamic_slice_in_dim(value, strand_idx * half, half, 0)
    parts = [value]
    for step in range(1, size):
        mine = shifted(own_half, axis, step)
        theirs = shifted(mine, "strand", 1)
        low = jnp.where(strand_idx == 0, mine, theirs)
        high = jnp.where(strand_idx == 0, theirs, mine)
        parts.append(jnp.concatenate([low, high], axis=0))
    return parts


def in_order(parts, axis):
    size = lax.axis_size(axis)
    if size == 2:
        own = lax.axis_index(axis) == 0
        return jnp.stack([jnp.where(own, parts[0], parts[1]), jnp.where(own, parts[1], parts[0])])
    stacked = jnp.stack(parts)
    return jnp.take(stacked, (lax.axis_index(axis) - jnp.arange(size)) % size, axis=0)


def rotate(values, cosine, sine):
    half = KDIM // 2
    heads = values.shape[1] // KDIM
    shaped = values.astype(BF16).astype(F32).reshape(values.shape[0], heads, KDIM)
    low, high = shaped[:, :, :half], shaped[:, :, half:]
    cosine, sine = cosine[:, None, :], sine[:, None, :]
    turned = jnp.concatenate([low * cosine - high * sine, high * cosine + low * sine], axis=2)
    return turned.astype(BF16)


def body(
    base_codes,
    embed_table,
    attn_gain,
    w_query,
    w_key,
    w_value,
    w_out,
    head_gain,
    w_tracks,
    track_pairs,
):
    rows = base_codes.shape[0] // BIN
    pos_total = lax.axis_size("pos")
    head_total = lax.axis_size("heads")
    strand_idx = lax.axis_index("strand")
    pos_idx = lax.axis_index("pos")
    features = w_query.shape[0]
    key_cols = w_key.shape[1]

    kv_parts = share_over_strand(
        jnp.concatenate([w_key.T, w_value.T], axis=0), "heads", strand_idx
    )
    embed_parts = share_over_strand(embed_table, "heads", strand_idx)
    own_codes = base_codes.reshape(rows, BIN).astype(BF16)
    code_blocks = [own_codes] + [shifted(own_codes, "pos", k) for k in range(1, pos_total)]
    codes = jnp.concatenate(code_blocks, axis=0)

    column = jnp.arange(BIN * BASES, dtype=jnp.int32)
    column = jnp.where(strand_idx == 0, column, BIN * BASES - 1 - column)
    spread = (jnp.arange(BIN, dtype=jnp.int32)[:, None] == column[None, :] // BASES).astype(BF16)
    onehot = (matmul(codes, spread) == (column % BASES).astype(F32)[None, :]).astype(BF16)

    block_idx = (pos_idx - jnp.arange(pos_total, dtype=jnp.int32)) % pos_total
    places = (block_idx[:, None] * rows + jnp.arange(rows, dtype=jnp.int32)[None, :]).reshape(-1)
    places = jnp.where(strand_idx == 0, places, pos_total * rows - 1 - places)
    half = KDIM // 2
    inverse = jnp.exp(jnp.arange(half, dtype=F32) * (-math.log(10000.0) / half))
    angles = places.astype(F32)[:, None] * inverse[None, :]
    cosine, sine = jnp.cos(angles), jnp.sin(angles)

    embed = in_order(embed_parts, "heads")
    inputs = jnp.concatenate(
        [matmul(onehot, embed[i]).astype(BF16) for i in range(head_total)], axis=1
    )
    floats = inputs.astype(F32)
    square = jnp.mean(floats * floats, axis=1, keepdims=True)
    normed = (floats * lax.rsqrt(square + 1e-06) * attn_gain).astype(BF16)
    kv_rows = in_order(kv_parts, "heads")
    key_rows = kv_rows[:, :key_cols].reshape(KDIM, features)
    value_rows = kv_rows[:, key_cols:].reshape(VDIM, features)
    contract = (((1,), (1,)), ((), ()))
    keys = lax.dot_general(normed, key_rows, contract, preferred_element_type=F32)
    keys = rotate(keys, cosine, sine)[:, 0]
    values = lax.dot_general(normed, value_rows, contract, preferred_element_type=F32).astype(BF16)
    queries = rotate(matmul(normed[:rows], w_query), cosine[:rows], sine[:rows])
    own_heads = []
    for head in range(queries.shape[1]):
        scores = lax.dot_general(
            queries[:, head], keys, contract, preferred_element_type=F32
        ) * KDIM ** (-0.5)
        weights = jnp.exp(scores - jnp.max(scores, axis=1, keepdims=True))
        total = jnp.sum(weights, axis=1, keepdims=True)
        own_heads.append((matmul(weights.astype(BF16), values) / total).astype(BF16))
    merged = jnp.concatenate(own_heads, axis=1)

    chunks = 2
    width = features // chunks
    shares = [
        matmul(merged, w_out[:, c * width : (c + 1) * width]).astype(BF16) for c in range(chunks)
    ]
    gained = []
    square = jnp.zeros((rows, 1), F32)
    for c in range(chunks):
        total = shares[c].astype(F32)
        for step in range(1, head_total):
            total = total + shifted(shares[c], "heads", step).astype(F32)
        hidden = inputs[:rows, c * width : (c + 1) * width].astype(F32) + total
        hidden = hidden.astype(BF16).astype(F32)
        square = square + jnp.sum(hidden * hidden, axis=1, keepdims=True)
        gained.append((hidden * head_gain[c * width : (c + 1) * width]).astype(BF16))
    scale = lax.rsqrt(square / features + 1e-06)
    tracks = w_tracks.transpose(1, 0, 2)

    def predict(which):
        weight = lax.dynamic_index_in_dim(tracks, which, 0, keepdims=False)
        logits = sum(
            matmul(gained[c], weight[c * width : (c + 1) * width]) for c in range(chunks)
        )
        return jax.nn.softplus(logits * scale).astype(BF16)

    received = shifted(predict(1 - strand_idx), "strand", 1)
    kept = predict(strand_idx)
    forward = jnp.where(strand_idx == 0, kept, received).astype(F32)
    reverse = jnp.where(strand_idx == 0, received, kept).astype(F32)
    index = jnp.arange(track_pairs.shape[0], dtype=jnp.int32)
    swapped = (track_pairs - index) % track_pairs.shape[0] != 0
    after = jnp.roll(reverse, -1, axis=1)
    before = jnp.roll(reverse, 1, axis=1)
    partner = jnp.where(index % 2 == 0, after, before)
    return 0.5 * (forward + jnp.where(swapped, partner, reverse))


def solution(mesh):
    placed = (
        P(("groups", "pos")),
        P(None, "heads"),
        P(),
        P(None, "heads"),
        P(None, "heads"),
        P(None, "heads"),
        P("heads", None),
        P(),
        P(None, None, "heads"),
        P(("strand", "heads")),
    )
    return jax.shard_map(
        body,
        mesh=mesh,
        in_specs=placed,
        out_specs=P(("groups", "pos"), ("strand", "heads")),
        check_vma=False,
    )
```

```python
import functools
import math

import jax
import jax.experimental.pallas as pl
import jax.experimental.pallas.tpu as pltpu
import jax.numpy as jnp
from jax import lax
from jax.sharding import PartitionSpec as P

KDIM = 128
VDIM = 192
BIN = 128
BASES = 4
LANES = 128
VMEM_LIMIT = 48 * 2**20
F32 = jnp.float32
BF16 = jnp.bfloat16


def shifted(value, axis, distance):
    size = lax.axis_size(axis)
    return lax.ppermute(value, axis, [(i, (i + distance) % size) for i in range(size)])


def matmul(a, b):
    return jnp.dot(a, b, preferred_element_type=F32)


def matmul_t(a, b):
    return lax.dot_general(a, b, (((1,), (1,)), ((), ())), preferred_element_type=F32)


def call(kernel, outs, operands, name, scratch=(), spaces=None, flops=0):
    vmem = pl.BlockSpec(memory_space=pltpu.VMEM)
    specs = [vmem if space is None else pl.BlockSpec(memory_space=space) for space in (spaces or [None] * len(operands))]
    moved = sum(math.prod(v.shape) * v.dtype.itemsize for v in list(operands) + list(outs))
    return pl.pallas_call(
        kernel,
        out_shape=list(outs),
        in_specs=specs,
        out_specs=[vmem] * len(outs),
        scratch_shapes=list(scratch),
        compiler_params=pltpu.CompilerParams(vmem_limit_bytes=VMEM_LIMIT),
        cost_estimate=pl.CostEstimate(flops=flops, bytes_accessed=moved, transcendentals=0),
        name=name,
    )(*operands)


def shape(dims, dtype):
    return jax.ShapeDtypeStruct(tuple(dims), dtype)


def over_blocks(total, block, step):
    if total == block:
        step(0)
    else:

        def one(i, carry):
            step(pl.multiple_of(i * block, block))
            return carry

        lax.fori_loop(0, total // block, one, 0)


def stage_kernel(embed, key_t, value_t, codes, half_kv, first, second, codes_out, sems):
    strand = lax.axis_index("strand")
    key_cols, value_cols = key_t.shape[0], value_t.shape[0]
    width = half_kv.shape[1]
    quarter = first.shape[0]
    cols = pl.ds(pl.multiple_of(strand * width, LANES), width)
    row = pl.multiple_of(strand * (2 * quarter), quarter)
    copies = [
        pltpu.make_async_copy(key_t.at[:, cols], half_kv.at[pl.ds(0, key_cols)], sems.at[0]),
        pltpu.make_async_copy(value_t.at[:, cols], half_kv.at[pl.ds(key_cols, value_cols)], sems.at[1]),
        pltpu.make_async_copy(embed.at[pl.ds(row, quarter)], first, sems.at[2]),
        pltpu.make_async_copy(embed.at[pl.ds(row + quarter, quarter)], second, sems.at[3]),
    ]
    for copy in copies:
        copy.start()
    codes_out[...] = codes[...].astype(F32).astype(BF16)
    for copy in copies:
        copy.wait()


def own_kernel(blocks, others, *refs):
    codes = refs[:blocks]
    embed, key_t, value_t = refs[blocks : blocks + 3]
    halves = refs[blocks + 3 : blocks + 3 + 2 * others]
    w_query, gain, onehot, kv_t, own, square, kv_sum, q_sum, table, all_codes = refs[blocks + 3 + 2 * others :]
    strand, mine = lax.axis_index("strand"), lax.axis_index("heads")
    size = others + 1
    key_cols, value_cols = key_t.shape[0], value_t.shape[0]
    features, width = w_query.shape[0], embed.shape[1]
    entries = embed.shape[0]
    quarter = entries // 4
    rows = codes[0].shape[0]
    total = blocks * rows
    for i in range(blocks):
        all_codes[i * rows : (i + 1) * rows, :] = codes[i][...]
    for i in range(4):
        part = strand if i % 2 == 0 else 1 - strand
        start = pl.multiple_of(part * (2 * quarter) + (i // 2) * quarter, quarter)
        table[i * quarter : (i + 1) * quarter, :] = embed[pl.ds(start, quarter), :]
    for step in range(size):
        owner = lax.rem(mine + size - step, size)
        key_rows = pl.ds(pl.multiple_of(owner * key_cols, 16), key_cols)
        value_rows = pl.ds(pl.multiple_of(KDIM + owner * value_cols, 16), value_cols)
        if step == 0:
            kv_t[key_rows, :] = key_t[...]
            kv_t[value_rows, :] = value_t[...]
        else:
            for k in range(2):
                piece = halves[2 * (step - 1) + k]
                part = strand if k == 0 else 1 - strand
                cols = pl.ds(pl.multiple_of(part * (features // 2), LANES), features // 2)
                kv_t[key_rows, cols] = piece[:key_cols, :]
                kv_t[value_rows, cols] = piece[key_cols:, :]
    spot = lax.broadcasted_iota(jnp.int32, (BIN, entries), 1)
    piece = spot // quarter
    half = jnp.where(piece % 2 == 0, strand, 1 - strand)
    entry = half * (2 * quarter) + (piece // 2) * quarter + spot % quarter
    entry = jnp.where(strand == 0, entry, entries - 1 - entry)
    place = lax.broadcasted_iota(jnp.int32, (BIN, entries), 0)
    spread = jnp.where(place == entry // BASES, 1.0, 0.0).astype(BF16)
    wanted = (entry[:1] % BASES).astype(F32)
    mine_cols = pl.ds(pl.multiple_of(mine * width, LANES), width)
    mine_gain = gain[:, mine_cols]

    def step(start):
        here = pl.ds(start, min(total, 4 * rows))
        hot = jnp.where(matmul(all_codes[here, :], spread) == wanted, 1.0, 0.0).astype(BF16)
        onehot[here, :] = hot
        values = matmul(hot, table[...]).astype(BF16)
        floats = values.astype(F32)
        square[here, :] = jnp.sum(floats * floats, axis=1, keepdims=True)
        gained = (floats * mine_gain).astype(BF16)
        kv_sum[here, :] = matmul_t(gained, kv_t[:, mine_cols])
        return values, gained

    if total <= 4 * rows:
        values, gained = step(0)
        own[...] = values[:rows]
        gained = gained[:rows]
    else:
        over_blocks(total, 4 * rows, lambda start: step(start) and None)
        values = matmul(onehot[:rows, :], table[...]).astype(BF16)
        own[...] = values
        gained = (values.astype(F32) * mine_gain).astype(BF16)
    q_sum[...] = matmul(gained, w_query[pl.ds(pl.multiple_of(mine * width, LANES), width), :])


def turn(values, cosine, sine):
    floats = values.astype(BF16).astype(F32)
    return (floats * cosine + pltpu.roll(floats, KDIM // 2, 1) * sine).astype(BF16)


def attend_kernel(others, *refs):
    pieces = refs[: 4 * others]
    (onehot, kv_t, own, square, kv_sum, q_sum, w_query, gain, cosine, sine, w_out) = refs[4 * others : 4 * others + 11]
    share, merged, inputs, table, squares, sums, keys, values = refs[4 * others + 11 :]
    mine = lax.axis_index("heads")
    size = others + 1
    rows, width = own.shape
    quarter = pieces[0].shape[0]
    total = onehot.shape[0]
    features = size * width
    block = min(total, 4 * rows)
    inputs[:, pl.ds(pl.multiple_of(mine * width, LANES), width)] = own[...]
    queries = q_sum[...]
    over_blocks(total, block, lambda start: squares.__setitem__((pl.ds(start, block), slice(None)), square[pl.ds(start, block), :]))
    for step in range(1, size):
        owner = lax.rem(mine + size - step, size)
        cols = pl.ds(pl.multiple_of(owner * width, LANES), width)
        for i in range(4):
            table[i * quarter : (i + 1) * quarter, :] = pieces[4 * (step - 1) + i][...]
        last = step == size - 1

        def add(start):
            here = pl.ds(start, block)
            found = matmul(onehot[here, :], table[...]).astype(BF16)
            floats = found.astype(F32)
            squares[here, :] = squares[here, :] + jnp.sum(floats * floats, axis=1, keepdims=True)
            gained = (floats * gain[:, cols]).astype(BF16)
            before = kv_sum[here, :] if step == 1 else sums[here, :]
            sums[here, :] = before + matmul_t(gained, kv_t[:, cols])
            return found, gained

        if total == block:
            found, gained = add(0)
            found, gained = found[:rows], gained[:rows]
        else:
            over_blocks(total, block, lambda start: add(start) and None)
            found = matmul(onehot[:rows, :], table[...]).astype(BF16)
            gained = (found.astype(F32) * gain[:, cols]).astype(BF16)
        inputs[:, cols] = found
        queries = queries + matmul(gained, w_query[cols, :])

    def finish(start):
        here = pl.ds(start, block)
        scale = lax.rsqrt(squares[here, :] / features + 1e-06)
        scaled = (sums[here, :] if others else kv_sum[here, :]) * scale
        keys[here, :] = turn(scaled[:, :KDIM], cosine[here, :], sine[here, :])
        values[here, :] = scaled[:, KDIM:].astype(BF16)

    over_blocks(total, block, finish)
    queries = queries * lax.rsqrt(squares[:rows, :] / features + 1e-06)
    result = None
    half = w_out.shape[1] // 2
    for head in range(queries.shape[1] // KDIM):
        query = turn(queries[:, head * KDIM : (head + 1) * KDIM], cosine[:rows, :], sine[:rows, :])
        scores = matmul_t(query, keys[...]) * KDIM ** (-0.5)
        weights = jnp.exp(scores - jnp.max(scores, axis=1, keepdims=True))
        weight_sum = jnp.sum(weights, axis=1, keepdims=True)
        found = (matmul(weights.astype(BF16), values[...]) / weight_sum).astype(BF16)
        merged[:, head * VDIM : (head + 1) * VDIM] = found
    share[...] = matmul(merged[...], w_out[:, :half]).astype(BF16)


def second_kernel(merged, w_out, share):
    half = w_out.shape[1] // 2
    share[...] = matmul(merged[...], w_out[:, half:]).astype(BF16)


def gather_hidden(shares, inputs, gain, chunk):
    width = shares[0].shape[1]
    cols = slice(chunk * width, (chunk + 1) * width)
    total = shares[0][...].astype(F32)
    for other in shares[1:]:
        total = total + other[...].astype(F32)
    hidden = (inputs[:, cols].astype(F32) + total).astype(BF16).astype(F32)
    return jnp.sum(hidden * hidden, axis=1, keepdims=True), (hidden * gain[:, cols]).astype(BF16)


def soft(logits):
    return jnp.maximum(logits, 0.0) + jnp.log1p(jnp.exp(-jnp.abs(logits)))


def first_tracks_kernel(size, *refs):
    shares = refs[:size]
    inputs, gain, tracks, square, to_send, to_keep = refs[size:]
    strand = lax.axis_index("strand")
    width = shares[0].shape[1]
    square[...], gained = gather_hidden(shares, inputs, gain, 0)
    to_send[...] = matmul(gained, tracks[1 - strand, :width, :])
    to_keep[...] = matmul(gained, tracks[strand, :width, :])


def send_kernel(size, *refs):
    shares = refs[:size]
    inputs, gain, tracks, square, to_send, sent, gained_out, scale_out = refs[size:]
    strand = lax.axis_index("strand")
    width = shares[0].shape[1]
    total, gained = gather_hidden(shares, inputs, gain, 1)
    scale = lax.rsqrt((square[...] + total) / (2 * width) + 1e-06)
    logits = to_send[...] + matmul(gained, tracks[1 - strand, width:, :])
    sent[...] = soft(logits * scale).astype(BF16)
    gained_out[...] = gained
    scale_out[...] = scale


def keep_kernel(gained, tracks, to_keep, scale, kept):
    strand = lax.axis_index("strand")
    width = gained.shape[1]
    logits = to_keep[...] + matmul(gained[...], tracks[strand, width:, :])
    kept[...] = soft(logits * scale[...]).astype(BF16)


def average_kernel(kept, received, pairs, out):
    strand = lax.axis_index("strand")
    count = kept.shape[1]
    mine, theirs = kept[...].astype(F32), received[...].astype(F32)
    forward = jnp.where(strand == 0, mine, theirs)
    reverse = jnp.where(strand == 0, theirs, mine)
    index = lax.broadcasted_iota(jnp.int32, (1, count), 1)
    even = index % 2 == 0
    swapped = (pairs[...] % 2 == 0) != even
    partner = jnp.where(even, pltpu.roll(reverse, count - 1, 1), pltpu.roll(reverse, 1, 1))
    out[...] = 0.5 * (forward + jnp.where(swapped, partner, reverse))


def body(
    base_codes,
    embed_table,
    attn_gain,
    w_query,
    w_key,
    w_value,
    w_out,
    head_gain,
    w_tracks,
    track_pairs,
):
    rows = base_codes.shape[0] // BIN
    blocks = lax.axis_size("pos")
    size = lax.axis_size("heads")
    strand = lax.axis_index("strand")
    pos = lax.axis_index("pos")
    features, q_cols = w_query.shape
    entries, width = embed_table.shape
    key_t, value_t = w_key.T, w_value.T
    kv_cols = key_t.shape[0] + value_t.shape[0]
    kv_all = KDIM + VDIM
    quarter = entries // 4
    total = blocks * rows
    tracks_half = w_tracks.shape[2]

    half_kv, first, second, own_codes = call(
        stage_kernel,
        [
            shape((kv_cols, features // 2), BF16),
            shape((quarter, width), BF16),
            shape((quarter, width), BF16),
            shape((rows, BIN), BF16),
        ],
        [embed_table, key_t, value_t, base_codes.reshape(rows, BIN)],
        "stage",
        scratch=[pltpu.SemaphoreType.DMA((4,))],
        spaces=[pl.ANY, pl.ANY, pl.ANY, None],
    )
    halves, pieces = [], []
    for step in range(1, size):
        here = [shifted(v, "heads", step) for v in (half_kv, first, second)]
        there = [shifted(v, "strand", 1) for v in here]
        halves += [here[0], there[0]]
        pieces += [here[1], there[1], here[2], there[2]]
    codes = [own_codes] + [shifted(own_codes, "pos", k) for k in range(1, blocks)]

    block_idx = (pos - jnp.arange(blocks, dtype=jnp.int32)) % blocks
    places = (block_idx[:, None] * rows + jnp.arange(rows, dtype=jnp.int32)[None, :]).reshape(-1)
    places = jnp.where(strand == 0, places, total - 1 - places)
    lane = jnp.arange(KDIM, dtype=jnp.int32)
    half = KDIM // 2
    inverse = jnp.exp((lane % half).astype(F32) * (-math.log(10000.0) / half))
    angles = places.astype(F32)[:, None] * inverse[None, :]
    cosine = jnp.cos(angles)
    sine = jnp.sin(angles) * jnp.where(lane < half, -1.0, 1.0)

    gain = attn_gain.reshape(1, features)
    onehot, kv_t, own, square, kv_sum, q_sum = call(
        functools.partial(own_kernel, blocks, size - 1),
        [
            shape((total, entries), BF16),
            shape((kv_all, features), BF16),
            shape((rows, width), BF16),
            shape((total, 1), F32),
            shape((total, kv_all), F32),
            shape((rows, q_cols), F32),
        ],
        codes + [embed_table, key_t, value_t] + halves + [w_query, gain],
        "own_features",
        scratch=[pltpu.VMEM((entries, width), BF16), pltpu.VMEM((total, BIN), BF16)],
        flops=2 * total * width * (entries + kv_all),
    )
    o_cols = q_cols // KDIM * VDIM
    share_one, merged, inputs = call(
        functools.partial(attend_kernel, size - 1),
        [
            shape((rows, features // 2), BF16),
            shape((rows, o_cols), BF16),
            shape((rows, features), BF16),
        ],
        pieces + [onehot, kv_t, own, square, kv_sum, q_sum, w_query, gain, cosine, sine, w_out],
        "attend",
        scratch=[
            pltpu.VMEM((entries, width), BF16),
            pltpu.VMEM((total, 1), F32),
            pltpu.VMEM((total, kv_all), F32),
            pltpu.VMEM((total, KDIM), BF16),
            pltpu.VMEM((total, VDIM), BF16),
        ],
        flops=2 * total * width * (entries + kv_all) * 2,
    )
    (share_two,) = call(
        second_kernel,
        [shape((rows, features // 2), BF16)],
        [merged, w_out],
        "second_share",
        flops=rows * o_cols * features,
    )
    ones = [share_one] + [shifted(share_one, "heads", k) for k in range(1, size)]
    twos = [share_two] + [shifted(share_two, "heads", k) for k in range(1, size)]
    weights, _ = lax.optimization_barrier((w_tracks, share_two))
    tracks = lax.optimization_barrier(weights.transpose(1, 0, 2))
    gain = head_gain.reshape(1, features)
    square, to_send, to_keep = call(
        functools.partial(first_tracks_kernel, size),
        [
            shape((rows, 1), F32),
            shape((rows, tracks_half), F32),
            shape((rows, tracks_half), F32),
        ],
        ones + [inputs, gain, tracks],
        "first_tracks",
        flops=2 * rows * features * tracks_half,
    )
    sent, gained, scale = call(
        functools.partial(send_kernel, size),
        [
            shape((rows, tracks_half), BF16),
            shape((rows, features // 2), BF16),
            shape((rows, 1), F32),
        ],
        twos + [inputs, gain, tracks, square, to_send],
        "sent_tracks",
        flops=rows * features * tracks_half,
    )
    received = shifted(sent, "strand", 1)
    (kept,) = call(
        keep_kernel,
        [shape((rows, tracks_half), BF16)],
        [gained, tracks, to_keep, scale],
        "kept_tracks",
        flops=rows * features * tracks_half,
    )
    (out,) = call(
        average_kernel,
        [shape((rows, tracks_half), F32)],
        [kept, received, track_pairs.reshape(1, tracks_half)],
        "average",
    )
    return out


def solution(mesh):
    placed = (
        P(("groups", "pos")),
        P(None, "heads"),
        P(),
        P(None, "heads"),
        P(None, "heads"),
        P(None, "heads"),
        P("heads", None),
        P(),
        P(None, None, "heads"),
        P(("strand", "heads")),
    )
    return jax.shard_map(
        body,
        mesh=mesh,
        in_specs=placed,
        out_specs=P(("groups", "pos"), ("strand", "heads")),
        check_vma=False,
    )
```

```python
import functools
import math

import jax
import jax.experimental.pallas as pl
import jax.experimental.pallas.tpu as pltpu
import jax.numpy as jnp
from jax import lax
from jax.sharding import PartitionSpec as P

KDIM = 128
VDIM = 192
BIN = 128
BASES = 4
LANES = 128
VMEM_LIMIT = 48 * 2**20
F32 = jnp.float32
BF16 = jnp.bfloat16


def shifted(value, axis, distance):
    size = lax.axis_size(axis)
    return lax.ppermute(value, axis, [(i, (i + distance) % size) for i in range(size)])


def matmul(a, b):
    return jnp.dot(a, b, preferred_element_type=F32)


def matmul_t(a, b):
    return lax.dot_general(a, b, (((1,), (1,)), ((), ())), preferred_element_type=F32)


def call(kernel, outs, operands, name, scratch=(), spaces=None, flops=0, spare=0):
    vmem = pl.BlockSpec(memory_space=pltpu.VMEM)
    spaces = spaces or [None] * len(operands)
    operands = [
        v if s is None else pltpu.with_memory_space_constraint(v, s) for v, s in zip(operands, spaces)
    ]
    specs = [vmem if s is None else pl.BlockSpec(memory_space=s) for s in spaces]
    held = [v for v, s in zip(operands, spaces) if s is None] + list(outs)
    held += [v for v in scratch if hasattr(v, "shape") and hasattr(v, "dtype") and v.memory_space == pltpu.VMEM]
    moved = sum(math.prod(v.shape[:-1]) * max(v.shape[-1], LANES) * jnp.dtype(v.dtype).itemsize for v in held)
    return pl.pallas_call(
        kernel,
        out_shape=list(outs),
        in_specs=specs,
        out_specs=[vmem] * len(outs),
        scratch_shapes=list(scratch),
        compiler_params=pltpu.CompilerParams(
            vmem_limit_bytes=min(VMEM_LIMIT, moved + moved // 4 + 6 * 2**20 + spare)
        ),
        cost_estimate=pl.CostEstimate(flops=flops, bytes_accessed=moved, transcendentals=0),
        name=name,
    )(*operands)


def shape(dims, dtype):
    return jax.ShapeDtypeStruct(tuple(dims), dtype)


def over_blocks(total, block, step):
    if total == block:
        step(0)
    else:

        def one(i, carry):
            step(pl.multiple_of(i * block, block))
            return carry

        lax.fori_loop(0, total // block, one, 0)


def stage_kernel(chunks, embed, key_t, value_t, *refs):
    part_kv, pieces, sems = refs[0], refs[1 : 1 + chunks], refs[1 + chunks]
    strand = lax.axis_index("strand")
    part = strand * lax.axis_size("groups") + lax.axis_index("groups")
    key_cols, value_cols = key_t.shape[0], value_t.shape[0]
    kv_width = part_kv.shape[1]
    half, width = pieces[0].shape
    cols = pl.ds(pl.multiple_of(part * kv_width, LANES), kv_width)
    rows = pl.ds(pl.multiple_of(strand * half, half), half)
    copies = [
        pltpu.make_async_copy(key_t.at[:, cols], part_kv.at[pl.ds(0, key_cols)], sems.at[0]),
        pltpu.make_async_copy(value_t.at[:, cols], part_kv.at[pl.ds(key_cols, value_cols)], sems.at[1]),
    ]
    for i in range(chunks):
        source = embed.at[rows, pl.ds(i * width, width)]
        copies.append(pltpu.make_async_copy(source, pieces[i], sems.at[2 + i]))
    for copy in copies:
        copy.start()
    for copy in copies:
        copy.wait()


def prepare_kernel(embed, key_t, value_t, w_query, gain, last_gain, codes, *refs):
    table, key_out, value_out, query_out, gain_out, last_out, cosine, sine, codes_out = refs[:9]
    raw_gain, raw_last, raw_codes, sems = refs[9:]
    strand, pos = lax.axis_index("strand"), lax.axis_index("pos")
    half = embed.shape[0] // 2
    pairs = [(codes, raw_codes), (gain, raw_gain), (last_gain, raw_last)]
    for i in range(2):
        part = strand if i == 0 else 1 - strand
        source = embed.at[pl.ds(pl.multiple_of(part * half, half), half)]
        pairs.append((source, table.at[pl.ds(i * half, half)]))
    pairs += [(key_t, key_out), (value_t, value_out), (w_query, query_out)]
    copies = [pltpu.make_async_copy(a, b, sems.at[i]) for i, (a, b) in enumerate(pairs)]
    for copy in copies:
        copy.start()
    total = cosine.shape[0]
    rows = codes.shape[0]
    blocks = total // rows
    lane = lax.broadcasted_iota(jnp.int32, (1, KDIM), 1)
    inverse = jnp.exp((lane % (KDIM // 2)).astype(F32) * (-math.log(10000.0) / (KDIM // 2)))
    sign = jnp.where(lane < KDIM // 2, -1.0, 1.0)
    offset = lax.broadcasted_iota(jnp.int32, (rows, KDIM), 0)
    for copy in copies[:3]:
        copy.wait()
    codes_out[...] = raw_codes[...].astype(F32).astype(BF16)
    gain_out[...] = raw_gain[...].reshape(gain_out.shape)
    last_out[...] = raw_last[...].reshape(last_out.shape)

    def step(begin):
        place = lax.rem(pos + blocks - begin // rows, blocks) * rows + offset
        angle = jnp.where(strand == 0, place, total - 1 - place).astype(F32) * inverse
        cosine[pl.ds(begin, rows), :] = jnp.cos(angle)
        sine[pl.ds(begin, rows), :] = jnp.sin(angle) * sign

    if blocks <= 4:
        for i in range(blocks):
            step(i * rows)
    else:
        over_blocks(total, rows, step)
    for copy in copies[3:]:
        copy.wait()


def absorb(onehot, table, rows, start, width, weights, before, after):
    kv_t, w_query, gain = weights
    total = onehot.shape[0]
    block = min(total, 4 * rows)
    cols = pl.ds(pl.multiple_of(start, LANES), width)

    def some(here):
        found = matmul(onehot[here, :], table[...]).astype(BF16)
        floats = found.astype(F32)
        return found, floats, (floats * gain[:, cols]).astype(BF16)

    def step(begin):
        here = pl.ds(begin, block)
        found, floats, gained = some(here)
        square = jnp.sum(floats * floats, axis=1, keepdims=True)
        kv = matmul_t(gained, kv_t[:, cols])
        after[0][here, :] = square if before is None else before[0][here, :] + square
        after[1][here, :] = kv if before is None else before[1][here, :] + kv
        return found, gained

    if total == block:
        found, gained = step(0)
        found, gained = found[:rows], gained[:rows]
    else:
        over_blocks(total, block, lambda begin: step(begin) and None)
        found, _, gained = some(pl.ds(0, rows))
    query = matmul(gained, w_query[cols, :])
    after[2][...] = query if before is None else before[2][...] + query
    return found


def own_kernel(blocks, kv_steps, *refs):
    codes = refs[:blocks]
    table, key_t, value_t = refs[blocks : blocks + 3]
    parts = refs[blocks + 3 : blocks + 3 + len(kv_steps)]
    w_query, gain, onehot, kv_t, own, square, kv_sum, q_sum, all_codes = refs[blocks + 3 + len(kv_steps) :]
    strand, mine, group = lax.axis_index("strand"), lax.axis_index("heads"), lax.axis_index("groups")
    size, groups = lax.axis_size("heads"), lax.axis_size("groups")
    key_cols, value_cols = key_t.shape[0], value_t.shape[0]
    entries, width = table.shape
    half = entries // 2
    rows = codes[0].shape[0]
    total = blocks * rows
    for i in range(blocks):
        all_codes[i * rows : (i + 1) * rows, :] = codes[i][...]

    def kv_rows(owner):
        key_rows = pl.ds(pl.multiple_of(owner * key_cols, 16), key_cols)
        return key_rows, pl.ds(pl.multiple_of(KDIM + owner * value_cols, 16), value_cols)

    key_rows, value_rows = kv_rows(mine)
    kv_t[key_rows, :] = key_t[...]
    kv_t[value_rows, :] = value_t[...]
    for piece, (step, group_step, core_step) in zip(parts, kv_steps):
        key_rows, value_rows = kv_rows(lax.rem(mine + size - step, size))
        core = strand if core_step == 0 else 1 - strand
        part = core * groups + lax.rem(group + groups - group_step, groups)
        cols = pl.ds(pl.multiple_of(part * piece.shape[1], LANES), piece.shape[1])
        kv_t[key_rows, cols] = piece[:key_cols, :]
        kv_t[value_rows, cols] = piece[key_cols:, :]
    spot = lax.broadcasted_iota(jnp.int32, (BIN, entries), 1)
    owner = jnp.where(spot < half, strand, 1 - strand)
    entry = owner * half + spot % half
    entry = jnp.where(strand == 0, entry, entries - 1 - entry)
    place = lax.broadcasted_iota(jnp.int32, (BIN, entries), 0)
    spread = jnp.where(place == entry // BASES, 1.0, 0.0).astype(BF16)
    wanted = (entry[:1] % BASES).astype(F32)
    block = min(total, 4 * rows)

    def mark(begin):
        here = pl.ds(begin, block)
        found = matmul(all_codes[here, :], spread) == wanted
        onehot[here, :] = jnp.where(found, 1.0, 0.0).astype(BF16)

    over_blocks(total, block, mark)
    own[...] = absorb(
        onehot, table, rows, mine * width, width, (kv_t, w_query, gain), None, (square, kv_sum, q_sum)
    )


def chunk_start(step, index, chunks, width):
    size = lax.axis_size("heads")
    owner = lax.rem(lax.axis_index("heads") + size - step, size)
    return (owner * chunks + index) * width


def chunk_kernel(step, index, chunks, rows, *refs):
    mine, theirs, onehot, kv_t, w_query, gain, square, kv_sum, q_sum = refs[:9]
    found, square_out, kv_out, q_out, table = refs[9:]
    half, width = mine.shape
    table[:half, :] = mine[...]
    table[half:, :] = theirs[...]
    found[...] = absorb(
        onehot,
        table,
        rows,
        chunk_start(step, index, chunks, width),
        width,
        (kv_t, w_query, gain),
        (square, kv_sum, q_sum),
        (square_out, kv_out, q_out),
    )


def turn(values, cosine, sine):
    floats = values.astype(BF16).astype(F32)
    return (floats * cosine + pltpu.roll(floats, KDIM // 2, 1) * sine).astype(BF16)


def attend_kernel(steps, chunks, *refs):
    mine, theirs, onehot, kv_t, w_query, gain, square, kv_sum, q_sum = refs[:9]
    own, cosine, sine, w_out = refs[9:13]
    founds = refs[13 : 13 + len(steps) - 1]
    share, merged, inputs, table, squares, sums, queries, keys, values = refs[12 + len(steps) :]
    half, width = mine.shape
    rows, own_width = own.shape
    features = inputs.shape[1]
    total = onehot.shape[0]
    block = min(total, 4 * rows)
    table[:half, :] = mine[...]
    table[half:, :] = theirs[...]
    start = chunk_start(*steps[-1], chunks, width)
    last = absorb(
        onehot, table, rows, start, width, (kv_t, w_query, gain), (square, kv_sum, q_sum), (squares, sums, queries)
    )
    inputs[:, pl.ds(pl.multiple_of(start, LANES), width)] = last
    for found, spot in zip(founds, steps):
        inputs[:, pl.ds(pl.multiple_of(chunk_start(*spot, chunks, width), LANES), width)] = found[...]
    begin = pl.multiple_of(lax.axis_index("heads") * own_width, LANES)
    inputs[:, pl.ds(begin, own_width)] = own[...]

    def finish(begin):
        here = pl.ds(begin, block)
        scaled = sums[here, :] * lax.rsqrt(squares[here, :] / features + 1e-06)
        keys[here, :] = turn(scaled[:, :KDIM], cosine[here, :], sine[here, :])
        values[here, :] = scaled[:, KDIM:].astype(BF16)

    over_blocks(total, block, finish)
    scaled = queries[...] * lax.rsqrt(squares[:rows, :] / features + 1e-06)
    for head in range(queries.shape[1] // KDIM):
        query = turn(scaled[:, head * KDIM : (head + 1) * KDIM], cosine[:rows, :], sine[:rows, :])
        scores = matmul_t(query, keys[...]) * KDIM ** (-0.5)
        weights = jnp.exp(scores - jnp.max(scores, axis=1, keepdims=True))
        weight_sum = jnp.sum(weights, axis=1, keepdims=True)
        found = (matmul(weights.astype(BF16), values[...]) / weight_sum).astype(BF16)
        merged[:, head * VDIM : (head + 1) * VDIM] = found
    share[...] = matmul(merged[...], w_out[:, : w_out.shape[1] // 2]).astype(BF16)


def second_kernel(merged, w_out, share):
    half = w_out.shape[1] // 2
    share[...] = matmul(merged[...], w_out[:, half:]).astype(BF16)


def gather_hidden(shares, inputs, gain, chunk):
    width = shares[0].shape[1]
    cols = slice(chunk * width, (chunk + 1) * width)
    total = shares[0][...].astype(F32)
    for other in shares[1:]:
        total = total + other[...].astype(F32)
    hidden = (inputs[:, cols].astype(F32) + total).astype(BF16).astype(F32)
    return jnp.sum(hidden * hidden, axis=1, keepdims=True), (hidden * gain[:, cols]).astype(BF16)


def soft(logits):
    return jnp.maximum(logits, 0.0) + jnp.log1p(jnp.exp(-jnp.abs(logits)))


def first_tracks_kernel(size, *refs):
    shares = refs[:size]
    inputs, gain, tracks, square, to_send, to_keep = refs[size:]
    strand = lax.axis_index("strand")
    width = shares[0].shape[1]
    square[...], gained = gather_hidden(shares, inputs, gain, 0)
    to_send[...] = matmul(gained, tracks[1 - strand, :width, :])
    to_keep[...] = matmul(gained, tracks[strand, :width, :])


def send_kernel(size, *refs):
    shares = refs[:size]
    inputs, gain, tracks, square, to_send, sent, gained_out, scale_out = refs[size:]
    strand = lax.axis_index("strand")
    width = shares[0].shape[1]
    total, gained = gather_hidden(shares, inputs, gain, 1)
    scale = lax.rsqrt((square[...] + total) / (2 * width) + 1e-06)
    logits = to_send[...] + matmul(gained, tracks[1 - strand, width:, :])
    sent[...] = soft(logits * scale).astype(BF16)
    gained_out[...] = gained
    scale_out[...] = scale


def keep_kernel(gained, tracks, to_keep, scale, kept):
    strand = lax.axis_index("strand")
    width = gained.shape[1]
    logits = to_keep[...] + matmul(gained[...], tracks[strand, width:, :])
    kept[...] = soft(logits * scale[...]).astype(BF16)


def average_kernel(kept, received, pairs, out):
    strand = lax.axis_index("strand")
    count = kept.shape[1]
    mine, theirs = kept[...].astype(F32), received[...].astype(F32)
    forward = jnp.where(strand == 0, mine, theirs)
    reverse = jnp.where(strand == 0, theirs, mine)
    index = lax.broadcasted_iota(jnp.int32, (1, count), 1)
    even = index % 2 == 0
    swapped = (pairs[...] % 2 == 0) != even
    partner = jnp.where(even, pltpu.roll(reverse, count - 1, 1), pltpu.roll(reverse, 1, 1))
    out[...] = 0.5 * (forward + jnp.where(swapped, partner, reverse))


def body(
    base_codes,
    embed_table,
    attn_gain,
    w_query,
    w_key,
    w_value,
    w_out,
    head_gain,
    w_tracks,
    track_pairs,
):
    rows = base_codes.shape[0] // BIN
    blocks = lax.axis_size("pos")
    size = lax.axis_size("heads")
    features, q_cols = w_query.shape
    entries, width = embed_table.shape
    groups = lax.axis_size("groups")
    key_t, value_t = w_key.T, w_value.T
    kv_cols = key_t.shape[0] + value_t.shape[0]
    kv_all = KDIM + VDIM
    half = entries // 2
    total = blocks * rows
    tracks_half = w_tracks.shape[2]
    chunks = 2 if width % (2 * LANES) == 0 else 1
    wide = width // chunks

    hbm = pltpu.HBM
    part_kv, *own_pieces = call(
        functools.partial(stage_kernel, chunks),
        [shape((kv_cols, features // (2 * groups)), BF16)] + [shape((half, wide), BF16)] * chunks,
        [embed_table, key_t, value_t],
        "stage",
        scratch=[pltpu.SemaphoreType.DMA((2 + chunks,))],
        spaces=[hbm] * 3,
    )
    table, key_own, value_own, query_own, gain, last_gain, cosine, sine, own_codes = call(
        prepare_kernel,
        [
            shape((entries, width), BF16),
            shape(key_t.shape, BF16),
            shape(value_t.shape, BF16),
            shape(w_query.shape, BF16),
            shape((1, features), F32),
            shape((1, features), F32),
            shape((total, KDIM), F32),
            shape((total, KDIM), F32),
            shape((rows, BIN), BF16),
        ],
        [embed_table, key_t, value_t, w_query, attn_gain, head_gain, base_codes.reshape(rows, BIN)],
        "prepare",
        scratch=[
            pltpu.VMEM((features,), F32),
            pltpu.VMEM((features,), F32),
            pltpu.VMEM((rows, BIN), jnp.int32),
            pltpu.SemaphoreType.DMA((8,)),
        ],
        spaces=[hbm] * 7,
    )
    kv_parts, kv_steps, pieces, steps = [], [], [], []
    from_heads = [shifted(part_kv, "heads", step) for step in range(1, size)]
    if from_heads:
        from_heads[0], own_codes = lax.optimization_barrier((from_heads[0], own_codes))
    codes = [own_codes] + [shifted(own_codes, "pos", k) for k in range(1, blocks)]
    for step in range(1, size):
        for k in range(groups):
            here = from_heads[step - 1] if k == 0 else shifted(from_heads[step - 1], "groups", k)
            if step == 1 and k == groups - 1:
                here, *codes = lax.optimization_barrier((here, *codes))
            kv_parts += [here, shifted(here, "strand", 1)]
            kv_steps += [(step, k, 0), (step, k, 1)]
    for step in range(1, size):
        for i in range(chunks):
            here = shifted(own_pieces[i], "heads", step)
            pieces.append((here, shifted(here, "strand", 1)))
            steps.append((step, i))

    sums = [shape((total, 1), F32), shape((total, kv_all), F32), shape((rows, q_cols), F32)]
    onehot, kv_t, own, *state = call(
        functools.partial(own_kernel, blocks, kv_steps),
        [shape((total, entries), BF16), shape((kv_all, features), BF16), shape((rows, width), BF16)] + sums,
        codes + [table, key_own, value_own] + kv_parts + [query_own, gain],
        "own_features",
        scratch=[pltpu.VMEM((total, BIN), BF16)],
        flops=2 * total * width * (entries + kv_all),
        spare=8 * total * entries,
    )
    founds = []
    for (step, i), pair in zip(steps[:-1], pieces[:-1]):
        found, *state = call(
            functools.partial(chunk_kernel, step, i, chunks, rows),
            [shape((rows, wide), BF16)] + sums,
            list(pair) + [onehot, kv_t, query_own, gain] + state,
            "other_features",
            scratch=[pltpu.VMEM((entries, wide), BF16)],
            flops=2 * total * wide * (entries + kv_all),
            spare=8 * total * entries,
        )
        founds.append(found)
    o_cols = q_cols // KDIM * VDIM
    share_one, merged, inputs = call(
        functools.partial(attend_kernel, steps, chunks),
        [
            shape((rows, features // 2), BF16),
            shape((rows, o_cols), BF16),
            shape((rows, features), BF16),
        ],
        list(pieces[-1]) + [onehot, kv_t, query_own, gain] + state + [own, cosine, sine, w_out] + founds,
        "attend",
        scratch=[
            pltpu.VMEM((entries, wide), BF16),
            pltpu.VMEM((total, 1), F32),
            pltpu.VMEM((total, kv_all), F32),
            pltpu.VMEM((rows, q_cols), F32),
            pltpu.VMEM((total, KDIM), BF16),
            pltpu.VMEM((total, VDIM), BF16),
        ],
        flops=2 * total * wide * (entries + kv_all) + 2 * total * q_cols * rows * 3,
        spare=8 * total * entries,
    )
    (share_two,) = call(
        second_kernel,
        [shape((rows, features // 2), BF16)],
        [merged, w_out],
        "second_share",
        flops=rows * o_cols * features,
    )
    ones = [share_one] + [shifted(share_one, "heads", k) for k in range(1, size)]
    twos = [share_two] + [shifted(share_two, "heads", k) for k in range(1, size)]
    weights, _ = lax.optimization_barrier((w_tracks, share_two))
    tracks = lax.optimization_barrier(weights.transpose(1, 0, 2))
    square, to_send, to_keep = call(
        functools.partial(first_tracks_kernel, size),
        [
            shape((rows, 1), F32),
            shape((rows, tracks_half), F32),
            shape((rows, tracks_half), F32),
        ],
        ones + [inputs, last_gain, tracks],
        "first_tracks",
        flops=2 * rows * features * tracks_half,
    )
    sent, gained, scale = call(
        functools.partial(send_kernel, size),
        [
            shape((rows, tracks_half), BF16),
            shape((rows, features // 2), BF16),
            shape((rows, 1), F32),
        ],
        twos + [inputs, last_gain, tracks, square, to_send],
        "sent_tracks",
        flops=rows * features * tracks_half,
    )
    received = shifted(sent, "strand", 1)
    (kept,) = call(
        keep_kernel,
        [shape((rows, tracks_half), BF16)],
        [gained, tracks, to_keep, scale],
        "kept_tracks",
        flops=rows * features * tracks_half,
    )
    (out,) = call(
        average_kernel,
        [shape((rows, tracks_half), F32)],
        [kept, received, track_pairs.reshape(1, tracks_half)],
        "average",
    )
    return out


def solution(mesh):
    placed = (
        P(("groups", "pos")),
        P(None, "heads"),
        P(),
        P(None, "heads"),
        P(None, "heads"),
        P(None, "heads"),
        P("heads", None),
        P(),
        P(None, None, "heads"),
        P(("strand", "heads")),
    )
    return jax.shard_map(
        body,
        mesh=mesh,
        in_specs=placed,
        out_specs=P(("groups", "pos"), ("strand", "heads")),
        check_vma=False,
    )
```

```python
import functools
import math

import jax
import jax.experimental.pallas as pl
import jax.experimental.pallas.tpu as pltpu
import jax.numpy as jnp
from jax import lax
from jax.sharding import PartitionSpec as P

KDIM = 128
VDIM = 192
BIN = 128
BASES = 4
LANES = 128
VMEM_LIMIT = 48 * 2**20
F32 = jnp.float32
BF16 = jnp.bfloat16


def shifted(value, axis, distance):
    size = lax.axis_size(axis)
    return lax.ppermute(value, axis, [(i, (i + distance) % size) for i in range(size)])


def matmul(a, b):
    return jnp.dot(a, b, preferred_element_type=F32)


def matmul_t(a, b):
    return lax.dot_general(a, b, (((1,), (1,)), ((), ())), preferred_element_type=F32)


def call(kernel, outs, operands, name, scratch=(), spaces=None, flops=0, spare=0):
    vmem = pl.BlockSpec(memory_space=pltpu.VMEM)
    spaces = spaces or [None] * len(operands)
    operands = [
        v if s is None else pltpu.with_memory_space_constraint(v, s) for v, s in zip(operands, spaces)
    ]
    specs = [vmem if s is None else pl.BlockSpec(memory_space=s) for s in spaces]
    held = [v for v, s in zip(operands, spaces) if s is None] + list(outs)
    held += [v for v in scratch if hasattr(v, "shape") and hasattr(v, "dtype") and v.memory_space == pltpu.VMEM]
    moved = sum(math.prod(v.shape[:-1]) * max(v.shape[-1], LANES) * jnp.dtype(v.dtype).itemsize for v in held)
    return pl.pallas_call(
        kernel,
        out_shape=list(outs),
        in_specs=specs,
        out_specs=[vmem] * len(outs),
        scratch_shapes=list(scratch),
        compiler_params=pltpu.CompilerParams(
            vmem_limit_bytes=min(VMEM_LIMIT, moved + moved // 4 + 6 * 2**20 + spare)
        ),
        cost_estimate=pl.CostEstimate(flops=flops, bytes_accessed=moved, transcendentals=0),
        name=name,
    )(*operands)


def shape(dims, dtype):
    return jax.ShapeDtypeStruct(tuple(dims), dtype)


def over_blocks(total, block, step):
    if total == block:
        step(0)
    else:

        def one(i, carry):
            step(pl.multiple_of(i * block, block))
            return carry

        lax.fori_loop(0, total // block, one, 0)


def stage_kernel(chunks, embed, key_t, value_t, codes, *refs):
    part_kv, pieces = refs[0], refs[1 : 1 + chunks]
    codes_out, raw_codes, sems = refs[1 + chunks :]
    strand = lax.axis_index("strand")
    part = strand * lax.axis_size("groups") + lax.axis_index("groups")
    key_cols, value_cols = key_t.shape[0], value_t.shape[0]
    kv_width = part_kv.shape[1]
    half, width = pieces[0].shape
    cols = pl.ds(pl.multiple_of(part * kv_width, LANES), kv_width)
    rows = pl.ds(pl.multiple_of(strand * half, half), half)
    copies = [
        pltpu.make_async_copy(key_t.at[:, cols], part_kv.at[pl.ds(0, key_cols)], sems.at[0]),
        pltpu.make_async_copy(value_t.at[:, cols], part_kv.at[pl.ds(key_cols, value_cols)], sems.at[1]),
    ]
    for i in range(chunks):
        source = embed.at[rows, pl.ds(i * width, width)]
        copies.append(pltpu.make_async_copy(source, pieces[i], sems.at[2 + i]))
    copies.append(pltpu.make_async_copy(codes, raw_codes, sems.at[2 + chunks]))
    for copy in copies:
        copy.start()
    copies[-1].wait()
    codes_out[...] = raw_codes[...].astype(F32).astype(BF16)
    for copy in copies[:-1]:
        copy.wait()


def prepare_kernel(rows, embed, key_t, value_t, w_query, gain, last_gain, *refs):
    table, key_out, value_out, query_out, gain_out, last_out, cosine, sine = refs[:8]
    raw_gain, raw_last, sems = refs[8:]
    strand, pos = lax.axis_index("strand"), lax.axis_index("pos")
    half = embed.shape[0] // 2
    pairs = [(gain, raw_gain), (last_gain, raw_last)]
    for i in range(2):
        part = strand if i == 0 else 1 - strand
        source = embed.at[pl.ds(pl.multiple_of(part * half, half), half)]
        pairs.append((source, table.at[pl.ds(i * half, half)]))
    pairs += [(key_t, key_out), (value_t, value_out), (w_query, query_out)]
    copies = [pltpu.make_async_copy(a, b, sems.at[i]) for i, (a, b) in enumerate(pairs)]
    for copy in copies:
        copy.start()
    total = cosine.shape[0]
    blocks = total // rows
    lane = lax.broadcasted_iota(jnp.int32, (1, KDIM), 1)
    inverse = jnp.exp((lane % (KDIM // 2)).astype(F32) * (-math.log(10000.0) / (KDIM // 2)))
    sign = jnp.where(lane < KDIM // 2, -1.0, 1.0)
    offset = lax.broadcasted_iota(jnp.int32, (rows, KDIM), 0)
    for copy in copies[:2]:
        copy.wait()
    gain_out[...] = raw_gain[...].reshape(gain_out.shape)
    last_out[...] = raw_last[...].reshape(last_out.shape)

    def step(begin):
        place = lax.rem(pos + blocks - begin // rows, blocks) * rows + offset
        angle = jnp.where(strand == 0, place, total - 1 - place).astype(F32) * inverse
        cosine[pl.ds(begin, rows), :] = jnp.cos(angle)
        sine[pl.ds(begin, rows), :] = jnp.sin(angle) * sign

    if blocks <= 4:
        for i in range(blocks):
            step(i * rows)
    else:
        over_blocks(total, rows, step)
    for copy in copies[2:]:
        copy.wait()


def fetch_kernel(w_out, first_out, second_out, sems):
    out_half = first_out.shape[1]
    copies = [
        pltpu.make_async_copy(w_out.at[:, pl.ds(0, out_half)], first_out, sems.at[0]),
        pltpu.make_async_copy(w_out.at[:, pl.ds(out_half, out_half)], second_out, sems.at[1]),
    ]
    for copy in copies:
        copy.start()
    for copy in copies:
        copy.wait()


def absorb(onehot, table, rows, start, width, weights, before, after):
    kv_t, w_query, gain = weights
    total = onehot.shape[0]
    block = min(total, 4 * rows)
    cols = pl.ds(pl.multiple_of(start, LANES), width)

    def some(here):
        found = matmul(onehot[here, :], table[...]).astype(BF16)
        floats = found.astype(F32)
        return found, floats, (floats * gain[:, cols]).astype(BF16)

    def step(begin):
        here = pl.ds(begin, block)
        found, floats, gained = some(here)
        square = jnp.sum(floats * floats, axis=1, keepdims=True)
        kv = matmul_t(gained, kv_t[:, cols])
        after[0][here, :] = square if before is None else before[0][here, :] + square
        after[1][here, :] = kv if before is None else before[1][here, :] + kv
        return found, gained

    if total == block:
        found, gained = step(0)
        found, gained = found[:rows], gained[:rows]
    else:
        over_blocks(total, block, lambda begin: step(begin) and None)
        found, _, gained = some(pl.ds(0, rows))
    query = matmul(gained, w_query[cols, :])
    after[2][...] = query if before is None else before[2][...] + query
    return found


def own_kernel(code_steps, kv_steps, *refs):
    blocks = len(code_steps)
    codes = refs[:blocks]
    table, key_t, value_t = refs[blocks : blocks + 3]
    parts = refs[blocks + 3 : blocks + 3 + len(kv_steps)]
    w_query, gain, onehot, kv_t, own, square, kv_sum, q_sum, all_codes = refs[blocks + 3 + len(kv_steps) :]
    strand, mine, group = lax.axis_index("strand"), lax.axis_index("heads"), lax.axis_index("groups")
    size, groups = lax.axis_size("heads"), lax.axis_size("groups")
    key_cols, value_cols = key_t.shape[0], value_t.shape[0]
    entries, width = table.shape
    half = entries // 2
    rows = codes[0].shape[0]
    total = blocks * rows
    for piece, (forward, reverse) in zip(codes, code_steps):
        spot = jnp.where(strand == 0, forward, reverse) * rows
        all_codes[pl.ds(pl.multiple_of(spot, rows), rows), :] = piece[...]

    def kv_rows(owner):
        key_rows = pl.ds(pl.multiple_of(owner * key_cols, 16), key_cols)
        return key_rows, pl.ds(pl.multiple_of(KDIM + owner * value_cols, 16), value_cols)

    key_rows, value_rows = kv_rows(mine)
    kv_t[key_rows, :] = key_t[...]
    kv_t[value_rows, :] = value_t[...]
    for piece, (step, group_step, core_step) in zip(parts, kv_steps):
        key_rows, value_rows = kv_rows(lax.rem(mine + size - step, size))
        core = strand if core_step == 0 else 1 - strand
        part = core * groups + lax.rem(group + groups - group_step, groups)
        cols = pl.ds(pl.multiple_of(part * piece.shape[1], LANES), piece.shape[1])
        kv_t[key_rows, cols] = piece[:key_cols, :]
        kv_t[value_rows, cols] = piece[key_cols:, :]
    spot = lax.broadcasted_iota(jnp.int32, (BIN, entries), 1)
    owner = jnp.where(spot < half, strand, 1 - strand)
    entry = owner * half + spot % half
    entry = jnp.where(strand == 0, entry, entries - 1 - entry)
    place = lax.broadcasted_iota(jnp.int32, (BIN, entries), 0)
    spread = jnp.where(place == entry // BASES, 1.0, 0.0).astype(BF16)
    wanted = (entry[:1] % BASES).astype(F32)
    block = min(total, 4 * rows)

    def mark(begin):
        here = pl.ds(begin, block)
        found = matmul(all_codes[here, :], spread) == wanted
        onehot[here, :] = jnp.where(found, 1.0, 0.0).astype(BF16)

    over_blocks(total, block, mark)
    own[...] = absorb(
        onehot, table, rows, mine * width, width, (kv_t, w_query, gain), None, (square, kv_sum, q_sum)
    )


def chunk_start(step, index, chunks, width):
    size = lax.axis_size("heads")
    owner = lax.rem(lax.axis_index("heads") + size - step, size)
    return (owner * chunks + index) * width


def chunk_kernel(step, index, chunks, rows, *refs):
    mine, theirs, onehot, kv_t, w_query, gain, square, kv_sum, q_sum = refs[:9]
    found, square_out, kv_out, q_out, table = refs[9:]
    half, width = mine.shape
    table[:half, :] = mine[...]
    table[half:, :] = theirs[...]
    found[...] = absorb(
        onehot,
        table,
        rows,
        chunk_start(step, index, chunks, width),
        width,
        (kv_t, w_query, gain),
        (square, kv_sum, q_sum),
        (square_out, kv_out, q_out),
    )


def turn(values, cosine, sine):
    floats = values.astype(BF16).astype(F32)
    return (floats * cosine + pltpu.roll(floats, KDIM // 2, 1) * sine).astype(BF16)


def attend_kernel(steps, chunks, *refs):
    mine, theirs, onehot, kv_t, w_query, gain, square, kv_sum, q_sum = refs[:9]
    own, cosine, sine, first_out = refs[9:13]
    founds = refs[13 : 13 + len(steps) - 1]
    share, merged, inputs = refs[12 + len(steps) : 15 + len(steps)]
    table, squares, sums, queries, keys, values = refs[15 + len(steps) :]
    half, width = mine.shape
    rows, own_width = own.shape
    features = inputs.shape[1]
    total = onehot.shape[0]
    block = min(total, 4 * rows)
    table[:half, :] = mine[...]
    table[half:, :] = theirs[...]
    start = chunk_start(*steps[-1], chunks, width)
    last = absorb(
        onehot, table, rows, start, width, (kv_t, w_query, gain), (square, kv_sum, q_sum), (squares, sums, queries)
    )
    inputs[:, pl.ds(pl.multiple_of(start, LANES), width)] = last
    for found, spot in zip(founds, steps):
        inputs[:, pl.ds(pl.multiple_of(chunk_start(*spot, chunks, width), LANES), width)] = found[...]
    begin = pl.multiple_of(lax.axis_index("heads") * own_width, LANES)
    inputs[:, pl.ds(begin, own_width)] = own[...]

    def finish(begin):
        here = pl.ds(begin, block)
        scaled = sums[here, :] * lax.rsqrt(squares[here, :] / features + 1e-06)
        keys[here, :] = turn(scaled[:, :KDIM], cosine[here, :], sine[here, :])
        values[here, :] = scaled[:, KDIM:].astype(BF16)

    over_blocks(total, block, finish)
    scaled = queries[...] * lax.rsqrt(squares[:rows, :] / features + 1e-06)
    for head in range(queries.shape[1] // KDIM):
        query = turn(scaled[:, head * KDIM : (head + 1) * KDIM], cosine[:rows, :], sine[:rows, :])
        scores = matmul_t(query, keys[...]) * KDIM ** (-0.5)
        weights = jnp.exp(scores - jnp.max(scores, axis=1, keepdims=True))
        weight_sum = jnp.sum(weights, axis=1, keepdims=True)
        found = (matmul(weights.astype(BF16), values[...]) / weight_sum).astype(BF16)
        merged[:, head * VDIM : (head + 1) * VDIM] = found
    share[...] = matmul(merged[...], first_out[...]).astype(BF16)


def second_kernel(merged, second_out, share):
    share[...] = matmul(merged[...], second_out[...]).astype(BF16)


def gather_hidden(shares, inputs, gain, chunk):
    width = shares[0].shape[1]
    cols = slice(chunk * width, (chunk + 1) * width)
    total = shares[0][...].astype(F32)
    for other in shares[1:]:
        total = total + other[...].astype(F32)
    hidden = (inputs[:, cols].astype(F32) + total).astype(BF16).astype(F32)
    return jnp.sum(hidden * hidden, axis=1, keepdims=True), (hidden * gain[:, cols]).astype(BF16)


def soft(logits):
    return jnp.maximum(logits, 0.0) + jnp.log1p(jnp.exp(-jnp.abs(logits)))


def first_tracks_kernel(size, *refs):
    shares = refs[:size]
    inputs, gain, tracks, square, to_send, to_keep = refs[size:]
    strand = lax.axis_index("strand")
    width = shares[0].shape[1]
    square[...], gained = gather_hidden(shares, inputs, gain, 0)
    to_send[...] = matmul(gained, tracks[1 - strand, :width, :])
    to_keep[...] = matmul(gained, tracks[strand, :width, :])


def send_kernel(size, *refs):
    shares = refs[:size]
    inputs, gain, tracks, square, to_send, sent, gained_out, scale_out = refs[size:]
    strand = lax.axis_index("strand")
    width = shares[0].shape[1]
    total, gained = gather_hidden(shares, inputs, gain, 1)
    scale = lax.rsqrt((square[...] + total) / (2 * width) + 1e-06)
    logits = to_send[...] + matmul(gained, tracks[1 - strand, width:, :])
    sent[...] = soft(logits * scale).astype(BF16)
    gained_out[...] = gained
    scale_out[...] = scale


def keep_kernel(gained, tracks, to_keep, scale, kept):
    strand = lax.axis_index("strand")
    width = gained.shape[1]
    logits = to_keep[...] + matmul(gained[...], tracks[strand, width:, :])
    kept[...] = soft(logits * scale[...]).astype(BF16)


def average_kernel(kept, received, pairs, out):
    strand = lax.axis_index("strand")
    count = kept.shape[1]
    mine, theirs = kept[...].astype(F32), received[...].astype(F32)
    forward = jnp.where(strand == 0, mine, theirs)
    reverse = jnp.where(strand == 0, theirs, mine)
    index = lax.broadcasted_iota(jnp.int32, (1, count), 1)
    even = index % 2 == 0
    swapped = (pairs[...] % 2 == 0) != even
    partner = jnp.where(even, pltpu.roll(reverse, count - 1, 1), pltpu.roll(reverse, 1, 1))
    out[...] = 0.5 * (forward + jnp.where(swapped, partner, reverse))


def body(
    base_codes,
    embed_table,
    attn_gain,
    w_query,
    w_key,
    w_value,
    w_out,
    head_gain,
    w_tracks,
    track_pairs,
):
    rows = base_codes.shape[0] // BIN
    blocks = lax.axis_size("pos")
    size = lax.axis_size("heads")
    features, q_cols = w_query.shape
    entries, width = embed_table.shape
    groups = lax.axis_size("groups")
    key_t, value_t = w_key.T, w_value.T
    kv_cols = key_t.shape[0] + value_t.shape[0]
    kv_all = KDIM + VDIM
    half = entries // 2
    total = blocks * rows
    tracks_half = w_tracks.shape[2]
    chunks = 2 if width % (2 * LANES) == 0 else 1
    wide = width // chunks

    hbm = pltpu.HBM
    part_kv, *own_pieces, own_codes = call(
        functools.partial(stage_kernel, chunks),
        [shape((kv_cols, features // (2 * groups)), BF16)]
        + [shape((half, wide), BF16)] * chunks
        + [shape((rows, BIN), BF16)],
        [embed_table, key_t, value_t, base_codes.reshape(rows, BIN)],
        "stage",
        scratch=[pltpu.VMEM((rows, BIN), jnp.int32), pltpu.SemaphoreType.DMA((3 + chunks,))],
        spaces=[hbm] * 4,
    )
    table, key_own, value_own, query_own, gain, last_gain, cosine, sine = call(
        functools.partial(prepare_kernel, rows),
        [
            shape((entries, width), BF16),
            shape(key_t.shape, BF16),
            shape(value_t.shape, BF16),
            shape(w_query.shape, BF16),
            shape((1, features), F32),
            shape((1, features), F32),
            shape((total, KDIM), F32),
            shape((total, KDIM), F32),
        ],
        [embed_table, key_t, value_t, w_query, attn_gain, head_gain],
        "prepare",
        scratch=[
            pltpu.VMEM((features,), F32),
            pltpu.VMEM((features,), F32),
            pltpu.SemaphoreType.DMA((7,)),
        ],
        spaces=[hbm] * 6,
    )
    kv_parts, kv_steps, pieces, steps = [], [], [], []
    from_heads = [shifted(part_kv, "heads", step) for step in range(1, size)]
    if from_heads:
        from_heads[0], table = lax.optimization_barrier((from_heads[0], table))
    to_core = [shifted(here, "strand", 1) for here in from_heads]
    out_in = w_out
    if to_core:
        out_in = w_out
    first_out, second_out = call(
        fetch_kernel,
        [shape((w_out.shape[0], features // 2), BF16)] * 2,
        [out_in],
        "fetch_out",
        scratch=[pltpu.SemaphoreType.DMA((2,))],
        spaces=[hbm],
    )
    raw, raw_steps = [], []
    for k in range(1, blocks, 2):
        if k + 1 < blocks:
            pairs = [((p, s), ((p + k + s) % blocks, s)) for p in range(blocks) for s in range(2)]
            pairs = [(2 * p + s, 2 * q + t) for (p, s), (q, t) in pairs]
            raw.append(lax.ppermute(own_codes, ("pos", "strand"), pairs))
            raw_steps.append((k, k + 1))
        else:
            raw.append(shifted(own_codes, "pos", k))
            raw_steps.append((k, k))
    if raw:
        raw[0], first_out = lax.optimization_barrier((raw[0], first_out))
    for step in range(1, size):
        for k in range(groups):
            here = from_heads[step - 1] if k == 0 else shifted(from_heads[step - 1], "groups", k)
            if step == 1 and k == groups - 1 and blocks > 1:
                here, *raw = lax.optimization_barrier((here, *raw))
            kv_parts += [here, to_core[step - 1] if k == 0 else shifted(here, "strand", 1)]
            kv_steps += [(step, k, 0), (step, k, 1)]
    for step in range(1, size):
        for i in range(chunks):
            here = shifted(own_pieces[i], "heads", step)
            pieces.append((here, shifted(here, "strand", 1)))
            steps.append((step, i))

    codes, code_steps = [own_codes], [(0, 0)]
    for here, (mine, other) in zip(raw, raw_steps):
        codes.append(here)
        code_steps.append((mine, other))
        if mine != other:
            codes.append(shifted(here, "strand", 1))
            code_steps.append((other, mine))
    sums = [shape((total, 1), F32), shape((total, kv_all), F32), shape((rows, q_cols), F32)]
    onehot, kv_t, own, *state = call(
        functools.partial(own_kernel, code_steps, kv_steps),
        [shape((total, entries), BF16), shape((kv_all, features), BF16), shape((rows, width), BF16)] + sums,
        codes + [table, key_own, value_own] + kv_parts + [query_own, gain],
        "own_features",
        scratch=[pltpu.VMEM((total, BIN), BF16)],
        flops=2 * total * width * (entries + kv_all),
        spare=8 * total * entries,
    )
    founds = []
    for (step, i), pair in zip(steps[:-1], pieces[:-1]):
        found, *state = call(
            functools.partial(chunk_kernel, step, i, chunks, rows),
            [shape((rows, wide), BF16)] + sums,
            list(pair) + [onehot, kv_t, query_own, gain] + state,
            "other_features",
            scratch=[pltpu.VMEM((entries, wide), BF16)],
            flops=2 * total * wide * (entries + kv_all),
            spare=8 * total * entries,
        )
        founds.append(found)
    o_cols = q_cols // KDIM * VDIM
    share_one, merged, inputs = call(
        functools.partial(attend_kernel, steps, chunks),
        [
            shape((rows, features // 2), BF16),
            shape((rows, o_cols), BF16),
            shape((rows, features), BF16),
        ],
        list(pieces[-1]) + [onehot, kv_t, query_own, gain] + state + [own, cosine, sine, first_out] + founds,
        "attend",
        scratch=[
            pltpu.VMEM((entries, wide), BF16),
            pltpu.VMEM((total, 1), F32),
            pltpu.VMEM((total, kv_all), F32),
            pltpu.VMEM((rows, q_cols), F32),
            pltpu.VMEM((total, KDIM), BF16),
            pltpu.VMEM((total, VDIM), BF16),
        ],
        flops=2 * total * wide * (entries + kv_all) + 2 * total * q_cols * rows * 3,
        spare=8 * total * entries,
    )
    (share_two,) = call(
        second_kernel,
        [shape((rows, features // 2), BF16)],
        [merged, second_out],
        "second_share",
        flops=rows * o_cols * features,
    )
    ones = [share_one] + [shifted(share_one, "heads", k) for k in range(1, size)]
    twos = [share_two] + [shifted(share_two, "heads", k) for k in range(1, size)]
    weights, _ = lax.optimization_barrier((w_tracks, share_two))
    tracks = lax.optimization_barrier(weights.transpose(1, 0, 2))
    square, to_send, to_keep = call(
        functools.partial(first_tracks_kernel, size),
        [
            shape((rows, 1), F32),
            shape((rows, tracks_half), F32),
            shape((rows, tracks_half), F32),
        ],
        ones + [inputs, last_gain, tracks],
        "first_tracks",
        flops=2 * rows * features * tracks_half,
    )
    sent, gained, scale = call(
        functools.partial(send_kernel, size),
        [
            shape((rows, tracks_half), BF16),
            shape((rows, features // 2), BF16),
            shape((rows, 1), F32),
        ],
        twos + [inputs, last_gain, tracks, square, to_send],
        "sent_tracks",
        flops=rows * features * tracks_half,
    )
    received = shifted(sent, "strand", 1)
    (kept,) = call(
        keep_kernel,
        [shape((rows, tracks_half), BF16)],
        [gained, tracks, to_keep, scale],
        "kept_tracks",
        flops=rows * features * tracks_half,
    )
    (out,) = call(
        average_kernel,
        [shape((rows, tracks_half), F32)],
        [kept, received, track_pairs.reshape(1, tracks_half)],
        "average",
    )
    return out


def solution(mesh):
    placed = (
        P(("groups", "pos")),
        P(None, "heads"),
        P(),
        P(None, "heads"),
        P(None, "heads"),
        P(None, "heads"),
        P("heads", None),
        P(),
        P(None, None, "heads"),
        P(("strand", "heads")),
    )
    return jax.shard_map(
        body,
        mesh=mesh,
        in_specs=placed,
        out_specs=P(("groups", "pos"), ("strand", "heads")),
        check_vma=False,
    )
```

```python
import functools
import math

import jax
import jax.experimental.pallas as pl
import jax.experimental.pallas.tpu as pltpu
import jax.numpy as jnp
from jax import lax
from jax.sharding import PartitionSpec as P

KDIM = 128
VDIM = 192
BIN = 128
BASES = 4
LANES = 128
VMEM_LIMIT = 48 * 2**20
F32 = jnp.float32
BF16 = jnp.bfloat16


def shifted(value, axis, distance):
    size = lax.axis_size(axis)
    return lax.ppermute(value, axis, [(i, (i + distance) % size) for i in range(size)])


def matmul(a, b):
    return jnp.dot(a, b, preferred_element_type=F32)


def matmul_t(a, b):
    return lax.dot_general(a, b, (((1,), (1,)), ((), ())), preferred_element_type=F32)


def call(kernel, outs, operands, name, scratch=(), spaces=None, flops=0, spare=0):
    vmem = pl.BlockSpec(memory_space=pltpu.VMEM)
    spaces = spaces or [None] * len(operands)
    operands = [
        v if s is None else pltpu.with_memory_space_constraint(v, s) for v, s in zip(operands, spaces)
    ]
    specs = [vmem if s is None else pl.BlockSpec(memory_space=s) for s in spaces]
    held = [v for v, s in zip(operands, spaces) if s is None] + list(outs)
    held += [v for v in scratch if hasattr(v, "shape") and hasattr(v, "dtype") and v.memory_space == pltpu.VMEM]
    moved = sum(math.prod(v.shape[:-1]) * max(v.shape[-1], LANES) * jnp.dtype(v.dtype).itemsize for v in held)
    return pl.pallas_call(
        kernel,
        out_shape=list(outs),
        in_specs=specs,
        out_specs=[vmem] * len(outs),
        scratch_shapes=list(scratch),
        compiler_params=pltpu.CompilerParams(
            vmem_limit_bytes=min(VMEM_LIMIT, moved + moved // 4 + 6 * 2**20 + spare)
        ),
        cost_estimate=pl.CostEstimate(flops=flops, bytes_accessed=moved, transcendentals=0),
        name=name,
    )(*operands)


def shape(dims, dtype):
    return jax.ShapeDtypeStruct(tuple(dims), dtype)


def over_blocks(total, block, step):
    if total == block:
        step(0)
    else:

        def one(i, carry):
            step(pl.multiple_of(i * block, block))
            return carry

        lax.fori_loop(0, total // block, one, 0)


def stage_kernel(chunks, embed, key_t, value_t, codes, *refs):
    part_kv, pieces = refs[0], refs[1 : 1 + chunks]
    codes_out, raw_codes, sems = refs[1 + chunks :]
    strand = lax.axis_index("strand")
    part = strand * lax.axis_size("groups") + lax.axis_index("groups")
    key_cols, value_cols = key_t.shape[0], value_t.shape[0]
    kv_width = part_kv.shape[1]
    half, width = pieces[0].shape
    cols = pl.ds(pl.multiple_of(part * kv_width, LANES), kv_width)
    rows = pl.ds(pl.multiple_of(strand * half, half), half)
    copies = [
        pltpu.make_async_copy(key_t.at[:, cols], part_kv.at[pl.ds(0, key_cols)], sems.at[0]),
        pltpu.make_async_copy(value_t.at[:, cols], part_kv.at[pl.ds(key_cols, value_cols)], sems.at[1]),
    ]
    for i in range(chunks):
        source = embed.at[rows, pl.ds(i * width, width)]
        copies.append(pltpu.make_async_copy(source, pieces[i], sems.at[2 + i]))
    copies.append(pltpu.make_async_copy(codes, raw_codes, sems.at[2 + chunks]))
    for copy in copies:
        copy.start()
    copies[-1].wait()
    codes_out[...] = raw_codes[...].astype(F32).astype(BF16)
    for copy in copies[:-1]:
        copy.wait()


def prepare_kernel(rows, slots, embed, key_t, value_t, w_query, gain, last_gain, *refs):
    table, key_out, value_out, query_out, gain_out, last_out, cosine, sine = refs[:8]
    raw_gain, raw_last, sems = refs[8:]
    strand, pos = lax.axis_index("strand"), lax.axis_index("pos")
    half = embed.shape[0] // 2
    pairs = [(gain, raw_gain), (last_gain, raw_last)]
    for i in range(2):
        part = strand if i == 0 else 1 - strand
        source = embed.at[pl.ds(pl.multiple_of(part * half, half), half)]
        pairs.append((source, table.at[pl.ds(i * half, half)]))
    pairs += [(key_t, key_out), (value_t, value_out), (w_query, query_out)]
    copies = [pltpu.make_async_copy(a, b, sems.at[i]) for i, (a, b) in enumerate(pairs)]
    for copy in copies:
        copy.start()
    total = cosine.shape[0]
    blocks = total // rows
    lane = lax.broadcasted_iota(jnp.int32, (1, KDIM), 1)
    inverse = jnp.exp((lane % (KDIM // 2)).astype(F32) * (-math.log(10000.0) / (KDIM // 2)))
    sign = jnp.where(lane < KDIM // 2, -1.0, 1.0)
    offset = lax.broadcasted_iota(jnp.int32, (rows, KDIM), 0)
    for copy in copies[:2]:
        copy.wait()
    gain_out[...] = raw_gain[...].reshape(gain_out.shape)
    last_out[...] = raw_last[...].reshape(last_out.shape)

    for i, (forward, reverse) in enumerate(slots):
        behind = jnp.where(strand == 0, forward, reverse)
        place = lax.rem(pos + blocks - behind, blocks) * rows + offset
        angle = jnp.where(strand == 0, place, total - 1 - place).astype(F32) * inverse
        cosine[i * rows : (i + 1) * rows, :] = jnp.cos(angle)
        sine[i * rows : (i + 1) * rows, :] = jnp.sin(angle) * sign
    for copy in copies[2:]:
        copy.wait()


def fetch_kernel(w_out, first_out, second_out, sems):
    out_half = first_out.shape[1]
    copies = [
        pltpu.make_async_copy(w_out.at[:, pl.ds(0, out_half)], first_out, sems.at[0]),
        pltpu.make_async_copy(w_out.at[:, pl.ds(out_half, out_half)], second_out, sems.at[1]),
    ]
    for copy in copies:
        copy.start()
    for copy in copies:
        copy.wait()


def block_of(count, rows):
    if count <= 4 * rows:
        return count
    return 4 * rows if count % (4 * rows) == 0 else rows


def mark(onehot, codes, first, entries, rows):
    strand = lax.axis_index("strand")
    half = entries // 2
    count = codes.shape[0]
    spot = lax.broadcasted_iota(jnp.int32, (BIN, entries), 1)
    owner = jnp.where(spot < half, strand, 1 - strand)
    entry = owner * half + spot % half
    entry = jnp.where(strand == 0, entry, entries - 1 - entry)
    place = lax.broadcasted_iota(jnp.int32, (BIN, entries), 0)
    spread = jnp.where(place == entry // BASES, 1.0, 0.0).astype(BF16)
    wanted = (entry[:1] % BASES).astype(F32)
    block = block_of(count, rows)

    def step(begin):
        found = matmul(codes[pl.ds(begin, block), :], spread) == wanted
        onehot[pl.ds(first + begin, block), :] = jnp.where(found, 1.0, 0.0).astype(BF16)

    over_blocks(count, block, step)


def absorb(onehot, span, table, rows, start, width, weights, before, after):
    kv_t, w_query, gain = weights
    first, count = span
    block = block_of(count, rows)
    cols = pl.ds(pl.multiple_of(start, LANES), width)

    def some(here):
        found = matmul(onehot[here, :], table[...]).astype(BF16)
        floats = found.astype(F32)
        return found, floats, (floats * gain[:, cols]).astype(BF16)

    def step(begin):
        here = pl.ds(first + begin, block)
        found, floats, gained = some(here)
        square = jnp.sum(floats * floats, axis=1, keepdims=True)
        kv = matmul_t(gained, kv_t[:, cols])
        after[0][here, :] = square if before is None else before[0][here, :] + square
        after[1][here, :] = kv if before is None else before[1][here, :] + kv
        return found, gained

    if count == block:
        found, gained = step(0)
        found, gained = found[:rows], gained[:rows]
    else:
        over_blocks(count, block, lambda begin: step(begin) and None)
        found, _, gained = some(pl.ds(0, rows))
    if first:
        return None
    query = matmul(gained, w_query[cols, :])
    after[2][...] = query if before is None else before[2][...] + query
    return found


def own_kernel(blocks, kv_steps, *refs):
    codes = refs[:blocks]
    table, key_t, value_t = refs[blocks : blocks + 3]
    parts = refs[blocks + 3 : blocks + 3 + len(kv_steps)]
    w_query, gain, onehot, kv_t, own, square, kv_sum, q_sum, all_codes = refs[blocks + 3 + len(kv_steps) :]
    strand, mine, group = lax.axis_index("strand"), lax.axis_index("heads"), lax.axis_index("groups")
    size, groups = lax.axis_size("heads"), lax.axis_size("groups")
    key_cols, value_cols = key_t.shape[0], value_t.shape[0]
    entries, width = table.shape
    rows = codes[0].shape[0]
    for i in range(blocks):
        all_codes[i * rows : (i + 1) * rows, :] = codes[i][...]

    def kv_rows(owner):
        key_rows = pl.ds(pl.multiple_of(owner * key_cols, 16), key_cols)
        return key_rows, pl.ds(pl.multiple_of(KDIM + owner * value_cols, 16), value_cols)

    key_rows, value_rows = kv_rows(mine)
    kv_t[key_rows, :] = key_t[...]
    kv_t[value_rows, :] = value_t[...]
    for piece, (step, group_step, core_step) in zip(parts, kv_steps):
        key_rows, value_rows = kv_rows(lax.rem(mine + size - step, size))
        core = strand if core_step == 0 else 1 - strand
        part = core * groups + lax.rem(group + groups - group_step, groups)
        cols = pl.ds(pl.multiple_of(part * piece.shape[1], LANES), piece.shape[1])
        kv_t[key_rows, cols] = piece[:key_cols, :]
        kv_t[value_rows, cols] = piece[key_cols:, :]
    mark(onehot, all_codes, 0, entries, rows)
    weights = (kv_t, w_query, gain)
    span = (0, blocks * rows)
    own[...] = absorb(onehot, span, table, rows, mine * width, width, weights, None, (square, kv_sum, q_sum))


def chunk_start(step, index, chunks, width):
    size = lax.axis_size("heads")
    owner = lax.rem(lax.axis_index("heads") + size - step, size)
    return (owner * chunks + index) * width


def join_kernel(step, index, chunks, rows, late, *refs):
    mine, theirs, onehot_in, kv_t, w_query, gain, square_in, kv_in, q_in, own_table = refs[:10]
    codes = refs[10 : 10 + late]
    onehot, found, square, kv_sum, q_sum, table, all_codes = refs[10 + late :]
    half, width = mine.shape
    own_width = own_table.shape[1]
    early = onehot_in.shape[0]
    weights = (kv_t, w_query, gain)
    for i in range(late):
        all_codes[i * rows : (i + 1) * rows, :] = codes[i][...]
    mark(onehot, all_codes, early, own_table.shape[0], rows)
    onehot[:early, :] = onehot_in[...]
    square[:early, :] = square_in[...]
    kv_sum[:early, :] = kv_in[...]
    span = (early, late * rows)
    begin = lax.axis_index("heads") * own_width
    absorb(onehot, span, own_table, rows, begin, own_width, weights, None, (square, kv_sum, None))
    table[:half, :] = mine[...]
    table[half:, :] = theirs[...]
    begin = chunk_start(step, index, chunks, width)
    span = (0, early + late * rows)
    sums = (square, kv_sum, q_sum)
    found[...] = absorb(onehot, span, table, rows, begin, width, weights, (square, kv_sum, q_in), sums)


def chunk_kernel(step, index, chunks, rows, *refs):
    mine, theirs, onehot, kv_t, w_query, gain, square, kv_sum, q_sum = refs[:9]
    found, square_out, kv_out, q_out, table = refs[9:]
    half, width = mine.shape
    table[:half, :] = mine[...]
    table[half:, :] = theirs[...]
    found[...] = absorb(
        onehot,
        (0, onehot.shape[0]),
        table,
        rows,
        chunk_start(step, index, chunks, width),
        width,
        (kv_t, w_query, gain),
        (square, kv_sum, q_sum),
        (square_out, kv_out, q_out),
    )


def turn(values, cosine, sine):
    floats = values.astype(BF16).astype(F32)
    return (floats * cosine + pltpu.roll(floats, KDIM // 2, 1) * sine).astype(BF16)


def attend_kernel(steps, chunks, *refs):
    mine, theirs, onehot, kv_t, w_query, gain, square, kv_sum, q_sum = refs[:9]
    own, cosine, sine, first_out = refs[9:13]
    founds = refs[13 : 13 + len(steps) - 1]
    share, merged, inputs = refs[12 + len(steps) : 15 + len(steps)]
    table, squares, sums, queries, keys, values = refs[15 + len(steps) :]
    half, width = mine.shape
    rows, own_width = own.shape
    features = inputs.shape[1]
    total = onehot.shape[0]
    block = block_of(total, rows)
    table[:half, :] = mine[...]
    table[half:, :] = theirs[...]
    start = chunk_start(*steps[-1], chunks, width)
    span, weights = (0, total), (kv_t, w_query, gain)
    before, after = (square, kv_sum, q_sum), (squares, sums, queries)
    last = absorb(onehot, span, table, rows, start, width, weights, before, after)
    inputs[:, pl.ds(pl.multiple_of(start, LANES), width)] = last
    for found, spot in zip(founds, steps):
        inputs[:, pl.ds(pl.multiple_of(chunk_start(*spot, chunks, width), LANES), width)] = found[...]
    begin = pl.multiple_of(lax.axis_index("heads") * own_width, LANES)
    inputs[:, pl.ds(begin, own_width)] = own[...]

    def finish(begin):
        here = pl.ds(begin, block)
        scaled = sums[here, :] * lax.rsqrt(squares[here, :] / features + 1e-06)
        keys[here, :] = turn(scaled[:, :KDIM], cosine[here, :], sine[here, :])
        values[here, :] = scaled[:, KDIM:].astype(BF16)

    over_blocks(total, block, finish)
    scaled = queries[...] * lax.rsqrt(squares[:rows, :] / features + 1e-06)
    for head in range(queries.shape[1] // KDIM):
        query = turn(scaled[:, head * KDIM : (head + 1) * KDIM], cosine[:rows, :], sine[:rows, :])
        scores = matmul_t(query, keys[...]) * KDIM ** (-0.5)
        weights = jnp.exp(scores - jnp.max(scores, axis=1, keepdims=True))
        weight_sum = jnp.sum(weights, axis=1, keepdims=True)
        found = (matmul(weights.astype(BF16), values[...]) / weight_sum).astype(BF16)
        merged[:, head * VDIM : (head + 1) * VDIM] = found
    share[...] = matmul(merged[...], first_out[...]).astype(BF16)


def second_kernel(merged, second_out, share):
    share[...] = matmul(merged[...], second_out[...]).astype(BF16)


def gather_hidden(shares, inputs, gain, chunk):
    width = shares[0].shape[1]
    cols = slice(chunk * width, (chunk + 1) * width)
    total = shares[0][...].astype(F32)
    for other in shares[1:]:
        total = total + other[...].astype(F32)
    hidden = (inputs[:, cols].astype(F32) + total).astype(BF16).astype(F32)
    return jnp.sum(hidden * hidden, axis=1, keepdims=True), (hidden * gain[:, cols]).astype(BF16)


def soft(logits):
    return jnp.maximum(logits, 0.0) + jnp.log1p(jnp.exp(-jnp.abs(logits)))


def first_tracks_kernel(size, *refs):
    shares = refs[:size]
    inputs, gain, tracks, square, to_send, to_keep = refs[size:]
    strand = lax.axis_index("strand")
    width = shares[0].shape[1]
    square[...], gained = gather_hidden(shares, inputs, gain, 0)
    to_send[...] = matmul(gained, tracks[1 - strand, :width, :])
    to_keep[...] = matmul(gained, tracks[strand, :width, :])


def send_kernel(size, *refs):
    shares = refs[:size]
    inputs, gain, tracks, square, to_send, sent, gained_out, scale_out = refs[size:]
    strand = lax.axis_index("strand")
    width = shares[0].shape[1]
    total, gained = gather_hidden(shares, inputs, gain, 1)
    scale = lax.rsqrt((square[...] + total) / (2 * width) + 1e-06)
    logits = to_send[...] + matmul(gained, tracks[1 - strand, width:, :])
    sent[...] = soft(logits * scale).astype(BF16)
    gained_out[...] = gained
    scale_out[...] = scale


def keep_kernel(gained, tracks, to_keep, scale, kept):
    strand = lax.axis_index("strand")
    width = gained.shape[1]
    logits = to_keep[...] + matmul(gained[...], tracks[strand, width:, :])
    kept[...] = soft(logits * scale[...]).astype(BF16)


def average_kernel(kept, received, pairs, out):
    strand = lax.axis_index("strand")
    count = kept.shape[1]
    mine, theirs = kept[...].astype(F32), received[...].astype(F32)
    forward = jnp.where(strand == 0, mine, theirs)
    reverse = jnp.where(strand == 0, theirs, mine)
    index = lax.broadcasted_iota(jnp.int32, (1, count), 1)
    even = index % 2 == 0
    swapped = (pairs[...] % 2 == 0) != even
    partner = jnp.where(even, pltpu.roll(reverse, count - 1, 1), pltpu.roll(reverse, 1, 1))
    out[...] = 0.5 * (forward + jnp.where(swapped, partner, reverse))


def body(
    base_codes,
    embed_table,
    attn_gain,
    w_query,
    w_key,
    w_value,
    w_out,
    head_gain,
    w_tracks,
    track_pairs,
):
    rows = base_codes.shape[0] // BIN
    blocks = lax.axis_size("pos")
    size = lax.axis_size("heads")
    features, q_cols = w_query.shape
    entries, width = embed_table.shape
    groups = lax.axis_size("groups")
    key_t, value_t = w_key.T, w_value.T
    kv_cols = key_t.shape[0] + value_t.shape[0]
    kv_all = KDIM + VDIM
    half = entries // 2
    total = blocks * rows
    tracks_half = w_tracks.shape[2]
    chunks = 2 if width % (2 * LANES) == 0 else 1
    wide = width // chunks

    early, late = [(0, 0)], []
    for k in range(1, blocks, 2):
        early.append((k, min(k + 1, blocks - 1)))
        if k + 1 < blocks:
            late.append((k + 1, k))

    hbm = pltpu.HBM
    part_kv, *own_pieces, own_codes = call(
        functools.partial(stage_kernel, chunks),
        [shape((kv_cols, features // (2 * groups)), BF16)]
        + [shape((half, wide), BF16)] * chunks
        + [shape((rows, BIN), BF16)],
        [embed_table, key_t, value_t, base_codes.reshape(rows, BIN)],
        "stage",
        scratch=[pltpu.VMEM((rows, BIN), jnp.int32), pltpu.SemaphoreType.DMA((3 + chunks,))],
        spaces=[hbm] * 4,
    )
    table, key_own, value_own, query_own, gain, last_gain, cosine, sine = call(
        functools.partial(prepare_kernel, rows, early + late),
        [
            shape((entries, width), BF16),
            shape(key_t.shape, BF16),
            shape(value_t.shape, BF16),
            shape(w_query.shape, BF16),
            shape((1, features), F32),
            shape((1, features), F32),
            shape((total, KDIM), F32),
            shape((total, KDIM), F32),
        ],
        [embed_table, key_t, value_t, w_query, attn_gain, head_gain],
        "prepare",
        scratch=[
            pltpu.VMEM((features,), F32),
            pltpu.VMEM((features,), F32),
            pltpu.SemaphoreType.DMA((7,)),
        ],
        spaces=[hbm] * 6,
    )
    kv_parts, kv_steps, pieces, steps = [], [], [], []
    from_heads = [shifted(part_kv, "heads", step) for step in range(1, size)]
    if from_heads:
        from_heads[0], table = lax.optimization_barrier((from_heads[0], table))
    to_core = [shifted(here, "strand", 1) for here in from_heads]
    out_in = w_out
    if to_core:
        out_in = w_out
    first_out, second_out = call(
        fetch_kernel,
        [shape((w_out.shape[0], features // 2), BF16)] * 2,
        [out_in],
        "fetch_out",
        scratch=[pltpu.SemaphoreType.DMA((2,))],
        spaces=[hbm],
    )
    raw = []
    for k, other in early[1:]:
        if k != other:
            pairs = [((p, s), ((p + k + s) % blocks, s)) for p in range(blocks) for s in range(2)]
            pairs = [(2 * p + s, 2 * q + t) for (p, s), (q, t) in pairs]
            raw.append(lax.ppermute(own_codes, ("pos", "strand"), pairs))
        else:
            if to_core:
                own_codes, to_core[0] = lax.optimization_barrier((own_codes, to_core[0]))
            raw.append(shifted(own_codes, "pos", k))
    if raw:
        raw[0], first_out = lax.optimization_barrier((raw[0], first_out))
    for step in range(1, size):
        for k in range(groups):
            here = from_heads[step - 1] if k == 0 else shifted(from_heads[step - 1], "groups", k)
            kv_parts += [here, to_core[step - 1] if k == 0 else shifted(here, "strand", 1)]
            kv_steps += [(step, k, 0), (step, k, 1)]
    for step in range(1, size):
        for i in range(chunks):
            here = shifted(own_pieces[i], "heads", step)
            if step == 1 and i == chunks - 1 and raw:
                here, *raw = lax.optimization_barrier((here, *raw))
            pieces.append((here, shifted(here, "strand", 1)))
            steps.append((step, i))

    swapped = [shifted(raw[i], "strand", 1) for i in range(len(late))]
    codes = [own_codes] + raw
    if len(steps) < 2:
        codes, swapped = codes + swapped, []

    def sums_of(count):
        return [shape((count, 1), F32), shape((count, kv_all), F32), shape((rows, q_cols), F32)]

    count = rows * len(codes)
    onehot, kv_t, own, *state = call(
        functools.partial(own_kernel, len(codes), kv_steps),
        [shape((count, entries), BF16), shape((kv_all, features), BF16), shape((rows, width), BF16)]
        + sums_of(count),
        codes + [table, key_own, value_own] + kv_parts + [query_own, gain],
        "own_features",
        scratch=[pltpu.VMEM((count, BIN), BF16)],
        flops=2 * count * width * (entries + kv_all),
        spare=8 * total * entries,
    )
    founds = []
    for (step, i), pair in zip(steps[:-1], pieces[:-1]):
        operands = list(pair) + [onehot, kv_t, query_own, gain] + state
        outs = [shape((rows, wide), BF16)] + sums_of(total)
        scratch = [pltpu.VMEM((entries, wide), BF16)]
        if swapped:
            kernel = functools.partial(join_kernel, step, i, chunks, rows, len(swapped))
            operands += [table] + swapped
            outs = [shape((total, entries), BF16)] + outs
            scratch.append(pltpu.VMEM((rows * len(swapped), BIN), BF16))
        else:
            kernel = functools.partial(chunk_kernel, step, i, chunks, rows)
        results = call(
            kernel,
            outs,
            operands,
            "other_features",
            scratch=scratch,
            flops=2 * total * wide * (entries + kv_all),
            spare=8 * total * entries,
        )
        if swapped:
            onehot, *results = results
            swapped = []
        found, *state = results
        founds.append(found)
    o_cols = q_cols // KDIM * VDIM
    share_one, merged, inputs = call(
        functools.partial(attend_kernel, steps, chunks),
        [
            shape((rows, features // 2), BF16),
            shape((rows, o_cols), BF16),
            shape((rows, features), BF16),
        ],
        list(pieces[-1]) + [onehot, kv_t, query_own, gain] + state + [own, cosine, sine, first_out] + founds,
        "attend",
        scratch=[
            pltpu.VMEM((entries, wide), BF16),
            pltpu.VMEM((total, 1), F32),
            pltpu.VMEM((total, kv_all), F32),
            pltpu.VMEM((rows, q_cols), F32),
            pltpu.VMEM((total, KDIM), BF16),
            pltpu.VMEM((total, VDIM), BF16),
        ],
        flops=2 * total * wide * (entries + kv_all) + 2 * total * q_cols * rows * 3,
        spare=8 * total * entries,
    )
    (share_two,) = call(
        second_kernel,
        [shape((rows, features // 2), BF16)],
        [merged, second_out],
        "second_share",
        flops=rows * o_cols * features,
    )
    ones = [share_one] + [shifted(share_one, "heads", k) for k in range(1, size)]
    twos = [share_two] + [shifted(share_two, "heads", k) for k in range(1, size)]
    weights, _ = lax.optimization_barrier((w_tracks, share_two))
    tracks = lax.optimization_barrier(weights.transpose(1, 0, 2))
    square, to_send, to_keep = call(
        functools.partial(first_tracks_kernel, size),
        [
            shape((rows, 1), F32),
            shape((rows, tracks_half), F32),
            shape((rows, tracks_half), F32),
        ],
        ones + [inputs, last_gain, tracks],
        "first_tracks",
        flops=2 * rows * features * tracks_half,
    )
    sent, gained, scale = call(
        functools.partial(send_kernel, size),
        [
            shape((rows, tracks_half), BF16),
            shape((rows, features // 2), BF16),
            shape((rows, 1), F32),
        ],
        twos + [inputs, last_gain, tracks, square, to_send],
        "sent_tracks",
        flops=rows * features * tracks_half,
    )
    received = shifted(sent, "strand", 1)
    (kept,) = call(
        keep_kernel,
        [shape((rows, tracks_half), BF16)],
        [gained, tracks, to_keep, scale],
        "kept_tracks",
        flops=rows * features * tracks_half,
    )
    (out,) = call(
        average_kernel,
        [shape((rows, tracks_half), F32)],
        [kept, received, track_pairs.reshape(1, tracks_half)],
        "average",
    )
    return out


def solution(mesh):
    placed = (
        P(("groups", "pos")),
        P(None, "heads"),
        P(),
        P(None, "heads"),
        P(None, "heads"),
        P(None, "heads"),
        P("heads", None),
        P(),
        P(None, None, "heads"),
        P(("strand", "heads")),
    )
    return jax.shard_map(
        body,
        mesh=mesh,
        in_specs=placed,
        out_specs=P(("groups", "pos"), ("strand", "heads")),
        check_vma=False,
    )
```

```python
import functools
import math

import jax
import jax.experimental.pallas as pl
import jax.experimental.pallas.tpu as pltpu
import jax.numpy as jnp
from jax import lax
from jax.sharding import PartitionSpec as P

KDIM = 128
VDIM = 192
BIN = 128
BASES = 4
LANES = 128
VMEM_LIMIT = 48 * 2**20
F32 = jnp.float32
BF16 = jnp.bfloat16


def shifted(value, axis, distance):
    size = lax.axis_size(axis)
    return lax.ppermute(value, axis, [(i, (i + distance) % size) for i in range(size)])


def matmul(a, b):
    return jnp.dot(a, b, preferred_element_type=F32)


def matmul_t(a, b):
    return lax.dot_general(a, b, (((1,), (1,)), ((), ())), preferred_element_type=F32)


def call(kernel, outs, operands, name, scratch=(), spaces=None, flops=0, spare=0, out_space=None):
    vmem = pl.BlockSpec(memory_space=pltpu.VMEM)
    spaces = spaces or [None] * len(operands)
    operands = [
        v if s is None else pltpu.with_memory_space_constraint(v, s) for v, s in zip(operands, spaces)
    ]
    specs = [vmem if s is None else pl.BlockSpec(memory_space=s) for s in spaces]
    held = [v for v, s in zip(operands, spaces) if s is None] + list(outs)
    held += [v for v in scratch if hasattr(v, "shape") and hasattr(v, "dtype") and v.memory_space == pltpu.VMEM]
    moved = sum(math.prod(v.shape[:-1]) * max(v.shape[-1], LANES) * jnp.dtype(v.dtype).itemsize for v in held)
    return pl.pallas_call(
        kernel,
        out_shape=list(outs),
        in_specs=specs,
        out_specs=[pl.BlockSpec(memory_space=out_space or pltpu.VMEM)] * len(outs),
        scratch_shapes=list(scratch),
        compiler_params=pltpu.CompilerParams(
            vmem_limit_bytes=min(VMEM_LIMIT, moved + moved // 4 + 6 * 2**20 + spare)
        ),
        cost_estimate=pl.CostEstimate(flops=flops, bytes_accessed=moved, transcendentals=0),
        name=name,
    )(*operands)


def shape(dims, dtype):
    return jax.ShapeDtypeStruct(tuple(dims), dtype)


def over_blocks(total, block, step):
    if total == block:
        step(0)
    else:

        def one(i, carry):
            step(pl.multiple_of(i * block, block))
            return carry

        lax.fori_loop(0, total // block, one, 0)


def stage_kernel(chunks, embed, key_t, value_t, codes, *refs):
    part_kv, pieces = refs[0], refs[1 : 1 + chunks]
    codes_out, raw_codes, sems = refs[1 + chunks :]
    strand = lax.axis_index("strand")
    part = strand * lax.axis_size("groups") + lax.axis_index("groups")
    key_cols, value_cols = key_t.shape[0], value_t.shape[0]
    kv_width = part_kv.shape[1]
    half, width = pieces[0].shape
    cols = pl.ds(pl.multiple_of(part * kv_width, LANES), kv_width)
    rows = pl.ds(pl.multiple_of(strand * half, half), half)
    copies = [
        pltpu.make_async_copy(key_t.at[:, cols], part_kv.at[pl.ds(0, key_cols)], sems.at[0]),
        pltpu.make_async_copy(value_t.at[:, cols], part_kv.at[pl.ds(key_cols, value_cols)], sems.at[1]),
    ]
    for i in range(chunks):
        source = embed.at[rows, pl.ds(i * width, width)]
        copies.append(pltpu.make_async_copy(source, pieces[i], sems.at[2 + i]))
    copies.append(pltpu.make_async_copy(codes, raw_codes, sems.at[2 + chunks]))
    for copy in copies:
        copy.start()
    copies[-1].wait()
    codes_out[...] = raw_codes[...].astype(F32).astype(BF16)
    for copy in copies[:-1]:
        copy.wait()


def prepare_kernel(rows, slots, embed, key_t, value_t, w_query, gain, last_gain, *refs):
    table, key_out, value_out, query_out, gain_out, last_out, cosine, sine = refs[:8]
    raw_gain, raw_last, sems = refs[8:]
    strand, pos = lax.axis_index("strand"), lax.axis_index("pos")
    half = embed.shape[0] // 2
    pairs = [(gain, raw_gain), (last_gain, raw_last)]
    for i in range(2):
        part = strand if i == 0 else 1 - strand
        source = embed.at[pl.ds(pl.multiple_of(part * half, half), half)]
        pairs.append((source, table.at[pl.ds(i * half, half)]))
    pairs += [(key_t, key_out), (value_t, value_out), (w_query, query_out)]
    copies = [pltpu.make_async_copy(a, b, sems.at[i]) for i, (a, b) in enumerate(pairs)]
    for copy in copies:
        copy.start()
    total = cosine.shape[0]
    blocks = total // rows
    lane = lax.broadcasted_iota(jnp.int32, (1, KDIM), 1)
    inverse = jnp.exp((lane % (KDIM // 2)).astype(F32) * (-math.log(10000.0) / (KDIM // 2)))
    sign = jnp.where(lane < KDIM // 2, -1.0, 1.0)
    offset = lax.broadcasted_iota(jnp.int32, (rows, KDIM), 0)
    for copy in copies[:2]:
        copy.wait()
    gain_out[...] = raw_gain[...].reshape(gain_out.shape)
    last_out[...] = raw_last[...].reshape(last_out.shape)

    for i, (forward, reverse) in enumerate(slots):
        behind = jnp.where(strand == 0, forward, reverse)
        place = lax.rem(pos + blocks - behind, blocks) * rows + offset
        angle = jnp.where(strand == 0, place, total - 1 - place).astype(F32) * inverse
        cosine[i * rows : (i + 1) * rows, :] = jnp.cos(angle)
        sine[i * rows : (i + 1) * rows, :] = jnp.sin(angle) * sign
    for copy in copies[2:]:
        copy.wait()


def fetch_kernel(w_out, first_out, second_out, sems):
    out_half = first_out.shape[1]
    copies = [
        pltpu.make_async_copy(w_out.at[:, pl.ds(0, out_half)], first_out, sems.at[0]),
        pltpu.make_async_copy(w_out.at[:, pl.ds(out_half, out_half)], second_out, sems.at[1]),
    ]
    for copy in copies:
        copy.start()
    for copy in copies:
        copy.wait()


def block_of(count, rows):
    if count <= 4 * rows:
        return count
    return 4 * rows if count % (4 * rows) == 0 else rows


def mark(onehot, codes, first, entries, rows):
    strand = lax.axis_index("strand")
    half = entries // 2
    count = codes.shape[0]
    spot = lax.broadcasted_iota(jnp.int32, (BIN, entries), 1)
    owner = jnp.where(spot < half, strand, 1 - strand)
    entry = owner * half + spot % half
    entry = jnp.where(strand == 0, entry, entries - 1 - entry)
    place = lax.broadcasted_iota(jnp.int32, (BIN, entries), 0)
    spread = jnp.where(place == entry // BASES, 1.0, 0.0).astype(BF16)
    wanted = (entry[:1] % BASES).astype(F32)
    block = block_of(count, rows)

    def step(begin):
        found = matmul(codes[pl.ds(begin, block), :], spread) == wanted
        onehot[pl.ds(first + begin, block), :] = jnp.where(found, 1.0, 0.0).astype(BF16)

    over_blocks(count, block, step)


def absorb(onehot, span, table, rows, start, width, weights, before, after):
    kv_t, w_query, gain = weights
    first, count = span
    block = block_of(count, rows)
    cols = pl.ds(pl.multiple_of(start, LANES), width)

    def some(here):
        found = matmul(onehot[here, :], table[...]).astype(BF16)
        floats = found.astype(F32)
        return found, floats, (floats * gain[:, cols]).astype(BF16)

    def step(begin):
        here = pl.ds(first + begin, block)
        found, floats, gained = some(here)
        square = jnp.sum(floats * floats, axis=1, keepdims=True)
        kv = matmul_t(gained, kv_t[:, cols])
        after[0][here, :] = square if before is None else before[0][here, :] + square
        after[1][here, :] = kv if before is None else before[1][here, :] + kv
        return found, gained

    if count == block:
        found, gained = step(0)
        found, gained = found[:rows], gained[:rows]
    else:
        over_blocks(count, block, lambda begin: step(begin) and None)
        found, _, gained = some(pl.ds(0, rows))
    if first:
        return None
    query = matmul(gained, w_query[cols, :])
    after[2][...] = query if before is None else before[2][...] + query
    return found


def own_kernel(blocks, kv_steps, *refs):
    codes = refs[:blocks]
    table, key_t, value_t = refs[blocks : blocks + 3]
    parts = refs[blocks + 3 : blocks + 3 + len(kv_steps)]
    w_query, gain, onehot, kv_t, own, square, kv_sum, q_sum, all_codes = refs[blocks + 3 + len(kv_steps) :]
    strand, mine, group = lax.axis_index("strand"), lax.axis_index("heads"), lax.axis_index("groups")
    size, groups = lax.axis_size("heads"), lax.axis_size("groups")
    key_cols, value_cols = key_t.shape[0], value_t.shape[0]
    entries, width = table.shape
    rows = codes[0].shape[0]
    for i in range(blocks):
        all_codes[i * rows : (i + 1) * rows, :] = codes[i][...]

    def kv_rows(owner):
        key_rows = pl.ds(pl.multiple_of(owner * key_cols, 16), key_cols)
        return key_rows, pl.ds(pl.multiple_of(KDIM + owner * value_cols, 16), value_cols)

    key_rows, value_rows = kv_rows(mine)
    kv_t[key_rows, :] = key_t[...]
    kv_t[value_rows, :] = value_t[...]
    for piece, (step, group_step, core_step) in zip(parts, kv_steps):
        key_rows, value_rows = kv_rows(lax.rem(mine + size - step, size))
        core = strand if core_step == 0 else 1 - strand
        part = core * groups + lax.rem(group + groups - group_step, groups)
        cols = pl.ds(pl.multiple_of(part * piece.shape[1], LANES), piece.shape[1])
        kv_t[key_rows, cols] = piece[:key_cols, :]
        kv_t[value_rows, cols] = piece[key_cols:, :]
    mark(onehot, all_codes, 0, entries, rows)
    weights = (kv_t, w_query, gain)
    span = (0, blocks * rows)
    own[...] = absorb(onehot, span, table, rows, mine * width, width, weights, None, (square, kv_sum, q_sum))


def chunk_start(step, index, chunks, width):
    size = lax.axis_size("heads")
    owner = lax.rem(lax.axis_index("heads") + size - step, size)
    return (owner * chunks + index) * width


def join_kernel(step, index, chunks, rows, late, *refs):
    mine, theirs, onehot_in, kv_t, w_query, gain, square_in, kv_in, q_in, own_table = refs[:10]
    codes = refs[10 : 10 + late]
    onehot, found, square, kv_sum, q_sum, table, all_codes = refs[10 + late :]
    half, width = mine.shape
    own_width = own_table.shape[1]
    early = onehot_in.shape[0]
    weights = (kv_t, w_query, gain)
    for i in range(late):
        all_codes[i * rows : (i + 1) * rows, :] = codes[i][...]
    mark(onehot, all_codes, early, own_table.shape[0], rows)
    onehot[:early, :] = onehot_in[...]
    square[:early, :] = square_in[...]
    kv_sum[:early, :] = kv_in[...]
    span = (early, late * rows)
    begin = lax.axis_index("heads") * own_width
    absorb(onehot, span, own_table, rows, begin, own_width, weights, None, (square, kv_sum, None))
    table[:half, :] = mine[...]
    table[half:, :] = theirs[...]
    begin = chunk_start(step, index, chunks, width)
    span = (0, early + late * rows)
    sums = (square, kv_sum, q_sum)
    found[...] = absorb(onehot, span, table, rows, begin, width, weights, (square, kv_sum, q_in), sums)


def chunk_kernel(step, index, chunks, rows, *refs):
    mine, theirs, onehot, kv_t, w_query, gain, square, kv_sum, q_sum = refs[:9]
    found, square_out, kv_out, q_out, table = refs[9:]
    half, width = mine.shape
    table[:half, :] = mine[...]
    table[half:, :] = theirs[...]
    found[...] = absorb(
        onehot,
        (0, onehot.shape[0]),
        table,
        rows,
        chunk_start(step, index, chunks, width),
        width,
        (kv_t, w_query, gain),
        (square, kv_sum, q_sum),
        (square_out, kv_out, q_out),
    )


def turn(values, cosine, sine):
    floats = values.astype(BF16).astype(F32)
    return (floats * cosine + pltpu.roll(floats, KDIM // 2, 1) * sine).astype(BF16)


def attend_kernel(steps, chunks, *refs):
    mine, theirs, onehot, kv_t, w_query, gain, square, kv_sum, q_sum = refs[:9]
    own, cosine, sine, first_out = refs[9:13]
    founds = refs[13 : 13 + len(steps) - 1]
    share, merged, inputs = refs[12 + len(steps) : 15 + len(steps)]
    table, squares, sums, queries, keys, values = refs[15 + len(steps) :]
    half, width = mine.shape
    rows, own_width = own.shape
    features = inputs.shape[1]
    total = onehot.shape[0]
    block = block_of(total, rows)
    table[:half, :] = mine[...]
    table[half:, :] = theirs[...]
    start = chunk_start(*steps[-1], chunks, width)
    span, weights = (0, total), (kv_t, w_query, gain)
    before, after = (square, kv_sum, q_sum), (squares, sums, queries)
    last = absorb(onehot, span, table, rows, start, width, weights, before, after)
    inputs[:, pl.ds(pl.multiple_of(start, LANES), width)] = last
    for found, spot in zip(founds, steps):
        inputs[:, pl.ds(pl.multiple_of(chunk_start(*spot, chunks, width), LANES), width)] = found[...]
    begin = pl.multiple_of(lax.axis_index("heads") * own_width, LANES)
    inputs[:, pl.ds(begin, own_width)] = own[...]

    def finish(begin):
        here = pl.ds(begin, block)
        scaled = sums[here, :] * lax.rsqrt(squares[here, :] / features + 1e-06)
        keys[here, :] = turn(scaled[:, :KDIM], cosine[here, :], sine[here, :])
        values[here, :] = scaled[:, KDIM:].astype(BF16)

    over_blocks(total, block, finish)
    scaled = queries[...] * lax.rsqrt(squares[:rows, :] / features + 1e-06)
    for head in range(queries.shape[1] // KDIM):
        query = turn(scaled[:, head * KDIM : (head + 1) * KDIM], cosine[:rows, :], sine[:rows, :])
        scores = matmul_t(query, keys[...]) * KDIM ** (-0.5)
        weights = jnp.exp(scores - jnp.max(scores, axis=1, keepdims=True))
        weight_sum = jnp.sum(weights, axis=1, keepdims=True)
        found = (matmul(weights.astype(BF16), values[...]) / weight_sum).astype(BF16)
        merged[:, head * VDIM : (head + 1) * VDIM] = found
    share[...] = matmul(merged[...], first_out[...]).astype(BF16)


def second_kernel(merged, second_out, share):
    share[...] = matmul(merged[...], second_out[...]).astype(BF16)


def gather_hidden(shares, inputs, gain, chunk):
    width = shares[0].shape[1]
    cols = slice(chunk * width, (chunk + 1) * width)
    total = shares[0][...].astype(F32)
    for other in shares[1:]:
        total = total + other[...].astype(F32)
    hidden = (inputs[:, cols].astype(F32) + total).astype(BF16).astype(F32)
    return jnp.sum(hidden * hidden, axis=1, keepdims=True), (hidden * gain[:, cols]).astype(BF16)


def soft(logits):
    return jnp.maximum(logits, 0.0) + jnp.log1p(jnp.exp(-jnp.abs(logits)))


def first_tracks_kernel(size, *refs):
    shares = refs[:size]
    inputs, gain, tracks, square, to_send, to_keep = refs[size:]
    strand = lax.axis_index("strand")
    width = shares[0].shape[1]
    square[...], gained = gather_hidden(shares, inputs, gain, 0)
    to_send[...] = matmul(gained, tracks[1 - strand, :width, :])
    to_keep[...] = matmul(gained, tracks[strand, :width, :])


def send_kernel(size, *refs):
    shares = refs[:size]
    inputs, gain, tracks, square, to_send, sent, gained_out, scale_out = refs[size:]
    strand = lax.axis_index("strand")
    width = shares[0].shape[1]
    total, gained = gather_hidden(shares, inputs, gain, 1)
    scale = lax.rsqrt((square[...] + total) / (2 * width) + 1e-06)
    logits = to_send[...] + matmul(gained, tracks[1 - strand, width:, :])
    sent[...] = soft(logits * scale).astype(BF16)
    gained_out[...] = gained
    scale_out[...] = scale


def keep_kernel(gained, tracks, to_keep, scale, kept):
    strand = lax.axis_index("strand")
    width = gained.shape[1]
    logits = to_keep[...] + matmul(gained[...], tracks[strand, width:, :])
    kept[...] = soft(logits * scale[...]).astype(BF16)


def average_kernel(parts, kept, received, pairs, out, stage, sems):
    strand = lax.axis_index("strand")
    count = kept.shape[1]
    rows = kept.shape[0] // parts
    index = lax.broadcasted_iota(jnp.int32, (1, count), 1)
    even = index % 2 == 0
    swapped = (pairs[...] % 2 == 0) != even
    copies = []
    for i in range(parts):
        here = slice(i * rows, (i + 1) * rows)
        mine, theirs = kept[here, :].astype(F32), received[here, :].astype(F32)
        forward = jnp.where(strand == 0, mine, theirs)
        reverse = jnp.where(strand == 0, theirs, mine)
        partner = jnp.where(even, pltpu.roll(reverse, count - 1, 1), pltpu.roll(reverse, 1, 1))
        stage[here, :] = 0.5 * (forward + jnp.where(swapped, partner, reverse))
        copies.append(pltpu.make_async_copy(stage.at[here], out.at[here], sems.at[i]))
        copies[-1].start()
    for copy in copies:
        copy.wait()


def body(
    base_codes,
    embed_table,
    attn_gain,
    w_query,
    w_key,
    w_value,
    w_out,
    head_gain,
    w_tracks,
    track_pairs,
):
    rows = base_codes.shape[0] // BIN
    blocks = lax.axis_size("pos")
    size = lax.axis_size("heads")
    features, q_cols = w_query.shape
    entries, width = embed_table.shape
    groups = lax.axis_size("groups")
    key_t, value_t = w_key.T, w_value.T
    kv_cols = key_t.shape[0] + value_t.shape[0]
    kv_all = KDIM + VDIM
    half = entries // 2
    total = blocks * rows
    tracks_half = w_tracks.shape[2]
    chunks = 2 if width % (2 * LANES) == 0 else 1
    wide = width // chunks

    early, late = [(0, 0)], []
    for k in range(1, blocks, 2):
        early.append((k, min(k + 1, blocks - 1)))
        if k + 1 < blocks:
            late.append((k + 1, k))

    hbm = pltpu.HBM
    part_kv, *own_pieces, own_codes = call(
        functools.partial(stage_kernel, chunks),
        [shape((kv_cols, features // (2 * groups)), BF16)]
        + [shape((half, wide), BF16)] * chunks
        + [shape((rows, BIN), BF16)],
        [embed_table, key_t, value_t, base_codes.reshape(rows, BIN)],
        "stage",
        scratch=[pltpu.VMEM((rows, BIN), jnp.int32), pltpu.SemaphoreType.DMA((3 + chunks,))],
        spaces=[hbm] * 4,
    )
    table, key_own, value_own, query_own, gain, last_gain, cosine, sine = call(
        functools.partial(prepare_kernel, rows, early + late),
        [
            shape((entries, width), BF16),
            shape(key_t.shape, BF16),
            shape(value_t.shape, BF16),
            shape(w_query.shape, BF16),
            shape((1, features), F32),
            shape((1, features), F32),
            shape((total, KDIM), F32),
            shape((total, KDIM), F32),
        ],
        [embed_table, key_t, value_t, w_query, attn_gain, head_gain],
        "prepare",
        scratch=[
            pltpu.VMEM((features,), F32),
            pltpu.VMEM((features,), F32),
            pltpu.SemaphoreType.DMA((7,)),
        ],
        spaces=[hbm] * 6,
    )
    kv_parts, kv_steps, pieces, steps = [], [], [], []
    from_heads = [shifted(part_kv, "heads", step) for step in range(1, size)]
    if from_heads:
        from_heads[0], table = lax.optimization_barrier((from_heads[0], table))
    to_core = [shifted(here, "strand", 1) for here in from_heads]
    out_in = w_out
    if to_core:
        out_in = w_out
    first_out, second_out = call(
        fetch_kernel,
        [shape((w_out.shape[0], features // 2), BF16)] * 2,
        [out_in],
        "fetch_out",
        scratch=[pltpu.SemaphoreType.DMA((2,))],
        spaces=[hbm],
    )
    raw = []
    for k, other in early[1:]:
        if k != other:
            pairs = [((p, s), ((p + k + s) % blocks, s)) for p in range(blocks) for s in range(2)]
            pairs = [(2 * p + s, 2 * q + t) for (p, s), (q, t) in pairs]
            raw.append(lax.ppermute(own_codes, ("pos", "strand"), pairs))
        else:
            if to_core:
                own_codes, to_core[0] = lax.optimization_barrier((own_codes, to_core[0]))
            raw.append(shifted(own_codes, "pos", k))
    if raw:
        raw[0], first_out = lax.optimization_barrier((raw[0], first_out))
    for step in range(1, size):
        for k in range(groups):
            here = from_heads[step - 1] if k == 0 else shifted(from_heads[step - 1], "groups", k)
            kv_parts += [here, to_core[step - 1] if k == 0 else shifted(here, "strand", 1)]
            kv_steps += [(step, k, 0), (step, k, 1)]
    for step in range(1, size):
        for i in range(chunks):
            here = shifted(own_pieces[i], "heads", step)
            if step == 1 and i == chunks - 1 and raw:
                here, *raw = lax.optimization_barrier((here, *raw))
            pieces.append((here, shifted(here, "strand", 1)))
            steps.append((step, i))

    swapped = [shifted(raw[i], "strand", 1) for i in range(len(late))]
    codes = [own_codes] + raw
    if len(steps) < 2:
        codes, swapped = codes + swapped, []

    def sums_of(count):
        return [shape((count, 1), F32), shape((count, kv_all), F32), shape((rows, q_cols), F32)]

    count = rows * len(codes)
    onehot, kv_t, own, *state = call(
        functools.partial(own_kernel, len(codes), kv_steps),
        [shape((count, entries), BF16), shape((kv_all, features), BF16), shape((rows, width), BF16)]
        + sums_of(count),
        codes + [table, key_own, value_own] + kv_parts + [query_own, gain],
        "own_features",
        scratch=[pltpu.VMEM((count, BIN), BF16)],
        flops=2 * count * width * (entries + kv_all),
        spare=8 * total * entries,
    )
    founds = []
    for (step, i), pair in zip(steps[:-1], pieces[:-1]):
        operands = list(pair) + [onehot, kv_t, query_own, gain] + state
        outs = [shape((rows, wide), BF16)] + sums_of(total)
        scratch = [pltpu.VMEM((entries, wide), BF16)]
        if swapped:
            kernel = functools.partial(join_kernel, step, i, chunks, rows, len(swapped))
            operands += [table] + swapped
            outs = [shape((total, entries), BF16)] + outs
            scratch.append(pltpu.VMEM((rows * len(swapped), BIN), BF16))
        else:
            kernel = functools.partial(chunk_kernel, step, i, chunks, rows)
        results = call(
            kernel,
            outs,
            operands,
            "other_features",
            scratch=scratch,
            flops=2 * total * wide * (entries + kv_all),
            spare=8 * total * entries,
        )
        if swapped:
            onehot, *results = results
            swapped = []
        found, *state = results
        founds.append(found)
    o_cols = q_cols // KDIM * VDIM
    share_one, merged, inputs = call(
        functools.partial(attend_kernel, steps, chunks),
        [
            shape((rows, features // 2), BF16),
            shape((rows, o_cols), BF16),
            shape((rows, features), BF16),
        ],
        list(pieces[-1]) + [onehot, kv_t, query_own, gain] + state + [own, cosine, sine, first_out] + founds,
        "attend",
        scratch=[
            pltpu.VMEM((entries, wide), BF16),
            pltpu.VMEM((total, 1), F32),
            pltpu.VMEM((total, kv_all), F32),
            pltpu.VMEM((rows, q_cols), F32),
            pltpu.VMEM((total, KDIM), BF16),
            pltpu.VMEM((total, VDIM), BF16),
        ],
        flops=2 * total * wide * (entries + kv_all) + 2 * total * q_cols * rows * 3,
        spare=8 * total * entries,
    )
    (share_two,) = call(
        second_kernel,
        [shape((rows, features // 2), BF16)],
        [merged, second_out],
        "second_share",
        flops=rows * o_cols * features,
    )
    ones = [share_one] + [shifted(share_one, "heads", k) for k in range(1, size)]
    twos = [share_two] + [shifted(share_two, "heads", k) for k in range(1, size)]
    weights, _ = lax.optimization_barrier((w_tracks, share_two))
    tracks = lax.optimization_barrier(weights.transpose(1, 0, 2))
    square, to_send, to_keep = call(
        functools.partial(first_tracks_kernel, size),
        [
            shape((rows, 1), F32),
            shape((rows, tracks_half), F32),
            shape((rows, tracks_half), F32),
        ],
        ones + [inputs, last_gain, tracks],
        "first_tracks",
        flops=2 * rows * features * tracks_half,
    )
    sent, gained, scale = call(
        functools.partial(send_kernel, size),
        [
            shape((rows, tracks_half), BF16),
            shape((rows, features // 2), BF16),
            shape((rows, 1), F32),
        ],
        twos + [inputs, last_gain, tracks, square, to_send],
        "sent_tracks",
        flops=rows * features * tracks_half,
    )
    received = shifted(sent, "strand", 1)
    (kept,) = call(
        keep_kernel,
        [shape((rows, tracks_half), BF16)],
        [gained, tracks, to_keep, scale],
        "kept_tracks",
        flops=rows * features * tracks_half,
    )
    (out,) = call(
        functools.partial(average_kernel, 4),
        [shape((rows, tracks_half), F32)],
        [kept, received, track_pairs.reshape(1, tracks_half)],
        "average",
        scratch=[pltpu.VMEM((rows, tracks_half), F32), pltpu.SemaphoreType.DMA((4,))],
        out_space=hbm,
    )
    return out


def solution(mesh):
    placed = (
        P(("groups", "pos")),
        P(None, "heads"),
        P(),
        P(None, "heads"),
        P(None, "heads"),
        P(None, "heads"),
        P("heads", None),
        P(),
        P(None, None, "heads"),
        P(("strand", "heads")),
    )
    return jax.shard_map(
        body,
        mesh=mesh,
        in_specs=placed,
        out_specs=P(("groups", "pos"), ("strand", "heads")),
        check_vma=False,
    )
```

```python
import functools
import math

import jax
import jax.experimental.pallas as pl
import jax.experimental.pallas.tpu as pltpu
import jax.numpy as jnp
from jax import lax
from jax.sharding import PartitionSpec as P

KDIM = 128
VDIM = 192
BIN = 128
BASES = 4
LANES = 128
VMEM_LIMIT = 48 * 2**20
F32 = jnp.float32
BF16 = jnp.bfloat16


def shifted(value, axis, distance):
    size = lax.axis_size(axis)
    return lax.ppermute(value, axis, [(i, (i + distance) % size) for i in range(size)])


def matmul(a, b):
    return jnp.dot(a, b, preferred_element_type=F32)


def matmul_t(a, b):
    return lax.dot_general(a, b, (((1,), (1,)), ((), ())), preferred_element_type=F32)


def call(kernel, outs, operands, name, scratch=(), spaces=None, flops=0, spare=0, out_space=None):
    vmem = pl.BlockSpec(memory_space=pltpu.VMEM)
    spaces = spaces or [None] * len(operands)
    operands = [
        v if s is None else pltpu.with_memory_space_constraint(v, s) for v, s in zip(operands, spaces)
    ]
    specs = [vmem if s is None else pl.BlockSpec(memory_space=s) for s in spaces]
    held = [v for v, s in zip(operands, spaces) if s is None] + list(outs)
    held += [v for v in scratch if hasattr(v, "shape") and hasattr(v, "dtype") and v.memory_space == pltpu.VMEM]
    moved = sum(math.prod(v.shape[:-1]) * max(v.shape[-1], LANES) * jnp.dtype(v.dtype).itemsize for v in held)
    return pl.pallas_call(
        kernel,
        out_shape=list(outs),
        in_specs=specs,
        out_specs=[pl.BlockSpec(memory_space=out_space or pltpu.VMEM)] * len(outs),
        scratch_shapes=list(scratch),
        compiler_params=pltpu.CompilerParams(
            vmem_limit_bytes=min(VMEM_LIMIT, moved + moved // 4 + 6 * 2**20 + spare)
        ),
        cost_estimate=pl.CostEstimate(flops=flops, bytes_accessed=moved, transcendentals=0),
        name=name,
    )(*operands)


def shape(dims, dtype):
    return jax.ShapeDtypeStruct(tuple(dims), dtype)


def over_blocks(total, block, step):
    if total == block:
        step(0)
    else:

        def one(i, carry):
            step(pl.multiple_of(i * block, block))
            return carry

        lax.fori_loop(0, total // block, one, 0)


def stage_kernel(chunks, embed, key_t, value_t, codes, *refs):
    part_kv, pieces = refs[0], refs[1 : 1 + chunks]
    codes_out, raw_codes, sems = refs[1 + chunks :]
    strand = lax.axis_index("strand")
    part = strand * lax.axis_size("groups") + lax.axis_index("groups")
    key_cols, value_cols = key_t.shape[0], value_t.shape[0]
    kv_width = part_kv.shape[1]
    half, width = pieces[0].shape
    cols = pl.ds(pl.multiple_of(part * kv_width, LANES), kv_width)
    rows = pl.ds(pl.multiple_of(strand * half, half), half)
    copies = [
        pltpu.make_async_copy(key_t.at[:, cols], part_kv.at[pl.ds(0, key_cols)], sems.at[0]),
        pltpu.make_async_copy(value_t.at[:, cols], part_kv.at[pl.ds(key_cols, value_cols)], sems.at[1]),
    ]
    for i in range(chunks):
        source = embed.at[rows, pl.ds(i * width, width)]
        copies.append(pltpu.make_async_copy(source, pieces[i], sems.at[2 + i]))
    copies.append(pltpu.make_async_copy(codes, raw_codes, sems.at[2 + chunks]))
    for copy in copies:
        copy.start()
    copies[-1].wait()
    codes_out[...] = raw_codes[...].astype(F32).astype(BF16)
    for copy in copies[:-1]:
        copy.wait()


def prepare_kernel(rows, slots, embed, key_t, value_t, w_query, gain, last_gain, *refs):
    table, key_out, value_out, query_out, gain_out, last_out, cosine, sine = refs[:8]
    raw_gain, raw_last, sems = refs[8:]
    strand, pos = lax.axis_index("strand"), lax.axis_index("pos")
    half = embed.shape[0] // 2
    pairs = [(gain, raw_gain), (last_gain, raw_last)]
    for i in range(2):
        part = strand if i == 0 else 1 - strand
        source = embed.at[pl.ds(pl.multiple_of(part * half, half), half)]
        pairs.append((source, table.at[pl.ds(i * half, half)]))
    pairs += [(key_t, key_out), (value_t, value_out), (w_query, query_out)]
    copies = [pltpu.make_async_copy(a, b, sems.at[i]) for i, (a, b) in enumerate(pairs)]
    for copy in copies:
        copy.start()
    total = cosine.shape[0]
    blocks = total // rows
    lane = lax.broadcasted_iota(jnp.int32, (1, KDIM), 1)
    inverse = jnp.exp((lane % (KDIM // 2)).astype(F32) * (-math.log(10000.0) / (KDIM // 2)))
    sign = jnp.where(lane < KDIM // 2, -1.0, 1.0)
    offset = lax.broadcasted_iota(jnp.int32, (rows, KDIM), 0)
    for copy in copies[:2]:
        copy.wait()
    gain_out[...] = raw_gain[...].reshape(gain_out.shape)
    last_out[...] = raw_last[...].reshape(last_out.shape)

    for i, (forward, reverse) in enumerate(slots):
        behind = jnp.where(strand == 0, forward, reverse)
        place = lax.rem(pos + blocks - behind, blocks) * rows + offset
        angle = jnp.where(strand == 0, place, total - 1 - place).astype(F32) * inverse
        cosine[i * rows : (i + 1) * rows, :] = jnp.cos(angle)
        sine[i * rows : (i + 1) * rows, :] = jnp.sin(angle) * sign
    for copy in copies[2:]:
        copy.wait()


def fetch_kernel(w_out, out, sems):
    heads = w_out.shape[0] // VDIM
    rest = VDIM - LANES
    copies = []
    for head in range(heads):
        for begin, count, spot in ((0, LANES, head * LANES), (LANES, rest, heads * LANES + head * rest)):
            source = w_out.at[pl.ds(head * VDIM + begin, count)]
            copies.append(pltpu.make_async_copy(source, out.at[pl.ds(spot, count)], sems.at[len(copies)]))
    for copy in copies:
        copy.start()
    for copy in copies:
        copy.wait()


def block_of(count, rows):
    if count <= 4 * rows:
        return count
    return 4 * rows if count % (4 * rows) == 0 else rows


def mark(onehot, codes, first, entries, rows):
    strand = lax.axis_index("strand")
    half = entries // 2
    count = codes.shape[0]
    spot = lax.broadcasted_iota(jnp.int32, (BIN, entries), 1)
    owner = jnp.where(spot < half, strand, 1 - strand)
    entry = owner * half + spot % half
    entry = jnp.where(strand == 0, entry, entries - 1 - entry)
    place = lax.broadcasted_iota(jnp.int32, (BIN, entries), 0)
    spread = jnp.where(place == entry // BASES, 1.0, 0.0).astype(BF16)
    wanted = (entry[:1] % BASES).astype(F32)
    block = block_of(count, rows)

    def step(begin):
        found = matmul(codes[pl.ds(begin, block), :], spread) == wanted
        onehot[pl.ds(first + begin, block), :] = jnp.where(found, 1.0, 0.0).astype(BF16)

    over_blocks(count, block, step)


def absorb(onehot, span, table, rows, start, width, weights, before, after):
    kv_t, w_query, gain = weights
    first, count = span
    block = block_of(count, rows)
    cols = pl.ds(pl.multiple_of(start, LANES), width)

    def some(here):
        found = matmul(onehot[here, :], table[...]).astype(BF16)
        floats = found.astype(F32)
        return found, floats, (floats * gain[:, cols]).astype(BF16)

    def step(begin):
        here = pl.ds(first + begin, block)
        found, floats, gained = some(here)
        square = jnp.sum(floats * floats, axis=1, keepdims=True)
        kv = matmul_t(gained, kv_t[:, cols])
        after[0][here, :] = square if before is None else before[0][here, :] + square
        after[1][here, :] = kv if before is None else before[1][here, :] + kv
        return found, gained

    if count == block:
        found, gained = step(0)
        found, gained = found[:rows], gained[:rows]
    else:
        over_blocks(count, block, lambda begin: step(begin) and None)
        found, _, gained = some(pl.ds(0, rows))
    if first:
        return None
    query = matmul(gained, w_query[cols, :])
    after[2][...] = query if before is None else before[2][...] + query
    return found


def own_kernel(blocks, kv_steps, *refs):
    codes = refs[:blocks]
    table, key_t, value_t = refs[blocks : blocks + 3]
    parts = refs[blocks + 3 : blocks + 3 + len(kv_steps)]
    w_query, gain, onehot, kv_t, own, square, kv_sum, q_sum, all_codes = refs[blocks + 3 + len(kv_steps) :]
    strand, mine, group = lax.axis_index("strand"), lax.axis_index("heads"), lax.axis_index("groups")
    size, groups = lax.axis_size("heads"), lax.axis_size("groups")
    key_cols, value_cols = key_t.shape[0], value_t.shape[0]
    entries, width = table.shape
    rows = codes[0].shape[0]
    for i in range(blocks):
        all_codes[i * rows : (i + 1) * rows, :] = codes[i][...]

    def kv_rows(owner):
        key_rows = pl.ds(pl.multiple_of(owner * key_cols, 16), key_cols)
        return key_rows, pl.ds(pl.multiple_of(KDIM + owner * value_cols, 16), value_cols)

    key_rows, value_rows = kv_rows(mine)
    kv_t[key_rows, :] = key_t[...]
    kv_t[value_rows, :] = value_t[...]
    for piece, (step, group_step, core_step) in zip(parts, kv_steps):
        key_rows, value_rows = kv_rows(lax.rem(mine + size - step, size))
        core = strand if core_step == 0 else 1 - strand
        part = core * groups + lax.rem(group + groups - group_step, groups)
        cols = pl.ds(pl.multiple_of(part * piece.shape[1], LANES), piece.shape[1])
        kv_t[key_rows, cols] = piece[:key_cols, :]
        kv_t[value_rows, cols] = piece[key_cols:, :]
    mark(onehot, all_codes, 0, entries, rows)
    weights = (kv_t, w_query, gain)
    span = (0, blocks * rows)
    own[...] = absorb(onehot, span, table, rows, mine * width, width, weights, None, (square, kv_sum, q_sum))


def chunk_start(step, index, chunks, width):
    size = lax.axis_size("heads")
    owner = lax.rem(lax.axis_index("heads") + size - step, size)
    return (owner * chunks + index) * width


def join_kernel(step, index, chunks, rows, late, *refs):
    mine, theirs, onehot_in, kv_t, w_query, gain, square_in, kv_in, q_in, own_table = refs[:10]
    codes = refs[10 : 10 + late]
    onehot, found, square, kv_sum, q_sum, table, all_codes = refs[10 + late :]
    half, width = mine.shape
    own_width = own_table.shape[1]
    early = onehot_in.shape[0]
    weights = (kv_t, w_query, gain)
    for i in range(late):
        all_codes[i * rows : (i + 1) * rows, :] = codes[i][...]
    mark(onehot, all_codes, early, own_table.shape[0], rows)
    onehot[:early, :] = onehot_in[...]
    square[:early, :] = square_in[...]
    kv_sum[:early, :] = kv_in[...]
    span = (early, late * rows)
    begin = lax.axis_index("heads") * own_width
    absorb(onehot, span, own_table, rows, begin, own_width, weights, None, (square, kv_sum, None))
    table[:half, :] = mine[...]
    table[half:, :] = theirs[...]
    begin = chunk_start(step, index, chunks, width)
    span = (0, early + late * rows)
    sums = (square, kv_sum, q_sum)
    found[...] = absorb(onehot, span, table, rows, begin, width, weights, (square, kv_sum, q_in), sums)


def chunk_kernel(step, index, chunks, rows, *refs):
    mine, theirs, onehot, kv_t, w_query, gain, square, kv_sum, q_sum = refs[:9]
    found, square_out, kv_out, q_out, table = refs[9:]
    half, width = mine.shape
    table[:half, :] = mine[...]
    table[half:, :] = theirs[...]
    found[...] = absorb(
        onehot,
        (0, onehot.shape[0]),
        table,
        rows,
        chunk_start(step, index, chunks, width),
        width,
        (kv_t, w_query, gain),
        (square, kv_sum, q_sum),
        (square_out, kv_out, q_out),
    )


def turn(values, cosine, sine):
    floats = values.astype(BF16).astype(F32)
    return (floats * cosine + pltpu.roll(floats, KDIM // 2, 1) * sine).astype(BF16)


def attend_kernel(steps, chunks, *refs):
    mine, theirs, onehot, kv_t, w_query, gain, square, kv_sum, q_sum = refs[:9]
    own, cosine, sine, out = refs[9:13]
    founds = refs[13 : 13 + len(steps) - 1]
    share, merged, inputs = refs[12 + len(steps) : 15 + len(steps)]
    table, squares, sums, queries, keys, values = refs[15 + len(steps) :]
    half, width = mine.shape
    rows, own_width = own.shape
    features = inputs.shape[1]
    total = onehot.shape[0]
    block = block_of(total, rows)
    table[:half, :] = mine[...]
    table[half:, :] = theirs[...]
    start = chunk_start(*steps[-1], chunks, width)
    span, weights = (0, total), (kv_t, w_query, gain)
    before, after = (square, kv_sum, q_sum), (squares, sums, queries)
    last = absorb(onehot, span, table, rows, start, width, weights, before, after)
    inputs[:, pl.ds(pl.multiple_of(start, LANES), width)] = last
    for found, spot in zip(founds, steps):
        inputs[:, pl.ds(pl.multiple_of(chunk_start(*spot, chunks, width), LANES), width)] = found[...]
    begin = pl.multiple_of(lax.axis_index("heads") * own_width, LANES)
    inputs[:, pl.ds(begin, own_width)] = own[...]

    def finish(begin):
        here = pl.ds(begin, block)
        scaled = sums[here, :] * lax.rsqrt(squares[here, :] / features + 1e-06)
        keys[here, :] = turn(scaled[:, :KDIM], cosine[here, :], sine[here, :])
        values[here, :] = scaled[:, KDIM:].astype(BF16)

    over_blocks(total, block, finish)
    scaled = queries[...] * lax.rsqrt(squares[:rows, :] / features + 1e-06)
    heads = queries.shape[1] // KDIM
    for head in range(heads):
        query = turn(scaled[:, head * KDIM : (head + 1) * KDIM], cosine[:rows, :], sine[:rows, :])
        scores = matmul_t(query, keys[...]) * KDIM ** (-0.5)
        weights = jnp.exp(scores - jnp.max(scores, axis=1, keepdims=True))
        weight_sum = jnp.sum(weights, axis=1, keepdims=True)
        found = (matmul(weights.astype(BF16), values[...]) / weight_sum).astype(BF16)
        merged[:, head * LANES : (head + 1) * LANES] = found[:, :LANES]
        spot = heads * LANES + head * (VDIM - LANES)
        merged[:, spot : spot + VDIM - LANES] = found[:, LANES:]
    share[...] = matmul(merged[...], out[:, : share.shape[1]]).astype(BF16)


def second_kernel(merged, out, share):
    share[...] = matmul(merged[...], out[:, share.shape[1] :]).astype(BF16)


def gather_hidden(shares, inputs, gain, chunk):
    width = shares[0].shape[1]
    cols = slice(chunk * width, (chunk + 1) * width)
    total = shares[0][...].astype(F32)
    for other in shares[1:]:
        total = total + other[...].astype(F32)
    hidden = (inputs[:, cols].astype(F32) + total).astype(BF16).astype(F32)
    return jnp.sum(hidden * hidden, axis=1, keepdims=True), (hidden * gain[:, cols]).astype(BF16)


def soft(logits):
    return jnp.maximum(logits, 0.0) + jnp.log1p(jnp.exp(-jnp.abs(logits)))


def first_tracks_kernel(size, *refs):
    shares = refs[:size]
    inputs, gain, tracks, square, to_send, to_keep = refs[size:]
    strand = lax.axis_index("strand")
    width = shares[0].shape[1]
    square[...], gained = gather_hidden(shares, inputs, gain, 0)
    to_send[...] = matmul(gained, tracks[1 - strand, :width, :])
    to_keep[...] = matmul(gained, tracks[strand, :width, :])


def send_kernel(size, *refs):
    shares = refs[:size]
    inputs, gain, tracks, square, to_send, sent, gained_out, scale_out = refs[size:]
    strand = lax.axis_index("strand")
    width = shares[0].shape[1]
    total, gained = gather_hidden(shares, inputs, gain, 1)
    scale = lax.rsqrt((square[...] + total) / (2 * width) + 1e-06)
    logits = to_send[...] + matmul(gained, tracks[1 - strand, width:, :])
    sent[...] = soft(logits * scale).astype(BF16)
    gained_out[...] = gained
    scale_out[...] = scale


def swap_pairs(values, pairs):
    even = lax.broadcasted_iota(jnp.int32, (1, LANES), 1) % 2 == 0
    parts = []
    for begin in range(0, values.shape[1], LANES):
        part = values[:, begin : begin + LANES]
        swapped = (pairs[:, begin : begin + LANES] % 2 == 0) != even
        partner = jnp.where(even, pltpu.roll(part, LANES - 1, 1), pltpu.roll(part, 1, 1))
        parts.append(jnp.where(swapped, partner, part))
    return jnp.concatenate(parts, axis=1)


def keep_kernel(gained, tracks, to_keep, scale, pairs, kept):
    strand = lax.axis_index("strand")
    width = gained.shape[1]
    logits = to_keep[...] + matmul(gained[...], tracks[strand, width:, :])
    found = soft(logits * scale[...]).astype(BF16).astype(F32)
    kept[...] = jnp.where(strand == 0, found, swap_pairs(found, pairs)).astype(BF16)


def average_kernel(parts, kept, received, pairs, out, stage, sems):
    strand = lax.axis_index("strand")
    rows = kept.shape[0] // parts
    copies = []
    for i in range(parts):
        here = slice(i * rows, (i + 1) * rows)
        theirs = received[here, :].astype(F32)
        theirs = jnp.where(strand == 0, swap_pairs(theirs, pairs), theirs)
        stage[here, :] = 0.5 * (kept[here, :].astype(F32) + theirs)
        copies.append(pltpu.make_async_copy(stage.at[here], out.at[here], sems.at[i]))
        copies[-1].start()
    for copy in copies:
        copy.wait()


def body(
    base_codes,
    embed_table,
    attn_gain,
    w_query,
    w_key,
    w_value,
    w_out,
    head_gain,
    w_tracks,
    track_pairs,
):
    rows = base_codes.shape[0] // BIN
    blocks = lax.axis_size("pos")
    size = lax.axis_size("heads")
    features, q_cols = w_query.shape
    entries, width = embed_table.shape
    groups = lax.axis_size("groups")
    key_t, value_t = w_key.T, w_value.T
    kv_cols = key_t.shape[0] + value_t.shape[0]
    kv_all = KDIM + VDIM
    half = entries // 2
    total = blocks * rows
    tracks_half = w_tracks.shape[2]
    chunks = 2 if width % (2 * LANES) == 0 else 1
    wide = width // chunks

    early, late = [(0, 0)], []
    for k in range(1, blocks, 2):
        early.append((k, min(k + 1, blocks - 1)))
        if k + 1 < blocks:
            late.append((k + 1, k))

    hbm = pltpu.HBM
    part_kv, *own_pieces, own_codes = call(
        functools.partial(stage_kernel, chunks),
        [shape((kv_cols, features // (2 * groups)), BF16)]
        + [shape((half, wide), BF16)] * chunks
        + [shape((rows, BIN), BF16)],
        [embed_table, key_t, value_t, base_codes.reshape(rows, BIN)],
        "stage",
        scratch=[pltpu.VMEM((rows, BIN), jnp.int32), pltpu.SemaphoreType.DMA((3 + chunks,))],
        spaces=[hbm] * 4,
    )
    table, key_own, value_own, query_own, gain, last_gain, cosine, sine = call(
        functools.partial(prepare_kernel, rows, early + late),
        [
            shape((entries, width), BF16),
            shape(key_t.shape, BF16),
            shape(value_t.shape, BF16),
            shape(w_query.shape, BF16),
            shape((1, features), F32),
            shape((1, features), F32),
            shape((total, KDIM), F32),
            shape((total, KDIM), F32),
        ],
        [embed_table, key_t, value_t, w_query, attn_gain, head_gain],
        "prepare",
        scratch=[
            pltpu.VMEM((features,), F32),
            pltpu.VMEM((features,), F32),
            pltpu.SemaphoreType.DMA((7,)),
        ],
        spaces=[hbm] * 6,
    )
    kv_parts, kv_steps, pieces, steps = [], [], [], []
    from_heads = [shifted(part_kv, "heads", step) for step in range(1, size)]
    if from_heads:
        from_heads[0], table = lax.optimization_barrier((from_heads[0], table))
    to_core = [shifted(here, "strand", 1) for here in from_heads]
    (out_here,) = call(
        fetch_kernel,
        [shape(w_out.shape, BF16)],
        [w_out],
        "fetch_out",
        scratch=[pltpu.SemaphoreType.DMA((2 * (q_cols // KDIM),))],
        spaces=[hbm],
    )
    raw = []
    for k, other in early[1:]:
        if k != other:
            pairs = [((p, s), ((p + k + s) % blocks, s)) for p in range(blocks) for s in range(2)]
            pairs = [(2 * p + s, 2 * q + t) for (p, s), (q, t) in pairs]
            raw.append(lax.ppermute(own_codes, ("pos", "strand"), pairs))
        else:
            if to_core:
                own_codes, to_core[0] = lax.optimization_barrier((own_codes, to_core[0]))
            raw.append(shifted(own_codes, "pos", k))
    if raw:
        raw[0], out_here = lax.optimization_barrier((raw[0], out_here))
    for step in range(1, size):
        for k in range(groups):
            here = from_heads[step - 1] if k == 0 else shifted(from_heads[step - 1], "groups", k)
            kv_parts += [here, to_core[step - 1] if k == 0 else shifted(here, "strand", 1)]
            kv_steps += [(step, k, 0), (step, k, 1)]
    for step in range(1, size):
        for i in range(chunks):
            here = shifted(own_pieces[i], "heads", step)
            if step == 1 and i == chunks - 1 and raw:
                here, *raw = lax.optimization_barrier((here, *raw))
            pieces.append((here, shifted(here, "strand", 1)))
            steps.append((step, i))

    swapped = [shifted(raw[i], "strand", 1) for i in range(len(late))]
    codes = [own_codes] + raw
    if len(steps) < 2:
        codes, swapped = codes + swapped, []

    def sums_of(count):
        return [shape((count, 1), F32), shape((count, kv_all), F32), shape((rows, q_cols), F32)]

    count = rows * len(codes)
    onehot, kv_t, own, *state = call(
        functools.partial(own_kernel, len(codes), kv_steps),
        [shape((count, entries), BF16), shape((kv_all, features), BF16), shape((rows, width), BF16)]
        + sums_of(count),
        codes + [table, key_own, value_own] + kv_parts + [query_own, gain],
        "own_features",
        scratch=[pltpu.VMEM((count, BIN), BF16)],
        flops=2 * count * width * (entries + kv_all),
        spare=8 * total * entries,
    )
    founds = []
    for (step, i), pair in zip(steps[:-1], pieces[:-1]):
        operands = list(pair) + [onehot, kv_t, query_own, gain] + state
        outs = [shape((rows, wide), BF16)] + sums_of(total)
        scratch = [pltpu.VMEM((entries, wide), BF16)]
        if swapped:
            kernel = functools.partial(join_kernel, step, i, chunks, rows, len(swapped))
            operands += [table] + swapped
            outs = [shape((total, entries), BF16)] + outs
            scratch.append(pltpu.VMEM((rows * len(swapped), BIN), BF16))
        else:
            kernel = functools.partial(chunk_kernel, step, i, chunks, rows)
        results = call(
            kernel,
            outs,
            operands,
            "other_features",
            scratch=scratch,
            flops=2 * total * wide * (entries + kv_all),
            spare=8 * total * entries,
        )
        if swapped:
            onehot, *results = results
            swapped = []
        found, *state = results
        founds.append(found)
    o_cols = q_cols // KDIM * VDIM
    share_one, merged, inputs = call(
        functools.partial(attend_kernel, steps, chunks),
        [
            shape((rows, features // 2), BF16),
            shape((rows, o_cols), BF16),
            shape((rows, features), BF16),
        ],
        list(pieces[-1]) + [onehot, kv_t, query_own, gain] + state + [own, cosine, sine, out_here] + founds,
        "attend",
        scratch=[
            pltpu.VMEM((entries, wide), BF16),
            pltpu.VMEM((total, 1), F32),
            pltpu.VMEM((total, kv_all), F32),
            pltpu.VMEM((rows, q_cols), F32),
            pltpu.VMEM((total, KDIM), BF16),
            pltpu.VMEM((total, VDIM), BF16),
        ],
        flops=2 * total * wide * (entries + kv_all) + 2 * total * q_cols * rows * 3,
        spare=8 * total * entries,
    )
    (share_two,) = call(
        second_kernel,
        [shape((rows, features // 2), BF16)],
        [merged, out_here],
        "second_share",
        flops=rows * o_cols * features,
    )
    ones = [share_one] + [shifted(share_one, "heads", k) for k in range(1, size)]
    twos = [share_two] + [shifted(share_two, "heads", k) for k in range(1, size)]
    weights, _ = lax.optimization_barrier((w_tracks, share_two))
    tracks = lax.optimization_barrier(weights.transpose(1, 0, 2))
    square, to_send, to_keep = call(
        functools.partial(first_tracks_kernel, size),
        [
            shape((rows, 1), F32),
            shape((rows, tracks_half), F32),
            shape((rows, tracks_half), F32),
        ],
        ones + [inputs, last_gain, tracks],
        "first_tracks",
        flops=2 * rows * features * tracks_half,
    )
    sent, gained, scale = call(
        functools.partial(send_kernel, size),
        [
            shape((rows, tracks_half), BF16),
            shape((rows, features // 2), BF16),
            shape((rows, 1), F32),
        ],
        twos + [inputs, last_gain, tracks, square, to_send],
        "sent_tracks",
        flops=rows * features * tracks_half,
    )
    received = shifted(sent, "strand", 1)
    pairs = track_pairs.reshape(1, tracks_half)
    (kept,) = call(
        keep_kernel,
        [shape((rows, tracks_half), BF16)],
        [gained, tracks, to_keep, scale, pairs],
        "kept_tracks",
        flops=rows * features * tracks_half,
    )
    (out,) = call(
        functools.partial(average_kernel, 4),
        [shape((rows, tracks_half), F32)],
        [kept, received, pairs],
        "average",
        scratch=[pltpu.VMEM((rows, tracks_half), F32), pltpu.SemaphoreType.DMA((4,))],
        out_space=hbm,
    )
    return out


def solution(mesh):
    placed = (
        P(("groups", "pos")),
        P(None, "heads"),
        P(),
        P(None, "heads"),
        P(None, "heads"),
        P(None, "heads"),
        P("heads", None),
        P(),
        P(None, None, "heads"),
        P(("strand", "heads")),
    )
    return jax.shard_map(
        body,
        mesh=mesh,
        in_specs=placed,
        out_specs=P(("groups", "pos"), ("strand", "heads")),
        check_vma=False,
    )
```

```python
import functools
import math

import jax
import jax.experimental.pallas as pl
import jax.experimental.pallas.tpu as pltpu
import jax.numpy as jnp
from jax import lax
from jax.sharding import PartitionSpec as P

KDIM = 128
VDIM = 192
BIN = 128
BASES = 4
LANES = 128
VMEM_LIMIT = 48 * 2**20
F32 = jnp.float32
BF16 = jnp.bfloat16


def shifted(value, axis, distance):
    size = lax.axis_size(axis)
    return lax.ppermute(value, axis, [(i, (i + distance) % size) for i in range(size)])


def matmul(a, b):
    return jnp.dot(a, b, preferred_element_type=F32)


def matmul_t(a, b):
    return lax.dot_general(a, b, (((1,), (1,)), ((), ())), preferred_element_type=F32)


def call(kernel, outs, operands, name, scratch=(), spaces=None, flops=0, spare=0, out_space=None):
    vmem = pl.BlockSpec(memory_space=pltpu.VMEM)
    spaces = spaces or [None] * len(operands)
    operands = [
        v if s is None else pltpu.with_memory_space_constraint(v, s) for v, s in zip(operands, spaces)
    ]
    specs = [vmem if s is None else pl.BlockSpec(memory_space=s) for s in spaces]
    held = [v for v, s in zip(operands, spaces) if s is None] + list(outs)
    held += [v for v in scratch if hasattr(v, "shape") and hasattr(v, "dtype") and v.memory_space == pltpu.VMEM]
    moved = sum(math.prod(v.shape[:-1]) * max(v.shape[-1], LANES) * jnp.dtype(v.dtype).itemsize for v in held)
    return pl.pallas_call(
        kernel,
        out_shape=list(outs),
        in_specs=specs,
        out_specs=[pl.BlockSpec(memory_space=out_space or pltpu.VMEM)] * len(outs),
        scratch_shapes=list(scratch),
        compiler_params=pltpu.CompilerParams(
            vmem_limit_bytes=min(VMEM_LIMIT, moved + moved // 4 + 6 * 2**20 + spare)
        ),
        cost_estimate=pl.CostEstimate(flops=flops, bytes_accessed=moved, transcendentals=0),
        name=name,
    )(*operands)


def shape(dims, dtype):
    return jax.ShapeDtypeStruct(tuple(dims), dtype)


def over_blocks(total, block, step):
    if total == block:
        step(0)
    else:

        def one(i, carry):
            step(pl.multiple_of(i * block, block))
            return carry

        lax.fori_loop(0, total // block, one, 0)


def stage_kernel(chunks, embed, key_t, value_t, codes, *refs):
    part_kv, pieces = refs[0], refs[1 : 1 + chunks]
    codes_out, raw_codes, sems = refs[1 + chunks :]
    strand = lax.axis_index("strand")
    part = strand * lax.axis_size("groups") + lax.axis_index("groups")
    key_cols, value_cols = key_t.shape[0], value_t.shape[0]
    kv_width = part_kv.shape[1]
    half, width = pieces[0].shape
    cols = pl.ds(pl.multiple_of(part * kv_width, LANES), kv_width)
    rows = pl.ds(pl.multiple_of(strand * half, half), half)
    copies = [
        pltpu.make_async_copy(key_t.at[:, cols], part_kv.at[pl.ds(0, key_cols)], sems.at[0]),
        pltpu.make_async_copy(value_t.at[:, cols], part_kv.at[pl.ds(key_cols, value_cols)], sems.at[1]),
    ]
    for i in range(chunks):
        source = embed.at[rows, pl.ds(i * width, width)]
        copies.append(pltpu.make_async_copy(source, pieces[i], sems.at[2 + i]))
    copies.append(pltpu.make_async_copy(codes, raw_codes, sems.at[2 + chunks]))
    for copy in copies:
        copy.start()
    copies[-1].wait()
    codes_out[...] = raw_codes[...].astype(F32).astype(BF16)
    for copy in copies[:-1]:
        copy.wait()


def prepare_kernel(rows, slots, embed, key_t, value_t, w_query, gain, last_gain, *refs):
    table, key_out, value_out, query_out, gain_out, last_out, cosine, sine = refs[:8]
    raw_gain, raw_last, sems = refs[8:]
    strand, pos = lax.axis_index("strand"), lax.axis_index("pos")
    half = embed.shape[0] // 2
    pairs = [(gain, raw_gain), (last_gain, raw_last)]
    for i in range(2):
        part = strand if i == 0 else 1 - strand
        source = embed.at[pl.ds(pl.multiple_of(part * half, half), half)]
        pairs.append((source, table.at[pl.ds(i * half, half)]))
    pairs += [(key_t, key_out), (value_t, value_out), (w_query, query_out)]
    copies = [pltpu.make_async_copy(a, b, sems.at[i]) for i, (a, b) in enumerate(pairs)]
    for copy in copies:
        copy.start()
    total = cosine.shape[0]
    blocks = total // rows
    lane = lax.broadcasted_iota(jnp.int32, (1, KDIM), 1)
    inverse = jnp.exp((lane % (KDIM // 2)).astype(F32) * (-math.log(10000.0) / (KDIM // 2)))
    sign = jnp.where(lane < KDIM // 2, -1.0, 1.0)
    offset = lax.broadcasted_iota(jnp.int32, (rows, KDIM), 0)
    for copy in copies[:2]:
        copy.wait()
    gain_out[...] = raw_gain[...].reshape(gain_out.shape)
    last_out[...] = raw_last[...].reshape(last_out.shape)

    for i, (forward, reverse) in enumerate(slots):
        behind = jnp.where(strand == 0, forward, reverse)
        place = lax.rem(pos + blocks - behind, blocks) * rows + offset
        angle = jnp.where(strand == 0, place, total - 1 - place).astype(F32) * inverse
        cosine[i * rows : (i + 1) * rows, :] = jnp.cos(angle)
        sine[i * rows : (i + 1) * rows, :] = jnp.sin(angle) * sign
    for copy in copies[2:]:
        copy.wait()


def fetch_kernel(w_out, out, sems):
    heads = w_out.shape[0] // VDIM
    rest = VDIM - LANES
    copies = []
    for head in range(heads):
        for begin, count, spot in ((0, LANES, head * LANES), (LANES, rest, heads * LANES + head * rest)):
            source = w_out.at[pl.ds(head * VDIM + begin, count)]
            copies.append(pltpu.make_async_copy(source, out.at[pl.ds(spot, count)], sems.at[len(copies)]))
    for copy in copies:
        copy.start()
    for copy in copies:
        copy.wait()


def block_of(count, rows):
    if count <= 4 * rows:
        return count
    return 4 * rows if count % (4 * rows) == 0 else rows


def mark(onehot, codes, first, entries, rows):
    strand = lax.axis_index("strand")
    half = entries // 2
    count = codes.shape[0]
    spot = lax.broadcasted_iota(jnp.int32, (BIN, entries), 1)
    owner = jnp.where(spot < half, strand, 1 - strand)
    entry = owner * half + spot % half
    entry = jnp.where(strand == 0, entry, entries - 1 - entry)
    place = lax.broadcasted_iota(jnp.int32, (BIN, entries), 0)
    spread = jnp.where(place == entry // BASES, 1.0, 0.0).astype(BF16)
    wanted = (entry[:1] % BASES).astype(F32)
    block = block_of(count, rows)

    def step(begin):
        found = matmul(codes[pl.ds(begin, block), :], spread) == wanted
        onehot[pl.ds(first + begin, block), :] = jnp.where(found, 1.0, 0.0).astype(BF16)

    over_blocks(count, block, step)


def absorb(onehot, span, table, rows, start, width, weights, before, after):
    kv_t, w_query, gain = weights
    first, count = span
    block = block_of(count, rows)
    cols = pl.ds(pl.multiple_of(start, LANES), width)

    def some(here):
        found = matmul(onehot[here, :], table[...]).astype(BF16)
        floats = found.astype(F32)
        return found, floats, (floats * gain[:, cols]).astype(BF16)

    def step(begin):
        here = pl.ds(first + begin, block)
        found, floats, gained = some(here)
        square = jnp.sum(floats * floats, axis=1, keepdims=True)
        kv = matmul_t(gained, kv_t[:, cols])
        after[0][here, :] = square if before is None else before[0][here, :] + square
        after[1][here, :] = kv if before is None else before[1][here, :] + kv
        return found, gained

    if count == block:
        found, gained = step(0)
        found, gained = found[:rows], gained[:rows]
    else:
        over_blocks(count, block, lambda begin: step(begin) and None)
        found, _, gained = some(pl.ds(0, rows))
    if first:
        return None
    query = matmul(gained, w_query[cols, :])
    after[2][...] = query if before is None else before[2][...] + query
    return found


def own_kernel(blocks, kv_steps, *refs):
    codes = refs[:blocks]
    table, key_t, value_t = refs[blocks : blocks + 3]
    parts = refs[blocks + 3 : blocks + 3 + len(kv_steps)]
    w_query, gain, onehot, kv_t, own, square, kv_sum, q_sum, all_codes = refs[blocks + 3 + len(kv_steps) :]
    strand, mine, group = lax.axis_index("strand"), lax.axis_index("heads"), lax.axis_index("groups")
    size, groups = lax.axis_size("heads"), lax.axis_size("groups")
    key_cols, value_cols = key_t.shape[0], value_t.shape[0]
    entries, width = table.shape
    rows = codes[0].shape[0]
    for i in range(blocks):
        all_codes[i * rows : (i + 1) * rows, :] = codes[i][...]

    def kv_rows(owner):
        key_rows = pl.ds(pl.multiple_of(owner * key_cols, 16), key_cols)
        return key_rows, pl.ds(pl.multiple_of(KDIM + owner * value_cols, 16), value_cols)

    key_rows, value_rows = kv_rows(mine)
    kv_t[key_rows, :] = key_t[...]
    kv_t[value_rows, :] = value_t[...]
    for piece, (step, group_step, core_step) in zip(parts, kv_steps):
        key_rows, value_rows = kv_rows(lax.rem(mine + size - step, size))
        core = strand if core_step == 0 else 1 - strand
        part = core * groups + lax.rem(group + groups - group_step, groups)
        cols = pl.ds(pl.multiple_of(part * piece.shape[1], LANES), piece.shape[1])
        kv_t[key_rows, cols] = piece[:key_cols, :]
        kv_t[value_rows, cols] = piece[key_cols:, :]
    mark(onehot, all_codes, 0, entries, rows)
    weights = (kv_t, w_query, gain)
    span = (0, blocks * rows)
    own[...] = absorb(onehot, span, table, rows, mine * width, width, weights, None, (square, kv_sum, q_sum))


def chunk_start(step, index, chunks, width):
    size = lax.axis_size("heads")
    owner = lax.rem(lax.axis_index("heads") + size - step, size)
    return (owner * chunks + index) * width


def join_kernel(step, index, chunks, carry, rows, late, *refs):
    mine, theirs, onehot_in, kv_t, w_query, gain, square_in, kv_in, q_in, own_table = refs[:10]
    codes = refs[10 : 10 + late]
    onehot, found, square, kv_sum, q_sum, table, all_codes = refs[10 + late :]
    half, width = mine.shape
    own_width = own_table.shape[1]
    early = onehot_in.shape[0]
    weights = (kv_t, w_query, gain)
    for i in range(late):
        all_codes[i * rows : (i + 1) * rows, :] = codes[i][...]
    mark(onehot, all_codes, early, own_table.shape[0], rows)
    onehot[:early, :] = onehot_in[...]
    square[:early, :] = square_in[...]
    kv_sum[:early, :] = kv_in[...]
    span = (early, late * rows)
    begin = lax.axis_index("heads") * own_width
    absorb(onehot, span, own_table, rows, begin, own_width, weights, None, (square, kv_sum, None))
    taken = width - carry
    table[:half, :] = mine[:, :taken]
    table[half:, :] = theirs[:, :taken]
    begin = chunk_start(step, index, chunks, width)
    span = (0, early + late * rows)
    sums = (square, kv_sum, q_sum)
    found[...] = absorb(onehot, span, table, rows, begin, taken, weights, (square, kv_sum, q_in), sums)


def chunk_kernel(step, index, chunks, carry, rows, *refs):
    mine, theirs, onehot, kv_t, w_query, gain, square, kv_sum, q_sum = refs[:9]
    found, square_out, kv_out, q_out, table = refs[9:]
    half, width = mine.shape
    taken = width - carry
    table[:half, :] = mine[:, :taken]
    table[half:, :] = theirs[:, :taken]
    found[...] = absorb(
        onehot,
        (0, onehot.shape[0]),
        table,
        rows,
        chunk_start(step, index, chunks, width),
        taken,
        (kv_t, w_query, gain),
        (square, kv_sum, q_sum),
        (square_out, kv_out, q_out),
    )


def turn(values, cosine, sine):
    floats = values.astype(BF16).astype(F32)
    return (floats * cosine + pltpu.roll(floats, KDIM // 2, 1) * sine).astype(BF16)


def attend_kernel(steps, chunks, carry, *refs):
    if carry:
        earlier, refs = refs[:2], refs[2:]
    mine, theirs, onehot, kv_t, w_query, gain, square, kv_sum, q_sum = refs[:9]
    own, cosine, sine, out = refs[9:13]
    founds = refs[13 : 13 + len(steps) - 1]
    share, merged, inputs = refs[12 + len(steps) : 15 + len(steps)]
    table, squares, sums, queries, keys, values = refs[15 + len(steps) :]
    half, width = mine.shape
    rows, own_width = own.shape
    features = inputs.shape[1]
    total = onehot.shape[0]
    block = block_of(total, rows)
    if carry:
        table[:half, :carry] = earlier[0][:, width - carry :]
        table[half:, :carry] = earlier[1][:, width - carry :]
    table[:half, carry:] = mine[...]
    table[half:, carry:] = theirs[...]
    start = chunk_start(*steps[-1], chunks, width) - carry
    span, weights = (0, total), (kv_t, w_query, gain)
    before, after = (square, kv_sum, q_sum), (squares, sums, queries)
    last = absorb(onehot, span, table, rows, start, width + carry, weights, before, after)
    inputs[:, pl.ds(pl.multiple_of(start, LANES), width + carry)] = last
    for found, spot in zip(founds, steps):
        inputs[:, pl.ds(pl.multiple_of(chunk_start(*spot, chunks, width), LANES), found.shape[1])] = found[...]
    begin = pl.multiple_of(lax.axis_index("heads") * own_width, LANES)
    inputs[:, pl.ds(begin, own_width)] = own[...]

    def finish(begin):
        here = pl.ds(begin, block)
        scaled = sums[here, :] * lax.rsqrt(squares[here, :] / features + 1e-06)
        keys[here, :] = turn(scaled[:, :KDIM], cosine[here, :], sine[here, :])
        values[here, :] = scaled[:, KDIM:].astype(BF16)

    over_blocks(total, block, finish)
    scaled = queries[...] * lax.rsqrt(squares[:rows, :] / features + 1e-06)
    heads = queries.shape[1] // KDIM
    for head in range(heads):
        query = turn(scaled[:, head * KDIM : (head + 1) * KDIM], cosine[:rows, :], sine[:rows, :])
        scores = matmul_t(query, keys[...]) * KDIM ** (-0.5)
        weights = jnp.exp(scores - jnp.max(scores, axis=1, keepdims=True))
        weight_sum = jnp.sum(weights, axis=1, keepdims=True)
        found = (matmul(weights.astype(BF16), values[...]) / weight_sum).astype(BF16)
        merged[:, head * LANES : (head + 1) * LANES] = found[:, :LANES]
        spot = heads * LANES + head * (VDIM - LANES)
        merged[:, spot : spot + VDIM - LANES] = found[:, LANES:]
    share[...] = matmul(merged[...], out[:, : share.shape[1]]).astype(BF16)


def second_kernel(merged, out, share):
    share[...] = matmul(merged[...], out[:, share.shape[1] :]).astype(BF16)


def gather_hidden(shares, inputs, gain, chunk):
    width = shares[0].shape[1]
    cols = slice(chunk * width, (chunk + 1) * width)
    total = shares[0][...].astype(F32)
    for other in shares[1:]:
        total = total + other[...].astype(F32)
    hidden = (inputs[:, cols].astype(F32) + total).astype(BF16).astype(F32)
    return jnp.sum(hidden * hidden, axis=1, keepdims=True), (hidden * gain[:, cols]).astype(BF16)


def soft(logits):
    return jnp.maximum(logits, 0.0) + jnp.log1p(jnp.exp(-jnp.abs(logits)))


def first_tracks_kernel(size, *refs):
    shares = refs[:size]
    inputs, gain, tracks, square, to_send, to_keep = refs[size:]
    strand = lax.axis_index("strand")
    width = shares[0].shape[1]
    square[...], gained = gather_hidden(shares, inputs, gain, 0)
    to_send[...] = matmul(gained, tracks[1 - strand, :width, :])
    to_keep[...] = matmul(gained, tracks[strand, :width, :])


def send_kernel(size, *refs):
    shares = refs[:size]
    inputs, gain, tracks, square, to_send, sent, gained_out, scale_out = refs[size:]
    strand = lax.axis_index("strand")
    width = shares[0].shape[1]
    total, gained = gather_hidden(shares, inputs, gain, 1)
    scale = lax.rsqrt((square[...] + total) / (2 * width) + 1e-06)
    logits = to_send[...] + matmul(gained, tracks[1 - strand, width:, :])
    sent[...] = soft(logits * scale).astype(BF16)
    gained_out[...] = gained
    scale_out[...] = scale


def swap_pairs(values, pairs):
    even = lax.broadcasted_iota(jnp.int32, (1, LANES), 1) % 2 == 0
    parts = []
    for begin in range(0, values.shape[1], LANES):
        part = values[:, begin : begin + LANES]
        swapped = (pairs[:, begin : begin + LANES] % 2 == 0) != even
        partner = jnp.where(even, pltpu.roll(part, LANES - 1, 1), pltpu.roll(part, 1, 1))
        parts.append(jnp.where(swapped, partner, part))
    return jnp.concatenate(parts, axis=1)


def keep_kernel(gained, tracks, to_keep, scale, pairs, kept):
    strand = lax.axis_index("strand")
    width = gained.shape[1]
    logits = to_keep[...] + matmul(gained[...], tracks[strand, width:, :])
    found = soft(logits * scale[...]).astype(BF16).astype(F32)
    kept[...] = jnp.where(strand == 0, found, swap_pairs(found, pairs)).astype(BF16)


def average_kernel(parts, kept, received, pairs, out, stage, sems):
    strand = lax.axis_index("strand")
    rows = kept.shape[0] // parts
    copies = []
    for i in range(parts):
        here = slice(i * rows, (i + 1) * rows)
        theirs = received[here, :].astype(F32)
        theirs = jnp.where(strand == 0, swap_pairs(theirs, pairs), theirs)
        stage[here, :] = 0.5 * (kept[here, :].astype(F32) + theirs)
        copies.append(pltpu.make_async_copy(stage.at[here], out.at[here], sems.at[i]))
        copies[-1].start()
    for copy in copies:
        copy.wait()


def body(
    base_codes,
    embed_table,
    attn_gain,
    w_query,
    w_key,
    w_value,
    w_out,
    head_gain,
    w_tracks,
    track_pairs,
):
    rows = base_codes.shape[0] // BIN
    blocks = lax.axis_size("pos")
    size = lax.axis_size("heads")
    features, q_cols = w_query.shape
    entries, width = embed_table.shape
    groups = lax.axis_size("groups")
    key_t, value_t = w_key.T, w_value.T
    kv_cols = key_t.shape[0] + value_t.shape[0]
    kv_all = KDIM + VDIM
    half = entries // 2
    total = blocks * rows
    tracks_half = w_tracks.shape[2]
    chunks = 2 if width % (2 * LANES) == 0 else 1
    wide = width // chunks
    carry = LANES if chunks == 2 and wide % (2 * LANES) and wide > LANES else 0

    early, late = [(0, 0)], []
    for k in range(1, blocks, 2):
        early.append((k, min(k + 1, blocks - 1)))
        if k + 1 < blocks:
            late.append((k + 1, k))

    hbm = pltpu.HBM
    part_kv, *own_pieces, own_codes = call(
        functools.partial(stage_kernel, chunks),
        [shape((kv_cols, features // (2 * groups)), BF16)]
        + [shape((half, wide), BF16)] * chunks
        + [shape((rows, BIN), BF16)],
        [embed_table, key_t, value_t, base_codes.reshape(rows, BIN)],
        "stage",
        scratch=[pltpu.VMEM((rows, BIN), jnp.int32), pltpu.SemaphoreType.DMA((3 + chunks,))],
        spaces=[hbm] * 4,
    )
    table, key_own, value_own, query_own, gain, last_gain, cosine, sine = call(
        functools.partial(prepare_kernel, rows, early + late),
        [
            shape((entries, width), BF16),
            shape(key_t.shape, BF16),
            shape(value_t.shape, BF16),
            shape(w_query.shape, BF16),
            shape((1, features), F32),
            shape((1, features), F32),
            shape((total, KDIM), F32),
            shape((total, KDIM), F32),
        ],
        [embed_table, key_t, value_t, w_query, attn_gain, head_gain],
        "prepare",
        scratch=[
            pltpu.VMEM((features,), F32),
            pltpu.VMEM((features,), F32),
            pltpu.SemaphoreType.DMA((7,)),
        ],
        spaces=[hbm] * 6,
    )
    kv_parts, kv_steps, pieces, steps = [], [], [], []
    from_heads = [shifted(part_kv, "heads", step) for step in range(1, size)]
    if from_heads:
        from_heads[0], table = lax.optimization_barrier((from_heads[0], table))
    to_core = [shifted(here, "strand", 1) for here in from_heads]
    (out_here,) = call(
        fetch_kernel,
        [shape(w_out.shape, BF16)],
        [w_out],
        "fetch_out",
        scratch=[pltpu.SemaphoreType.DMA((2 * (q_cols // KDIM),))],
        spaces=[hbm],
    )
    raw = []
    for k, other in early[1:]:
        if k != other:
            pairs = [((p, s), ((p + k + s) % blocks, s)) for p in range(blocks) for s in range(2)]
            pairs = [(2 * p + s, 2 * q + t) for (p, s), (q, t) in pairs]
            raw.append(lax.ppermute(own_codes, ("pos", "strand"), pairs))
        else:
            if to_core:
                own_codes, to_core[0] = lax.optimization_barrier((own_codes, to_core[0]))
            raw.append(shifted(own_codes, "pos", k))
    if raw:
        raw[0], out_here = lax.optimization_barrier((raw[0], out_here))
    for step in range(1, size):
        for k in range(groups):
            here = from_heads[step - 1] if k == 0 else shifted(from_heads[step - 1], "groups", k)
            kv_parts += [here, to_core[step - 1] if k == 0 else shifted(here, "strand", 1)]
            kv_steps += [(step, k, 0), (step, k, 1)]
    for step in range(1, size):
        for i in range(chunks):
            here = shifted(own_pieces[i], "heads", step)
            if step == 1 and i == chunks - 1 and raw:
                here, *raw = lax.optimization_barrier((here, *raw))
            pieces.append((here, shifted(here, "strand", 1)))
            steps.append((step, i))

    swapped = [shifted(raw[i], "strand", 1) for i in range(len(late))]
    codes = [own_codes] + raw
    if len(steps) < 2:
        codes, swapped = codes + swapped, []

    def sums_of(count):
        return [shape((count, 1), F32), shape((count, kv_all), F32), shape((rows, q_cols), F32)]

    count = rows * len(codes)
    onehot, kv_t, own, *state = call(
        functools.partial(own_kernel, len(codes), kv_steps),
        [shape((count, entries), BF16), shape((kv_all, features), BF16), shape((rows, width), BF16)]
        + sums_of(count),
        codes + [table, key_own, value_own] + kv_parts + [query_own, gain],
        "own_features",
        scratch=[pltpu.VMEM((count, BIN), BF16)],
        flops=2 * count * width * (entries + kv_all),
        spare=8 * total * entries,
    )
    founds = []
    for (step, i), pair in zip(steps[:-1], pieces[:-1]):
        left = carry if step == size - 1 else 0
        operands = list(pair) + [onehot, kv_t, query_own, gain] + state
        outs = [shape((rows, wide - left), BF16)] + sums_of(total)
        scratch = [pltpu.VMEM((entries, wide - left), BF16)]
        if swapped:
            kernel = functools.partial(join_kernel, step, i, chunks, left, rows, len(swapped))
            operands += [table] + swapped
            outs = [shape((total, entries), BF16)] + outs
            scratch.append(pltpu.VMEM((rows * len(swapped), BIN), BF16))
        else:
            kernel = functools.partial(chunk_kernel, step, i, chunks, left, rows)
        results = call(
            kernel,
            outs,
            operands,
            "other_features",
            scratch=scratch,
            flops=2 * total * wide * (entries + kv_all),
            spare=8 * total * entries,
        )
        if swapped:
            onehot, *results = results
            swapped = []
        found, *state = results
        founds.append(found)
    o_cols = q_cols // KDIM * VDIM
    share_one, merged, inputs = call(
        functools.partial(attend_kernel, steps, chunks, carry),
        [
            shape((rows, features // 2), BF16),
            shape((rows, o_cols), BF16),
            shape((rows, features), BF16),
        ],
        (list(pieces[-2]) if carry else [])
        + list(pieces[-1])
        + [onehot, kv_t, query_own, gain]
        + state
        + [own, cosine, sine, out_here] + founds,
        "attend",
        scratch=[
            pltpu.VMEM((entries, wide + carry), BF16),
            pltpu.VMEM((total, 1), F32),
            pltpu.VMEM((total, kv_all), F32),
            pltpu.VMEM((rows, q_cols), F32),
            pltpu.VMEM((total, KDIM), BF16),
            pltpu.VMEM((total, VDIM), BF16),
        ],
        flops=2 * total * wide * (entries + kv_all) + 2 * total * q_cols * rows * 3,
        spare=8 * total * entries,
    )
    (share_two,) = call(
        second_kernel,
        [shape((rows, features // 2), BF16)],
        [merged, out_here],
        "second_share",
        flops=rows * o_cols * features,
    )
    ones = [share_one] + [shifted(share_one, "heads", k) for k in range(1, size)]
    twos = [share_two] + [shifted(share_two, "heads", k) for k in range(1, size)]
    weights, _ = lax.optimization_barrier((w_tracks, share_two))
    tracks = lax.optimization_barrier(weights.transpose(1, 0, 2))
    square, to_send, to_keep = call(
        functools.partial(first_tracks_kernel, size),
        [
            shape((rows, 1), F32),
            shape((rows, tracks_half), F32),
            shape((rows, tracks_half), F32),
        ],
        ones + [inputs, last_gain, tracks],
        "first_tracks",
        flops=2 * rows * features * tracks_half,
    )
    sent, gained, scale = call(
        functools.partial(send_kernel, size),
        [
            shape((rows, tracks_half), BF16),
            shape((rows, features // 2), BF16),
            shape((rows, 1), F32),
        ],
        twos + [inputs, last_gain, tracks, square, to_send],
        "sent_tracks",
        flops=rows * features * tracks_half,
    )
    received = shifted(sent, "strand", 1)
    pairs = track_pairs.reshape(1, tracks_half)
    (kept,) = call(
        keep_kernel,
        [shape((rows, tracks_half), BF16)],
        [gained, tracks, to_keep, scale, pairs],
        "kept_tracks",
        flops=rows * features * tracks_half,
    )
    (out,) = call(
        functools.partial(average_kernel, 4),
        [shape((rows, tracks_half), F32)],
        [kept, received, pairs],
        "average",
        scratch=[pltpu.VMEM((rows, tracks_half), F32), pltpu.SemaphoreType.DMA((4,))],
        out_space=hbm,
    )
    return out


def solution(mesh):
    placed = (
        P(("groups", "pos")),
        P(None, "heads"),
        P(),
        P(None, "heads"),
        P(None, "heads"),
        P(None, "heads"),
        P("heads", None),
        P(),
        P(None, None, "heads"),
        P(("strand", "heads")),
    )
    return jax.shard_map(
        body,
        mesh=mesh,
        in_specs=placed,
        out_specs=P(("groups", "pos"), ("strand", "heads")),
        check_vma=False,
    )
```

```python
import functools
import math

import jax
import jax.experimental.pallas as pl
import jax.experimental.pallas.tpu as pltpu
import jax.numpy as jnp
from jax import lax
from jax.sharding import PartitionSpec as P

KDIM = 128
VDIM = 192
BIN = 128
BASES = 4
LANES = 128
VMEM_LIMIT = 48 * 2**20
F32 = jnp.float32
BF16 = jnp.bfloat16


def shifted(value, axis, distance):
    size = lax.axis_size(axis)
    return lax.ppermute(value, axis, [(i, (i + distance) % size) for i in range(size)])


def matmul(a, b):
    return jnp.dot(a, b, preferred_element_type=F32)


def matmul_t(a, b):
    return lax.dot_general(a, b, (((1,), (1,)), ((), ())), preferred_element_type=F32)


def call(kernel, outs, operands, name, scratch=(), spaces=None, flops=0, spare=0, out_space=None):
    vmem = pl.BlockSpec(memory_space=pltpu.VMEM)
    spaces = spaces or [None] * len(operands)
    operands = [
        v if s is None else pltpu.with_memory_space_constraint(v, s) for v, s in zip(operands, spaces)
    ]
    specs = [vmem if s is None else pl.BlockSpec(memory_space=s) for s in spaces]
    held = [v for v, s in zip(operands, spaces) if s is None] + list(outs)
    held += [v for v in scratch if hasattr(v, "shape") and hasattr(v, "dtype") and v.memory_space == pltpu.VMEM]
    moved = sum(math.prod(v.shape[:-1]) * max(v.shape[-1], LANES) * jnp.dtype(v.dtype).itemsize for v in held)
    return pl.pallas_call(
        kernel,
        out_shape=list(outs),
        in_specs=specs,
        out_specs=[pl.BlockSpec(memory_space=out_space or pltpu.VMEM)] * len(outs),
        scratch_shapes=list(scratch),
        compiler_params=pltpu.CompilerParams(
            vmem_limit_bytes=min(VMEM_LIMIT, moved + moved // 4 + 6 * 2**20 + spare)
        ),
        cost_estimate=pl.CostEstimate(flops=flops, bytes_accessed=moved, transcendentals=0),
        name=name,
    )(*operands)


def shape(dims, dtype):
    return jax.ShapeDtypeStruct(tuple(dims), dtype)


def over_blocks(total, block, step):
    if total == block:
        step(0)
    else:

        def one(i, carry):
            step(pl.multiple_of(i * block, block))
            return carry

        lax.fori_loop(0, total // block, one, 0)


def stage_kernel(chunks, embed, key_t, value_t, codes, *refs):
    part_kv, pieces = refs[0], refs[1 : 1 + chunks]
    codes_out, raw_codes, sems = refs[1 + chunks :]
    strand = lax.axis_index("strand")
    part = strand * lax.axis_size("groups") + lax.axis_index("groups")
    key_cols, value_cols = key_t.shape[0], value_t.shape[0]
    kv_width = part_kv.shape[1]
    half, width = pieces[0].shape
    cols = pl.ds(pl.multiple_of(part * kv_width, LANES), kv_width)
    rows = pl.ds(pl.multiple_of(strand * half, half), half)
    copies = [
        pltpu.make_async_copy(key_t.at[:, cols], part_kv.at[pl.ds(0, key_cols)], sems.at[0]),
        pltpu.make_async_copy(value_t.at[:, cols], part_kv.at[pl.ds(key_cols, value_cols)], sems.at[1]),
    ]
    for i in range(chunks):
        source = embed.at[rows, pl.ds(i * width, width)]
        copies.append(pltpu.make_async_copy(source, pieces[i], sems.at[2 + i]))
    copies.append(pltpu.make_async_copy(codes, raw_codes, sems.at[2 + chunks]))
    for copy in copies:
        copy.start()
    copies[-1].wait()
    codes_out[...] = raw_codes[...].astype(F32).astype(BF16)
    for copy in copies[:-1]:
        copy.wait()


def prepare_kernel(rows, slots, embed, key_t, value_t, w_query, gain, last_gain, *refs):
    table, key_out, value_out, query_out, gain_out, last_out, cosine, sine = refs[:8]
    raw_gain, raw_last, sems = refs[8:]
    strand, pos = lax.axis_index("strand"), lax.axis_index("pos")
    half = embed.shape[0] // 2
    pairs = [(gain, raw_gain), (last_gain, raw_last)]
    for i in range(2):
        part = strand if i == 0 else 1 - strand
        source = embed.at[pl.ds(pl.multiple_of(part * half, half), half)]
        pairs.append((source, table.at[pl.ds(i * half, half)]))
    pairs += [(key_t, key_out), (value_t, value_out), (w_query, query_out)]
    copies = [pltpu.make_async_copy(a, b, sems.at[i]) for i, (a, b) in enumerate(pairs)]
    for copy in copies:
        copy.start()
    total = cosine.shape[0]
    blocks = total // rows
    lane = lax.broadcasted_iota(jnp.int32, (1, KDIM), 1)
    inverse = jnp.exp((lane % (KDIM // 2)).astype(F32) * (-math.log(10000.0) / (KDIM // 2)))
    sign = jnp.where(lane < KDIM // 2, -1.0, 1.0)
    offset = lax.broadcasted_iota(jnp.int32, (rows, KDIM), 0)
    for copy in copies[:2]:
        copy.wait()
    gain_out[...] = raw_gain[...].reshape(gain_out.shape)
    last_out[...] = raw_last[...].reshape(last_out.shape)

    for i, (forward, reverse) in enumerate(slots):
        behind = jnp.where(strand == 0, forward, reverse)
        place = lax.rem(pos + blocks - behind, blocks) * rows + offset
        angle = jnp.where(strand == 0, place, total - 1 - place).astype(F32) * inverse
        cosine[i * rows : (i + 1) * rows, :] = jnp.cos(angle)
        sine[i * rows : (i + 1) * rows, :] = jnp.sin(angle) * sign
    for copy in copies[2:]:
        copy.wait()


def fetch_kernel(w_out, out, sems):
    heads = w_out.shape[0] // VDIM
    rest = VDIM - LANES
    copies = []
    for head in range(heads):
        for begin, count, spot in ((0, LANES, head * LANES), (LANES, rest, heads * LANES + head * rest)):
            source = w_out.at[pl.ds(head * VDIM + begin, count)]
            copies.append(pltpu.make_async_copy(source, out.at[pl.ds(spot, count)], sems.at[len(copies)]))
    for copy in copies:
        copy.start()
    for copy in copies:
        copy.wait()


def block_of(count, rows):
    if count <= 4 * rows:
        return count
    return 4 * rows if count % (4 * rows) == 0 else rows


def mark(onehot, codes, first, entries, rows):
    strand = lax.axis_index("strand")
    half = entries // 2
    count = codes.shape[0]
    spot = lax.broadcasted_iota(jnp.int32, (BIN, entries), 1)
    owner = jnp.where(spot < half, strand, 1 - strand)
    entry = owner * half + spot % half
    entry = jnp.where(strand == 0, entry, entries - 1 - entry)
    place = lax.broadcasted_iota(jnp.int32, (BIN, entries), 0)
    spread = jnp.where(place == entry // BASES, 1.0, 0.0).astype(BF16)
    wanted = (entry[:1] % BASES).astype(F32)
    block = block_of(count, rows)

    def step(begin):
        found = matmul(codes[pl.ds(begin, block), :], spread) == wanted
        onehot[pl.ds(first + begin, block), :] = jnp.where(found, 1.0, 0.0).astype(BF16)

    over_blocks(count, block, step)


def absorb(onehot, span, table, rows, start, width, weights, before, after):
    kv_t, w_query, gain = weights
    first, count = span
    block = block_of(count, rows)
    cols = pl.ds(pl.multiple_of(start, LANES), width)

    def some(here):
        found = matmul(onehot[here, :], table[...]).astype(BF16)
        floats = found.astype(F32)
        return found, floats, (floats * gain[:, cols]).astype(BF16)

    def step(begin):
        here = pl.ds(first + begin, block)
        found, floats, gained = some(here)
        square = jnp.sum(floats * floats, axis=1, keepdims=True)
        kv = matmul_t(gained, kv_t[:, cols])
        after[0][here, :] = square if before is None else before[0][here, :] + square
        after[1][here, :] = kv if before is None else before[1][here, :] + kv
        return found, gained

    if count == block:
        found, gained = step(0)
        found, gained = found[:rows], gained[:rows]
    else:
        over_blocks(count, block, lambda begin: step(begin) and None)
        found, _, gained = some(pl.ds(0, rows))
    if first:
        return None
    query = matmul(gained, w_query[cols, :])
    after[2][...] = query if before is None else before[2][...] + query
    return found


def own_kernel(blocks, kv_steps, *refs):
    codes = refs[:blocks]
    table, key_t, value_t = refs[blocks : blocks + 3]
    parts = refs[blocks + 3 : blocks + 3 + len(kv_steps)]
    w_query, gain, onehot, kv_t, own, square, kv_sum, q_sum, all_codes = refs[blocks + 3 + len(kv_steps) :]
    strand, mine, group = lax.axis_index("strand"), lax.axis_index("heads"), lax.axis_index("groups")
    size, groups = lax.axis_size("heads"), lax.axis_size("groups")
    key_cols, value_cols = key_t.shape[0], value_t.shape[0]
    entries, width = table.shape
    rows = codes[0].shape[0]
    for i in range(blocks):
        all_codes[i * rows : (i + 1) * rows, :] = codes[i][...]

    def kv_rows(owner):
        key_rows = pl.ds(pl.multiple_of(owner * key_cols, 16), key_cols)
        return key_rows, pl.ds(pl.multiple_of(KDIM + owner * value_cols, 16), value_cols)

    key_rows, value_rows = kv_rows(mine)
    kv_t[key_rows, :] = key_t[...]
    kv_t[value_rows, :] = value_t[...]
    for piece, (step, group_step, core_step) in zip(parts, kv_steps):
        key_rows, value_rows = kv_rows(lax.rem(mine + size - step, size))
        core = strand if core_step == 0 else 1 - strand
        part = core * groups + lax.rem(group + groups - group_step, groups)
        cols = pl.ds(pl.multiple_of(part * piece.shape[1], LANES), piece.shape[1])
        kv_t[key_rows, cols] = piece[:key_cols, :]
        kv_t[value_rows, cols] = piece[key_cols:, :]
    mark(onehot, all_codes, 0, entries, rows)
    weights = (kv_t, w_query, gain)
    span = (0, blocks * rows)
    own[...] = absorb(onehot, span, table, rows, mine * width, width, weights, None, (square, kv_sum, q_sum))


def chunk_start(step, index, chunks, width):
    size = lax.axis_size("heads")
    owner = lax.rem(lax.axis_index("heads") + size - step, size)
    return (owner * chunks + index) * width


def join_kernel(step, index, chunks, carry, rows, late, *refs):
    mine, theirs, onehot_in, kv_t, w_query, gain, square_in, kv_in, q_in, own_table = refs[:10]
    codes = refs[10 : 10 + late]
    onehot, found, square, kv_sum, q_sum, table, all_codes = refs[10 + late :]
    half, width = mine.shape
    own_width = own_table.shape[1]
    early = onehot_in.shape[0]
    weights = (kv_t, w_query, gain)
    for i in range(late):
        all_codes[i * rows : (i + 1) * rows, :] = codes[i][...]
    mark(onehot, all_codes, early, own_table.shape[0], rows)
    onehot[:early, :] = onehot_in[...]
    square[:early, :] = square_in[...]
    kv_sum[:early, :] = kv_in[...]
    span = (early, late * rows)
    begin = lax.axis_index("heads") * own_width
    absorb(onehot, span, own_table, rows, begin, own_width, weights, None, (square, kv_sum, None))
    taken = width - carry
    table[:half, :] = mine[:, :taken]
    table[half:, :] = theirs[:, :taken]
    begin = chunk_start(step, index, chunks, width)
    span = (0, early + late * rows)
    sums = (square, kv_sum, q_sum)
    found[...] = absorb(onehot, span, table, rows, begin, taken, weights, (square, kv_sum, q_in), sums)


def chunk_kernel(step, index, chunks, carry, rows, *refs):
    mine, theirs, onehot, kv_t, w_query, gain, square, kv_sum, q_sum = refs[:9]
    found, square_out, kv_out, q_out, table = refs[9:]
    half, width = mine.shape
    taken = width - carry
    table[:half, :] = mine[:, :taken]
    table[half:, :] = theirs[:, :taken]
    found[...] = absorb(
        onehot,
        (0, onehot.shape[0]),
        table,
        rows,
        chunk_start(step, index, chunks, width),
        taken,
        (kv_t, w_query, gain),
        (square, kv_sum, q_sum),
        (square_out, kv_out, q_out),
    )


def turn(values, cosine, sine):
    floats = values.astype(BF16).astype(F32)
    return (floats * cosine + pltpu.roll(floats, KDIM // 2, 1) * sine).astype(BF16)


def attend_kernel(steps, chunks, carry, *refs):
    if carry:
        earlier, refs = refs[:2], refs[2:]
    mine, theirs, onehot, kv_t, w_query, gain, square, kv_sum, q_sum = refs[:9]
    cosine, sine, out = refs[9:12]
    share, merged, last = refs[12:15]
    table, squares, sums, queries, keys, values = refs[15:]
    half, width = mine.shape
    rows, features = merged.shape[0], w_query.shape[0]
    total = onehot.shape[0]
    block = block_of(total, rows)
    if carry:
        table[:half, :carry] = earlier[0][:, width - carry :]
        table[half:, :carry] = earlier[1][:, width - carry :]
    table[:half, carry:] = mine[...]
    table[half:, carry:] = theirs[...]
    start = chunk_start(*steps[-1], chunks, width) - carry
    span, weights = (0, total), (kv_t, w_query, gain)
    before, after = (square, kv_sum, q_sum), (squares, sums, queries)
    last[...] = absorb(onehot, span, table, rows, start, width + carry, weights, before, after)

    def finish(begin):
        here = pl.ds(begin, block)
        scaled = sums[here, :] * lax.rsqrt(squares[here, :] / features + 1e-06)
        keys[here, :] = turn(scaled[:, :KDIM], cosine[here, :], sine[here, :])
        values[here, :] = scaled[:, KDIM:].astype(BF16)

    over_blocks(total, block, finish)
    scaled = queries[...] * lax.rsqrt(squares[:rows, :] / features + 1e-06)
    heads = queries.shape[1] // KDIM
    for head in range(heads):
        query = turn(scaled[:, head * KDIM : (head + 1) * KDIM], cosine[:rows, :], sine[:rows, :])
        scores = matmul_t(query, keys[...]) * KDIM ** (-0.5)
        weights = jnp.exp(scores - jnp.max(scores, axis=1, keepdims=True))
        weight_sum = jnp.sum(weights, axis=1, keepdims=True)
        found = (matmul(weights.astype(BF16), values[...]) / weight_sum).astype(BF16)
        merged[:, head * LANES : (head + 1) * LANES] = found[:, :LANES]
        spot = heads * LANES + head * (VDIM - LANES)
        merged[:, spot : spot + VDIM - LANES] = found[:, LANES:]
    share[...] = matmul(merged[...], out[:, : share.shape[1]]).astype(BF16)


def second_kernel(spots, full, *refs):
    merged, out, own = refs[:3]
    founds, (share, inputs) = refs[3:-2], refs[-2:]
    share[...] = matmul(merged[...], out[:, share.shape[1] :]).astype(BF16)
    inputs[:, pl.ds(pl.multiple_of(lax.axis_index("heads") * full, LANES), full)] = own[...]
    for found, spot in zip(founds, spots):
        begin = pl.multiple_of(chunk_start(spot[0], 0, 1, full) + spot[1], LANES)
        inputs[:, pl.ds(begin, found.shape[1])] = found[...]


def gather_hidden(shares, inputs, gain, chunk):
    width = shares[0].shape[1]
    cols = slice(chunk * width, (chunk + 1) * width)
    total = shares[0][...].astype(F32)
    for other in shares[1:]:
        total = total + other[...].astype(F32)
    hidden = (inputs[:, cols].astype(F32) + total).astype(BF16).astype(F32)
    return jnp.sum(hidden * hidden, axis=1, keepdims=True), (hidden * gain[:, cols]).astype(BF16)


def soft(logits):
    return jnp.maximum(logits, 0.0) + jnp.log1p(jnp.exp(-jnp.abs(logits)))


def first_tracks_kernel(size, *refs):
    shares = refs[:size]
    inputs, gain, tracks, square, to_send, to_keep = refs[size:]
    strand = lax.axis_index("strand")
    width = shares[0].shape[1]
    square[...], gained = gather_hidden(shares, inputs, gain, 0)
    to_send[...] = matmul(gained, tracks[1 - strand, :width, :])
    to_keep[...] = matmul(gained, tracks[strand, :width, :])


def send_kernel(size, *refs):
    shares = refs[:size]
    inputs, gain, tracks, square, to_send, sent, gained_out, scale_out = refs[size:]
    strand = lax.axis_index("strand")
    width = shares[0].shape[1]
    total, gained = gather_hidden(shares, inputs, gain, 1)
    scale = lax.rsqrt((square[...] + total) / (2 * width) + 1e-06)
    logits = to_send[...] + matmul(gained, tracks[1 - strand, width:, :])
    sent[...] = soft(logits * scale).astype(BF16)
    gained_out[...] = gained
    scale_out[...] = scale


def swap_pairs(values, pairs):
    even = lax.broadcasted_iota(jnp.int32, (1, LANES), 1) % 2 == 0
    parts = []
    for begin in range(0, values.shape[1], LANES):
        part = values[:, begin : begin + LANES]
        swapped = (pairs[:, begin : begin + LANES] % 2 == 0) != even
        partner = jnp.where(even, pltpu.roll(part, LANES - 1, 1), pltpu.roll(part, 1, 1))
        parts.append(jnp.where(swapped, partner, part))
    return jnp.concatenate(parts, axis=1)


def keep_kernel(gained, tracks, to_keep, scale, pairs, kept):
    strand = lax.axis_index("strand")
    width = gained.shape[1]
    logits = to_keep[...] + matmul(gained[...], tracks[strand, width:, :])
    found = soft(logits * scale[...]).astype(BF16).astype(F32)
    kept[...] = jnp.where(strand == 0, found, swap_pairs(found, pairs)).astype(BF16)


def average_kernel(parts, kept, received, pairs, out, stage, sems):
    strand = lax.axis_index("strand")
    rows = kept.shape[0] // parts
    copies = []
    for i in range(parts):
        here = slice(i * rows, (i + 1) * rows)
        theirs = received[here, :].astype(F32)
        theirs = jnp.where(strand == 0, swap_pairs(theirs, pairs), theirs)
        stage[here, :] = 0.5 * (kept[here, :].astype(F32) + theirs)
        copies.append(pltpu.make_async_copy(stage.at[here], out.at[here], sems.at[i]))
        copies[-1].start()
    for copy in copies:
        copy.wait()


def body(
    base_codes,
    embed_table,
    attn_gain,
    w_query,
    w_key,
    w_value,
    w_out,
    head_gain,
    w_tracks,
    track_pairs,
):
    rows = base_codes.shape[0] // BIN
    blocks = lax.axis_size("pos")
    size = lax.axis_size("heads")
    features, q_cols = w_query.shape
    entries, width = embed_table.shape
    groups = lax.axis_size("groups")
    key_t, value_t = w_key.T, w_value.T
    kv_cols = key_t.shape[0] + value_t.shape[0]
    kv_all = KDIM + VDIM
    half = entries // 2
    total = blocks * rows
    tracks_half = w_tracks.shape[2]
    chunks = 2 if width % (2 * LANES) == 0 else 1
    wide = width // chunks
    carry = LANES if chunks == 2 and wide % (2 * LANES) and wide > LANES else 0

    early, late = [(0, 0)], []
    for k in range(1, blocks, 2):
        early.append((k, min(k + 1, blocks - 1)))
        if k + 1 < blocks:
            late.append((k + 1, k))

    hbm = pltpu.HBM
    part_kv, *own_pieces, own_codes = call(
        functools.partial(stage_kernel, chunks),
        [shape((kv_cols, features // (2 * groups)), BF16)]
        + [shape((half, wide), BF16)] * chunks
        + [shape((rows, BIN), BF16)],
        [embed_table, key_t, value_t, base_codes.reshape(rows, BIN)],
        "stage",
        scratch=[pltpu.VMEM((rows, BIN), jnp.int32), pltpu.SemaphoreType.DMA((3 + chunks,))],
        spaces=[hbm] * 4,
    )
    table, key_own, value_own, query_own, gain, last_gain, cosine, sine = call(
        functools.partial(prepare_kernel, rows, early + late),
        [
            shape((entries, width), BF16),
            shape(key_t.shape, BF16),
            shape(value_t.shape, BF16),
            shape(w_query.shape, BF16),
            shape((1, features), F32),
            shape((1, features), F32),
            shape((total, KDIM), F32),
            shape((total, KDIM), F32),
        ],
        [embed_table, key_t, value_t, w_query, attn_gain, head_gain],
        "prepare",
        scratch=[
            pltpu.VMEM((features,), F32),
            pltpu.VMEM((features,), F32),
            pltpu.SemaphoreType.DMA((7,)),
        ],
        spaces=[hbm] * 6,
    )
    kv_parts, kv_steps, pieces, steps = [], [], [], []
    from_heads = [shifted(part_kv, "heads", step) for step in range(1, size)]
    if from_heads:
        from_heads[0], table = lax.optimization_barrier((from_heads[0], table))
    to_core = [shifted(here, "strand", 1) for here in from_heads]
    (out_here,) = call(
        fetch_kernel,
        [shape(w_out.shape, BF16)],
        [w_out],
        "fetch_out",
        scratch=[pltpu.SemaphoreType.DMA((2 * (q_cols // KDIM),))],
        spaces=[hbm],
    )
    raw = []
    for k, other in early[1:]:
        if k != other:
            pairs = [((p, s), ((p + k + s) % blocks, s)) for p in range(blocks) for s in range(2)]
            pairs = [(2 * p + s, 2 * q + t) for (p, s), (q, t) in pairs]
            raw.append(lax.ppermute(own_codes, ("pos", "strand"), pairs))
        else:
            if to_core:
                own_codes, to_core[0] = lax.optimization_barrier((own_codes, to_core[0]))
            raw.append(shifted(own_codes, "pos", k))
    if raw:
        raw[0], out_here = lax.optimization_barrier((raw[0], out_here))
    for step in range(1, size):
        for k in range(groups):
            here = from_heads[step - 1] if k == 0 else shifted(from_heads[step - 1], "groups", k)
            kv_parts += [here, to_core[step - 1] if k == 0 else shifted(here, "strand", 1)]
            kv_steps += [(step, k, 0), (step, k, 1)]
    for step in range(1, size):
        for i in range(chunks):
            here = shifted(own_pieces[i], "heads", step)
            if step == 1 and i == chunks - 1 and raw:
                here, *raw = lax.optimization_barrier((here, *raw))
            pieces.append((here, shifted(here, "strand", 1)))
            steps.append((step, i))

    swapped = [shifted(raw[i], "strand", 1) for i in range(len(late))]
    codes = [own_codes] + raw
    if len(steps) < 2:
        codes, swapped = codes + swapped, []

    def sums_of(count):
        return [shape((count, 1), F32), shape((count, kv_all), F32), shape((rows, q_cols), F32)]

    count = rows * len(codes)
    onehot, kv_t, own, *state = call(
        functools.partial(own_kernel, len(codes), kv_steps),
        [shape((count, entries), BF16), shape((kv_all, features), BF16), shape((rows, width), BF16)]
        + sums_of(count),
        codes + [table, key_own, value_own] + kv_parts + [query_own, gain],
        "own_features",
        scratch=[pltpu.VMEM((count, BIN), BF16)],
        flops=2 * count * width * (entries + kv_all),
        spare=8 * total * entries,
    )
    founds = []
    for (step, i), pair in zip(steps[:-1], pieces[:-1]):
        left = carry if step == size - 1 else 0
        operands = list(pair) + [onehot, kv_t, query_own, gain] + state
        outs = [shape((rows, wide - left), BF16)] + sums_of(total)
        scratch = [pltpu.VMEM((entries, wide - left), BF16)]
        if swapped:
            kernel = functools.partial(join_kernel, step, i, chunks, left, rows, len(swapped))
            operands += [table] + swapped
            outs = [shape((total, entries), BF16)] + outs
            scratch.append(pltpu.VMEM((rows * len(swapped), BIN), BF16))
        else:
            kernel = functools.partial(chunk_kernel, step, i, chunks, left, rows)
        results = call(
            kernel,
            outs,
            operands,
            "other_features",
            scratch=scratch,
            flops=2 * total * wide * (entries + kv_all),
            spare=8 * total * entries,
        )
        if swapped:
            onehot, *results = results
            swapped = []
        found, *state = results
        founds.append(found)
    o_cols = q_cols // KDIM * VDIM
    share_one, merged, last = call(
        functools.partial(attend_kernel, steps, chunks, carry),
        [
            shape((rows, features // 2), BF16),
            shape((rows, o_cols), BF16),
            shape((rows, wide + carry), BF16),
        ],
        (list(pieces[-2]) if carry else [])
        + list(pieces[-1])
        + [onehot, kv_t, query_own, gain]
        + state
        + [cosine, sine, out_here],
        "attend",
        scratch=[
            pltpu.VMEM((entries, wide + carry), BF16),
            pltpu.VMEM((total, 1), F32),
            pltpu.VMEM((total, kv_all), F32),
            pltpu.VMEM((rows, q_cols), F32),
            pltpu.VMEM((total, KDIM), BF16),
            pltpu.VMEM((total, VDIM), BF16),
        ],
        flops=2 * total * wide * (entries + kv_all) + 2 * total * q_cols * rows * 3,
        spare=8 * total * entries,
    )
    spots = [(step, i * wide) for step, i in steps]
    spots[-1] = (spots[-1][0], spots[-1][1] - carry)
    share_two, inputs = call(
        functools.partial(second_kernel, spots, width),
        [shape((rows, features // 2), BF16), shape((rows, features), BF16)],
        [merged, out_here, own] + founds + [last],
        "second_share",
        flops=rows * o_cols * features,
    )
    ones = [share_one] + [shifted(share_one, "heads", k) for k in range(1, size)]
    twos = [share_two] + [shifted(share_two, "heads", k) for k in range(1, size)]
    weights, _ = lax.optimization_barrier((w_tracks, share_two))
    tracks = lax.optimization_barrier(weights.transpose(1, 0, 2))
    square, to_send, to_keep = call(
        functools.partial(first_tracks_kernel, size),
        [
            shape((rows, 1), F32),
            shape((rows, tracks_half), F32),
            shape((rows, tracks_half), F32),
        ],
        ones + [inputs, last_gain, tracks],
        "first_tracks",
        flops=2 * rows * features * tracks_half,
    )
    sent, gained, scale = call(
        functools.partial(send_kernel, size),
        [
            shape((rows, tracks_half), BF16),
            shape((rows, features // 2), BF16),
            shape((rows, 1), F32),
        ],
        twos + [inputs, last_gain, tracks, square, to_send],
        "sent_tracks",
        flops=rows * features * tracks_half,
    )
    received = shifted(sent, "strand", 1)
    pairs = track_pairs.reshape(1, tracks_half)
    (kept,) = call(
        keep_kernel,
        [shape((rows, tracks_half), BF16)],
        [gained, tracks, to_keep, scale, pairs],
        "kept_tracks",
        flops=rows * features * tracks_half,
    )
    (out,) = call(
        functools.partial(average_kernel, 4),
        [shape((rows, tracks_half), F32)],
        [kept, received, pairs],
        "average",
        scratch=[pltpu.VMEM((rows, tracks_half), F32), pltpu.SemaphoreType.DMA((4,))],
        out_space=hbm,
    )
    return out


def solution(mesh):
    placed = (
        P(("groups", "pos")),
        P(None, "heads"),
        P(),
        P(None, "heads"),
        P(None, "heads"),
        P(None, "heads"),
        P("heads", None),
        P(),
        P(None, None, "heads"),
        P(("strand", "heads")),
    )
    return jax.shard_map(
        body,
        mesh=mesh,
        in_specs=placed,
        out_specs=P(("groups", "pos"), ("strand", "heads")),
        check_vma=False,
    )
```

```python
import functools
import math

import jax
import jax.experimental.pallas as pl
import jax.experimental.pallas.tpu as pltpu
import jax.numpy as jnp
from jax import lax
from jax.sharding import PartitionSpec as P

KDIM = 128
VDIM = 192
BIN = 128
BASES = 4
LANES = 128
VMEM_LIMIT = 48 * 2**20
F32 = jnp.float32
BF16 = jnp.bfloat16


def shifted(value, axis, distance):
    size = lax.axis_size(axis)
    return lax.ppermute(value, axis, [(i, (i + distance) % size) for i in range(size)])


def matmul(a, b):
    return jnp.dot(a, b, preferred_element_type=F32)


def matmul_t(a, b):
    return lax.dot_general(a, b, (((1,), (1,)), ((), ())), preferred_element_type=F32)


def call(kernel, outs, operands, name, scratch=(), spaces=None, flops=0, spare=0, out_space=None):
    vmem = pl.BlockSpec(memory_space=pltpu.VMEM)
    spaces = spaces or [None] * len(operands)
    operands = [
        v if s is None else pltpu.with_memory_space_constraint(v, s) for v, s in zip(operands, spaces)
    ]
    specs = [vmem if s is None else pl.BlockSpec(memory_space=s) for s in spaces]
    held = [v for v, s in zip(operands, spaces) if s is None] + list(outs)
    held += [v for v in scratch if hasattr(v, "shape") and hasattr(v, "dtype") and v.memory_space == pltpu.VMEM]
    moved = sum(math.prod(v.shape[:-1]) * max(v.shape[-1], LANES) * jnp.dtype(v.dtype).itemsize for v in held)
    return pl.pallas_call(
        kernel,
        out_shape=list(outs),
        in_specs=specs,
        out_specs=[pl.BlockSpec(memory_space=out_space or pltpu.VMEM)] * len(outs),
        scratch_shapes=list(scratch),
        compiler_params=pltpu.CompilerParams(
            vmem_limit_bytes=min(VMEM_LIMIT, moved + moved // 4 + 6 * 2**20 + spare)
        ),
        cost_estimate=pl.CostEstimate(flops=flops, bytes_accessed=moved, transcendentals=0),
        name=name,
    )(*operands)


def shape(dims, dtype):
    return jax.ShapeDtypeStruct(tuple(dims), dtype)


def over_blocks(total, block, step):
    if total == block:
        step(0)
    else:

        def one(i, carry):
            step(pl.multiple_of(i * block, block))
            return carry

        lax.fori_loop(0, total // block, one, 0)


def stage_kernel(chunks, embed, key_t, value_t, codes, *refs):
    part_kv, pieces = refs[0], refs[1 : 1 + chunks]
    codes_out, raw_codes, sems = refs[1 + chunks :]
    strand = lax.axis_index("strand")
    part = strand * lax.axis_size("groups") + lax.axis_index("groups")
    key_cols, value_cols = key_t.shape[0], value_t.shape[0]
    kv_width = part_kv.shape[1]
    half, width = pieces[0].shape
    cols = pl.ds(pl.multiple_of(part * kv_width, LANES), kv_width)
    rows = pl.ds(pl.multiple_of(strand * half, half), half)
    copies = [
        pltpu.make_async_copy(key_t.at[:, cols], part_kv.at[pl.ds(0, key_cols)], sems.at[0]),
        pltpu.make_async_copy(value_t.at[:, cols], part_kv.at[pl.ds(key_cols, value_cols)], sems.at[1]),
    ]
    for i in range(chunks):
        source = embed.at[rows, pl.ds(i * width, width)]
        copies.append(pltpu.make_async_copy(source, pieces[i], sems.at[2 + i]))
    copies.append(pltpu.make_async_copy(codes, raw_codes, sems.at[2 + chunks]))
    for copy in copies:
        copy.start()
    copies[-1].wait()
    codes_out[...] = raw_codes[...].astype(F32).astype(BF16)
    for copy in copies[:-1]:
        copy.wait()


def prepare_kernel(rows, slots, embed, key_t, value_t, w_query, gain, last_gain, *refs):
    table, key_out, value_out, query_out, gain_out, last_out, cosine, sine = refs[:8]
    raw_gain, raw_last, sems = refs[8:]
    strand, pos = lax.axis_index("strand"), lax.axis_index("pos")
    half = embed.shape[0] // 2
    pairs = [(gain, raw_gain), (last_gain, raw_last)]
    for i in range(2):
        part = strand if i == 0 else 1 - strand
        source = embed.at[pl.ds(pl.multiple_of(part * half, half), half)]
        pairs.append((source, table.at[pl.ds(i * half, half)]))
    pairs += [(key_t, key_out), (value_t, value_out), (w_query, query_out)]
    copies = [pltpu.make_async_copy(a, b, sems.at[i]) for i, (a, b) in enumerate(pairs)]
    for copy in copies:
        copy.start()
    total = cosine.shape[0]
    blocks = total // rows
    lane = lax.broadcasted_iota(jnp.int32, (1, KDIM), 1)
    inverse = jnp.exp((lane % (KDIM // 2)).astype(F32) * (-math.log(10000.0) / (KDIM // 2)))
    sign = jnp.where(lane < KDIM // 2, -1.0, 1.0)
    offset = lax.broadcasted_iota(jnp.int32, (rows, KDIM), 0)
    for copy in copies[:2]:
        copy.wait()
    gain_out[...] = raw_gain[...].reshape(gain_out.shape)
    last_out[...] = raw_last[...].reshape(last_out.shape)

    for i, (forward, reverse) in enumerate(slots):
        behind = jnp.where(strand == 0, forward, reverse)
        place = lax.rem(pos + blocks - behind, blocks) * rows + offset
        angle = jnp.where(strand == 0, place, total - 1 - place).astype(F32) * inverse
        cosine[i * rows : (i + 1) * rows, :] = jnp.cos(angle)
        sine[i * rows : (i + 1) * rows, :] = jnp.sin(angle) * sign
    for copy in copies[2:]:
        copy.wait()


def fetch_kernel(w_out, out, sems):
    heads = w_out.shape[0] // VDIM
    rest = VDIM - LANES
    copies = []
    for head in range(heads):
        for begin, count, spot in ((0, LANES, head * LANES), (LANES, rest, heads * LANES + head * rest)):
            source = w_out.at[pl.ds(head * VDIM + begin, count)]
            copies.append(pltpu.make_async_copy(source, out.at[pl.ds(spot, count)], sems.at[len(copies)]))
    for copy in copies:
        copy.start()
    for copy in copies:
        copy.wait()


def block_of(count, rows):
    if count <= 4 * rows:
        return count
    return 4 * rows if count % (4 * rows) == 0 else rows


def mark(onehot, codes, first, entries, rows):
    strand = lax.axis_index("strand")
    half = entries // 2
    count = codes.shape[0]
    spot = lax.broadcasted_iota(jnp.int32, (BIN, entries), 1)
    owner = jnp.where(spot < half, strand, 1 - strand)
    entry = owner * half + spot % half
    entry = jnp.where(strand == 0, entry, entries - 1 - entry)
    place = lax.broadcasted_iota(jnp.int32, (BIN, entries), 0)
    spread = jnp.where(place == entry // BASES, 1.0, 0.0).astype(BF16)
    wanted = (entry[:1] % BASES).astype(F32)
    block = block_of(count, rows)

    def step(begin):
        found = matmul(codes[pl.ds(begin, block), :], spread) == wanted
        onehot[pl.ds(first + begin, block), :] = jnp.where(found, 1.0, 0.0).astype(BF16)

    over_blocks(count, block, step)


def absorb(onehot, span, table, rows, start, width, weights, before, after):
    kv_t, w_query, gain = weights
    first, count = span
    block = block_of(count, rows)
    cols = pl.ds(pl.multiple_of(start, LANES), width)

    def some(here):
        found = matmul(onehot[here, :], table[...]).astype(BF16)
        floats = found.astype(F32)
        return found, floats, (floats * gain[:, cols]).astype(BF16)

    def step(begin):
        here = pl.ds(first + begin, block)
        found, floats, gained = some(here)
        square = jnp.sum(floats * floats, axis=1, keepdims=True)
        kv = matmul_t(gained, kv_t[:, cols])
        after[0][here, :] = square if before is None else before[0][here, :] + square
        after[1][here, :] = kv if before is None else before[1][here, :] + kv
        return found, gained

    if count == block:
        found, gained = step(0)
        found, gained = found[:rows], gained[:rows]
    else:
        over_blocks(count, block, lambda begin: step(begin) and None)
        found, _, gained = some(pl.ds(0, rows))
    if first:
        return None
    query = matmul(gained, w_query[cols, :])
    after[2][...] = query if before is None else before[2][...] + query
    return found


def own_kernel(blocks, kv_steps, *refs):
    codes = refs[:blocks]
    table, key_t, value_t = refs[blocks : blocks + 3]
    parts = refs[blocks + 3 : blocks + 3 + len(kv_steps)]
    w_query, gain, onehot, kv_t, own, square, kv_sum, q_sum, all_codes = refs[blocks + 3 + len(kv_steps) :]
    strand, mine, group = lax.axis_index("strand"), lax.axis_index("heads"), lax.axis_index("groups")
    size, groups = lax.axis_size("heads"), lax.axis_size("groups")
    key_cols, value_cols = key_t.shape[0], value_t.shape[0]
    entries, width = table.shape
    rows = codes[0].shape[0]
    for i in range(blocks):
        all_codes[i * rows : (i + 1) * rows, :] = codes[i][...]

    def kv_rows(owner):
        key_rows = pl.ds(pl.multiple_of(owner * key_cols, 16), key_cols)
        return key_rows, pl.ds(pl.multiple_of(KDIM + owner * value_cols, 16), value_cols)

    key_rows, value_rows = kv_rows(mine)
    kv_t[key_rows, :] = key_t[...]
    kv_t[value_rows, :] = value_t[...]
    for piece, (step, group_step, core_step) in zip(parts, kv_steps):
        key_rows, value_rows = kv_rows(lax.rem(mine + size - step, size))
        core = strand if core_step == 0 else 1 - strand
        part = core * groups + lax.rem(group + groups - group_step, groups)
        cols = pl.ds(pl.multiple_of(part * piece.shape[1], LANES), piece.shape[1])
        kv_t[key_rows, cols] = piece[:key_cols, :]
        kv_t[value_rows, cols] = piece[key_cols:, :]
    mark(onehot, all_codes, 0, entries, rows)
    weights = (kv_t, w_query, gain)
    span = (0, blocks * rows)
    own[...] = absorb(onehot, span, table, rows, mine * width, width, weights, None, (square, kv_sum, q_sum))


def chunk_start(step, index, chunks, width):
    size = lax.axis_size("heads")
    owner = lax.rem(lax.axis_index("heads") + size - step, size)
    return (owner * chunks + index) * width


def join_kernel(step, index, chunks, carry, rows, late, *refs):
    mine, theirs, onehot_in, kv_t, w_query, gain, square_in, kv_in, q_in, own_table = refs[:10]
    codes = refs[10 : 10 + late]
    onehot, found, square, kv_sum, q_sum, table, all_codes = refs[10 + late :]
    half, width = mine.shape
    own_width = own_table.shape[1]
    early = onehot_in.shape[0]
    weights = (kv_t, w_query, gain)
    for i in range(late):
        all_codes[i * rows : (i + 1) * rows, :] = codes[i][...]
    mark(onehot, all_codes, early, own_table.shape[0], rows)
    onehot[:early, :] = onehot_in[...]
    square[:early, :] = square_in[...]
    kv_sum[:early, :] = kv_in[...]
    span = (early, late * rows)
    begin = lax.axis_index("heads") * own_width
    absorb(onehot, span, own_table, rows, begin, own_width, weights, None, (square, kv_sum, None))
    taken = width - carry
    table[:half, :] = mine[:, :taken]
    table[half:, :] = theirs[:, :taken]
    begin = chunk_start(step, index, chunks, width)
    span = (0, early + late * rows)
    sums = (square, kv_sum, q_sum)
    found[...] = absorb(onehot, span, table, rows, begin, taken, weights, (square, kv_sum, q_in), sums)


def chunk_kernel(step, index, chunks, carry, rows, *refs):
    mine, theirs, onehot, kv_t, w_query, gain, square, kv_sum, q_sum = refs[:9]
    found, square_out, kv_out, q_out, table = refs[9:]
    half, width = mine.shape
    taken = width - carry
    table[:half, :] = mine[:, :taken]
    table[half:, :] = theirs[:, :taken]
    found[...] = absorb(
        onehot,
        (0, onehot.shape[0]),
        table,
        rows,
        chunk_start(step, index, chunks, width),
        taken,
        (kv_t, w_query, gain),
        (square, kv_sum, q_sum),
        (square_out, kv_out, q_out),
    )


def turn(values, cosine, sine):
    floats = values.astype(BF16).astype(F32)
    return (floats * cosine + pltpu.roll(floats, KDIM // 2, 1) * sine).astype(BF16)


def attend_kernel(steps, chunks, carry, *refs):
    if carry:
        earlier, refs = refs[:2], refs[2:]
    mine, theirs, onehot, kv_t, w_query, gain, square, kv_sum, q_sum = refs[:9]
    cosine, sine, out = refs[9:12]
    share, merged, last = refs[12:15]
    table, squares, sums, queries, keys, values = refs[15:]
    half, width = mine.shape
    rows, features = merged.shape[0], w_query.shape[0]
    total = onehot.shape[0]
    block = block_of(total, rows)
    if carry:
        table[:half, :carry] = earlier[0][:, width - carry :]
        table[half:, :carry] = earlier[1][:, width - carry :]
    table[:half, carry:] = mine[...]
    table[half:, carry:] = theirs[...]
    start = chunk_start(*steps[-1], chunks, width) - carry
    span, weights = (0, total), (kv_t, w_query, gain)
    before, after = (square, kv_sum, q_sum), (squares, sums, queries)
    last[...] = absorb(onehot, span, table, rows, start, width + carry, weights, before, after)

    def finish(begin):
        here = pl.ds(begin, block)
        scaled = sums[here, :] * lax.rsqrt(squares[here, :] / features + 1e-06)
        keys[here, :] = turn(scaled[:, :KDIM], cosine[here, :], sine[here, :])
        values[here, :] = scaled[:, KDIM:].astype(BF16)

    over_blocks(total, block, finish)
    scaled = queries[...] * lax.rsqrt(squares[:rows, :] / features + 1e-06)
    heads = queries.shape[1] // KDIM
    for head in range(heads):
        query = turn(scaled[:, head * KDIM : (head + 1) * KDIM], cosine[:rows, :], sine[:rows, :])
        scores = matmul_t(query, keys[...]) * KDIM ** (-0.5)
        weights = jnp.exp(scores - jnp.max(scores, axis=1, keepdims=True))
        weight_sum = jnp.sum(weights, axis=1, keepdims=True)
        found = (matmul(weights.astype(BF16), values[...]) / weight_sum).astype(BF16)
        merged[:, head * LANES : (head + 1) * LANES] = found[:, :LANES]
        spot = heads * LANES + head * (VDIM - LANES)
        merged[:, spot : spot + VDIM - LANES] = found[:, LANES:]
    share[...] = matmul(merged[...], out[:, : share.shape[1]]).astype(BF16)


def second_kernel(spots, full, *refs):
    merged, out, own = refs[:3]
    founds, (share, inputs) = refs[3:-2], refs[-2:]
    share[...] = matmul(merged[...], out[:, share.shape[1] :]).astype(BF16)
    inputs[:, pl.ds(pl.multiple_of(lax.axis_index("heads") * full, LANES), full)] = own[...]
    for found, spot in zip(founds, spots):
        begin = pl.multiple_of(chunk_start(spot[0], 0, 1, full) + spot[1], LANES)
        inputs[:, pl.ds(begin, found.shape[1])] = found[...]


def gather_hidden(shares, inputs, gain, chunk):
    width = shares[0].shape[1]
    cols = slice(chunk * width, (chunk + 1) * width)
    total = shares[0][...].astype(F32)
    for other in shares[1:]:
        total = total + other[...].astype(F32)
    hidden = (inputs[:, cols].astype(F32) + total).astype(BF16).astype(F32)
    return jnp.sum(hidden * hidden, axis=1, keepdims=True), (hidden * gain[:, cols]).astype(BF16)


def soft(logits):
    return jnp.maximum(logits, 0.0) + jnp.log1p(jnp.exp(-jnp.abs(logits)))


def first_tracks_kernel(size, *refs):
    shares = refs[:size]
    inputs, gain, tracks, second, square, to_send, to_keep, base = refs[size:]
    strand = lax.axis_index("strand")
    width = shares[0].shape[1]
    base[...] = inputs[:, width:].astype(F32) + second[...].astype(F32)
    square[...], gained = gather_hidden(shares, inputs, gain, 0)
    to_send[...] = matmul(gained, tracks[1 - strand, :width, :])
    to_keep[...] = matmul(gained, tracks[strand, :width, :])


def send_kernel(size, *refs):
    shares = refs[: size - 1]
    base, gain, tracks, square, to_send, sent, gained_out, scale_out = refs[size - 1 :]
    strand = lax.axis_index("strand")
    width = base.shape[1]
    hidden = base[...]
    for other in shares:
        hidden = hidden + other[...].astype(F32)
    hidden = hidden.astype(BF16).astype(F32)
    total = jnp.sum(hidden * hidden, axis=1, keepdims=True)
    gained = (hidden * gain[:, width:]).astype(BF16)
    scale = lax.rsqrt((square[...] + total) / (2 * width) + 1e-06)
    logits = to_send[...] + matmul(gained, tracks[1 - strand, width:, :])
    sent[...] = soft(logits * scale).astype(BF16)
    gained_out[...] = gained
    scale_out[...] = scale


def swap_pairs(values, pairs):
    even = lax.broadcasted_iota(jnp.int32, (1, LANES), 1) % 2 == 0
    parts = []
    for begin in range(0, values.shape[1], LANES):
        part = values[:, begin : begin + LANES]
        swapped = (pairs[:, begin : begin + LANES] % 2 == 0) != even
        partner = jnp.where(even, pltpu.roll(part, LANES - 1, 1), pltpu.roll(part, 1, 1))
        parts.append(jnp.where(swapped, partner, part))
    return jnp.concatenate(parts, axis=1)


def keep_kernel(gained, tracks, to_keep, scale, pairs, kept):
    strand = lax.axis_index("strand")
    width = gained.shape[1]
    logits = to_keep[...] + matmul(gained[...], tracks[strand, width:, :])
    found = soft(logits * scale[...]).astype(BF16).astype(F32)
    kept[...] = jnp.where(strand == 0, found, swap_pairs(found, pairs)).astype(BF16)


def average_kernel(parts, kept, received, pairs, out, stage, sems):
    strand = lax.axis_index("strand")
    rows = kept.shape[0] // parts
    copies = []
    for i in range(parts):
        here = slice(i * rows, (i + 1) * rows)
        theirs = received[here, :].astype(F32)
        theirs = jnp.where(strand == 0, swap_pairs(theirs, pairs), theirs)
        stage[here, :] = 0.5 * (kept[here, :].astype(F32) + theirs)
        copies.append(pltpu.make_async_copy(stage.at[here], out.at[here], sems.at[i]))
        copies[-1].start()
    for copy in copies:
        copy.wait()


def body(
    base_codes,
    embed_table,
    attn_gain,
    w_query,
    w_key,
    w_value,
    w_out,
    head_gain,
    w_tracks,
    track_pairs,
):
    rows = base_codes.shape[0] // BIN
    blocks = lax.axis_size("pos")
    size = lax.axis_size("heads")
    features, q_cols = w_query.shape
    entries, width = embed_table.shape
    groups = lax.axis_size("groups")
    key_t, value_t = w_key.T, w_value.T
    kv_cols = key_t.shape[0] + value_t.shape[0]
    kv_all = KDIM + VDIM
    half = entries // 2
    total = blocks * rows
    tracks_half = w_tracks.shape[2]
    chunks = 2 if width % (2 * LANES) == 0 else 1
    wide = width // chunks
    carry = LANES if chunks == 2 and wide % (2 * LANES) and wide > LANES else 0

    early, late = [(0, 0)], []
    for k in range(1, blocks, 2):
        early.append((k, min(k + 1, blocks - 1)))
        if k + 1 < blocks:
            late.append((k + 1, k))

    hbm = pltpu.HBM
    part_kv, *own_pieces, own_codes = call(
        functools.partial(stage_kernel, chunks),
        [shape((kv_cols, features // (2 * groups)), BF16)]
        + [shape((half, wide), BF16)] * chunks
        + [shape((rows, BIN), BF16)],
        [embed_table, key_t, value_t, base_codes.reshape(rows, BIN)],
        "stage",
        scratch=[pltpu.VMEM((rows, BIN), jnp.int32), pltpu.SemaphoreType.DMA((3 + chunks,))],
        spaces=[hbm] * 4,
    )
    table, key_own, value_own, query_own, gain, last_gain, cosine, sine = call(
        functools.partial(prepare_kernel, rows, early + late),
        [
            shape((entries, width), BF16),
            shape(key_t.shape, BF16),
            shape(value_t.shape, BF16),
            shape(w_query.shape, BF16),
            shape((1, features), F32),
            shape((1, features), F32),
            shape((total, KDIM), F32),
            shape((total, KDIM), F32),
        ],
        [embed_table, key_t, value_t, w_query, attn_gain, head_gain],
        "prepare",
        scratch=[
            pltpu.VMEM((features,), F32),
            pltpu.VMEM((features,), F32),
            pltpu.SemaphoreType.DMA((7,)),
        ],
        spaces=[hbm] * 6,
    )
    kv_parts, kv_steps, pieces, steps = [], [], [], []
    from_heads = [shifted(part_kv, "heads", step) for step in range(1, size)]
    if from_heads:
        from_heads[0], table = lax.optimization_barrier((from_heads[0], table))
    to_core = [shifted(here, "strand", 1) for here in from_heads]
    (out_here,) = call(
        fetch_kernel,
        [shape(w_out.shape, BF16)],
        [w_out],
        "fetch_out",
        scratch=[pltpu.SemaphoreType.DMA((2 * (q_cols // KDIM),))],
        spaces=[hbm],
    )
    raw = []
    for k, other in early[1:]:
        if k != other:
            pairs = [((p, s), ((p + k + s) % blocks, s)) for p in range(blocks) for s in range(2)]
            pairs = [(2 * p + s, 2 * q + t) for (p, s), (q, t) in pairs]
            raw.append(lax.ppermute(own_codes, ("pos", "strand"), pairs))
        else:
            if to_core:
                own_codes, to_core[0] = lax.optimization_barrier((own_codes, to_core[0]))
            raw.append(shifted(own_codes, "pos", k))
    if raw:
        raw[0], out_here = lax.optimization_barrier((raw[0], out_here))
    for step in range(1, size):
        for k in range(groups):
            here = from_heads[step - 1] if k == 0 else shifted(from_heads[step - 1], "groups", k)
            kv_parts += [here, to_core[step - 1] if k == 0 else shifted(here, "strand", 1)]
            kv_steps += [(step, k, 0), (step, k, 1)]
    for step in range(1, size):
        for i in range(chunks):
            here = shifted(own_pieces[i], "heads", step)
            if step == 1 and i == chunks - 1 and raw:
                here, *raw = lax.optimization_barrier((here, *raw))
            pieces.append((here, shifted(here, "strand", 1)))
            steps.append((step, i))

    swapped = [shifted(raw[i], "strand", 1) for i in range(len(late))]
    codes = [own_codes] + raw
    if len(steps) < 2:
        codes, swapped = codes + swapped, []

    def sums_of(count):
        return [shape((count, 1), F32), shape((count, kv_all), F32), shape((rows, q_cols), F32)]

    count = rows * len(codes)
    onehot, kv_t, own, *state = call(
        functools.partial(own_kernel, len(codes), kv_steps),
        [shape((count, entries), BF16), shape((kv_all, features), BF16), shape((rows, width), BF16)]
        + sums_of(count),
        codes + [table, key_own, value_own] + kv_parts + [query_own, gain],
        "own_features",
        scratch=[pltpu.VMEM((count, BIN), BF16)],
        flops=2 * count * width * (entries + kv_all),
        spare=8 * total * entries,
    )
    founds = []
    for (step, i), pair in zip(steps[:-1], pieces[:-1]):
        left = carry if step == size - 1 else 0
        operands = list(pair) + [onehot, kv_t, query_own, gain] + state
        outs = [shape((rows, wide - left), BF16)] + sums_of(total)
        scratch = [pltpu.VMEM((entries, wide - left), BF16)]
        if swapped:
            kernel = functools.partial(join_kernel, step, i, chunks, left, rows, len(swapped))
            operands += [table] + swapped
            outs = [shape((total, entries), BF16)] + outs
            scratch.append(pltpu.VMEM((rows * len(swapped), BIN), BF16))
        else:
            kernel = functools.partial(chunk_kernel, step, i, chunks, left, rows)
        results = call(
            kernel,
            outs,
            operands,
            "other_features",
            scratch=scratch,
            flops=2 * total * wide * (entries + kv_all),
            spare=8 * total * entries,
        )
        if swapped:
            onehot, *results = results
            swapped = []
        found, *state = results
        founds.append(found)
    o_cols = q_cols // KDIM * VDIM
    share_one, merged, last = call(
        functools.partial(attend_kernel, steps, chunks, carry),
        [
            shape((rows, features // 2), BF16),
            shape((rows, o_cols), BF16),
            shape((rows, wide + carry), BF16),
        ],
        (list(pieces[-2]) if carry else [])
        + list(pieces[-1])
        + [onehot, kv_t, query_own, gain]
        + state
        + [cosine, sine, out_here],
        "attend",
        scratch=[
            pltpu.VMEM((entries, wide + carry), BF16),
            pltpu.VMEM((total, 1), F32),
            pltpu.VMEM((total, kv_all), F32),
            pltpu.VMEM((rows, q_cols), F32),
            pltpu.VMEM((total, KDIM), BF16),
            pltpu.VMEM((total, VDIM), BF16),
        ],
        flops=2 * total * wide * (entries + kv_all) + 2 * total * q_cols * rows * 3,
        spare=8 * total * entries,
    )
    spots = [(step, i * wide) for step, i in steps]
    spots[-1] = (spots[-1][0], spots[-1][1] - carry)
    share_two, inputs = call(
        functools.partial(second_kernel, spots, width),
        [shape((rows, features // 2), BF16), shape((rows, features), BF16)],
        [merged, out_here, own] + founds + [last],
        "second_share",
        flops=rows * o_cols * features,
    )
    ones = [share_one] + [shifted(share_one, "heads", k) for k in range(1, size)]
    twos = [share_two] + [shifted(share_two, "heads", k) for k in range(1, size)]
    weights, _ = lax.optimization_barrier((w_tracks, share_two))
    tracks = lax.optimization_barrier(weights.transpose(1, 0, 2))
    square, to_send, to_keep, base = call(
        functools.partial(first_tracks_kernel, size),
        [
            shape((rows, 1), F32),
            shape((rows, tracks_half), F32),
            shape((rows, tracks_half), F32),
            shape((rows, features // 2), F32),
        ],
        ones + [inputs, last_gain, tracks, share_two],
        "first_tracks",
        flops=2 * rows * features * tracks_half,
    )
    sent, gained, scale = call(
        functools.partial(send_kernel, size),
        [
            shape((rows, tracks_half), BF16),
            shape((rows, features // 2), BF16),
            shape((rows, 1), F32),
        ],
        twos[1:] + [base, last_gain, tracks, square, to_send],
        "sent_tracks",
        flops=rows * features * tracks_half,
    )
    received = shifted(sent, "strand", 1)
    pairs = track_pairs.reshape(1, tracks_half)
    (kept,) = call(
        keep_kernel,
        [shape((rows, tracks_half), BF16)],
        [gained, tracks, to_keep, scale, pairs],
        "kept_tracks",
        flops=rows * features * tracks_half,
    )
    (out,) = call(
        functools.partial(average_kernel, 4),
        [shape((rows, tracks_half), F32)],
        [kept, received, pairs],
        "average",
        scratch=[pltpu.VMEM((rows, tracks_half), F32), pltpu.SemaphoreType.DMA((4,))],
        out_space=hbm,
    )
    return out


def solution(mesh):
    placed = (
        P(("groups", "pos")),
        P(None, "heads"),
        P(),
        P(None, "heads"),
        P(None, "heads"),
        P(None, "heads"),
        P("heads", None),
        P(),
        P(None, None, "heads"),
        P(("strand", "heads")),
    )
    return jax.shard_map(
        body,
        mesh=mesh,
        in_specs=placed,
        out_specs=P(("groups", "pos"), ("strand", "heads")),
        check_vma=False,
    )
```
